32 devices in a mesh: groups: 2 (over y), cell: 8 (over z, x), gene: 2 (over core).
Axes of the slice: x: 2, y: 2, z: 4, core: 2. Of those that a mesh axis runs over, the one named last changes fastest.
Arguments:
- block_values: bfloat16 [16, 2, 64, 128, 128], P(('groups', 'cell'), 'gene'), parts along dimension 0, may hold values from 0 to 5632, as said below
- block_rows: int32 [16, 2, 64], P(('groups', 'cell'), 'gene'), parts along dimension 0, may hold values from 0 to 7
- block_cols: int32 [16, 2, 64], P(('groups', 'cell'), 'gene'), parts along dimension 0, may hold values from 0 to 15
- block_count: int32 [16, 2], P(('groups', 'cell'), 'gene'), parts along dimension 0, may hold values from 32 to 64, as said below
- cell_factor: float32 [512, 8192], P(('groups', 'gene'), 'cell'), parts along dimension 0, may hold values from 0 to 1
- gene_factor: float32 [512, 4096], P(('groups', 'cell'), 'gene'), parts along dimension 0, may hold values from 0 to 1
Outputs:
- cell_next: float32 [512, 8192], P(('groups', 'gene'), 'cell'), parts along dimension 0
- gene_next: float32 [512, 4096], P(('groups', 'cell'), 'gene'), parts along dimension 0
The draws below stay inside these ranges and needn't reach their ends.
There are 2 independent parts, one for each index of `groups`. The reference program is written for one: setup_inputs(seed, part) draws one part's arguments, and reference() takes and returns one part's arrays. A program takes and returns all parts, laid end to end along the dimension named above; each array names one. Nothing has to cross between parts.
Inputs may be any that keep to these rules, and one draw needn't show every extreme that they name: Within a tile, the first block_count entries of block_rows and block_cols name distinct blocks; every tile's later entries are valid indices too. block_count reaches 64 on some tile of every draw. `block_values`: Positive.
All inputs are finite; a program needn't handle non-finite values.
Results may differ from the reference program's by a relative error of at most 0.0014.
Values may be sent and summed in bfloat16 or wider, within the bound.
No kernel may reach another device: no remote copies, remote signals or barrier semaphores. Data moves between devices by JAX's collectives and lax.ppermute only.
A program may use at most 64 MiB of HBM per device.

```python
import math
import jax
import jax.numpy as jnp
from jax import lax

K = 256
BLK = 128
CELL_DEV = 1024
GENE_DEV = 2048
NB_MAX = 64
CELLS = 8192
GENES = 4096
N_CELL = 8
N_GENE = 2


def tile_layout(key):
    slots = CELL_DEV // BLK * (GENE_DEV // BLK)
    key_count, key_place = jax.random.split(key)
    counts = jax.random.randint(key_count, (N_CELL, N_GENE), (NB_MAX + 1) // 2, NB_MAX + 1)
    counts = counts.at[0, 0].set(NB_MAX)
    keys = jax.random.split(key_place, N_CELL * N_GENE)
    places = jax.vmap(lambda one: jax.random.permutation(one, slots)[:NB_MAX])(keys)
    return (counts.astype(jnp.int32), places.reshape(N_CELL, N_GENE, NB_MAX).astype(jnp.int32))


def draw_block_rows(key, part):
    counts, places = tile_layout(key)
    return (places // (GENE_DEV // BLK)).astype(jnp.int32)


def draw_block_cols(key, part):
    counts, places = tile_layout(key)
    return (places % (GENE_DEV // BLK)).astype(jnp.int32)


def draw_block_count(key, part):
    counts, places = tile_layout(key)
    return counts


def draw_block_values(key, part):
    counts, places = tile_layout(key)
    key = jax.random.fold_in(key, 7)
    key_depth, key_gene, key_noise = jax.random.split(key, 3)
    row_blocks = CELL_DEV // BLK
    col_blocks = GENE_DEV // BLK
    rows = places // col_blocks
    cols = places % col_blocks
    low_end = math.log(0.3)
    high_end = math.log(3.0)
    log_depth = jax.random.uniform(key_depth, (N_CELL, row_blocks, BLK), jnp.float32, low_end, high_end)
    log_gene = jax.random.uniform(key_gene, (N_GENE, col_blocks, BLK), jnp.float32, low_end, high_end)
    depth_blocks = log_depth[jnp.arange(N_CELL)[:, None, None], rows]
    gene_blocks = log_gene[jnp.arange(N_GENE)[None, :, None], cols]
    shape = (N_CELL, N_GENE, NB_MAX, BLK, BLK)
    noise = 0.6 * jnp.clip(jax.random.normal(key_noise, shape, jnp.float32), -3.0, 3.0)
    scale = K * row_blocks * col_blocks / (5.0 * NB_MAX)
    logged = depth_blocks[..., :, None] + gene_blocks[..., None, :] + noise
    return (scale * jnp.exp(logged)).astype(jnp.bfloat16)


def block_levels(rng, dims, cuts, low, high):
    gain, own = 1.0, jax.random.fold_in(rng, 6)
    for axis_at, parts in cuts:
        steps = jnp.exp(jax.random.uniform(jax.random.fold_in(own, axis_at), (parts,), jnp.float32, low / len(cuts), high / len(cuts)))
        gain = gain * jnp.repeat(steps, dims[axis_at] // parts).reshape([-1 if axis == axis_at else 1 for axis in range(len(dims))])
    return gain


def setup_inputs(seed: int = 0, part: int = 0) -> dict:
    arg_keys = jax.random.split(jax.random.key(seed), 7)
    part_keys = jax.random.split(jax.random.fold_in(arg_keys[6], part), 7)
    block_values = draw_block_values(jax.random.fold_in(jax.random.fold_in(arg_keys[6], part), 71), part)
    block_rows = draw_block_rows(jax.random.fold_in(jax.random.fold_in(arg_keys[6], part), 71), part)
    block_cols = draw_block_cols(jax.random.fold_in(jax.random.fold_in(arg_keys[6], part), 71), part)
    block_count = draw_block_count(jax.random.fold_in(jax.random.fold_in(arg_keys[6], part), 71), part)
    cell_factor = jnp.clip(1.0 * jax.random.uniform(part_keys[4], (K, CELLS), jnp.float32) ** block_levels(part_keys[4], (K, CELLS), ((0, 2), (1, 8)), -0.2, 0.2), 0.0, 1.0)
    gene_factor = jnp.clip(1.0 * jax.random.uniform(part_keys[5], (K, GENES), jnp.float32) ** block_levels(part_keys[5], (K, GENES), ((0, 8), (1, 2)), -0.2, 0.2), 0.0, 1.0)
    return {"block_values": block_values, "block_rows": block_rows, "block_cols": block_cols, "block_count": block_count, "cell_factor": cell_factor, "gene_factor": gene_factor}


def tile_data_gene(values, rows, cols, count, panel):
    live = (jnp.arange(values.shape[0]) < count).astype(jnp.float32)
    vals = values.astype(jnp.float32) * live[:, None, None]
    row_pick = (rows[:, None] == jnp.arange(CELL_DEV // BLK)[None, :]).astype(jnp.float32)
    col_pick = (cols[:, None] == jnp.arange(GENE_DEV // BLK)[None, :]).astype(jnp.float32)
    picked = jnp.einsum('ng,kgc->nkc', col_pick, panel.reshape(K, GENE_DEV // BLK, BLK).astype(jnp.float32))
    partial_rows = jnp.einsum('nrc,nkc->nkr', vals, picked)
    return jnp.einsum('nkr,nb->kbr', partial_rows, row_pick).reshape(K, CELL_DEV)

def tile_data_cell(values, rows, cols, count, panel):
    live = (jnp.arange(values.shape[0]) < count).astype(jnp.float32)
    vals = values.astype(jnp.float32) * live[:, None, None]
    row_pick = (rows[:, None] == jnp.arange(CELL_DEV // BLK)[None, :]).astype(jnp.float32)
    col_pick = (cols[:, None] == jnp.arange(GENE_DEV // BLK)[None, :]).astype(jnp.float32)
    picked = jnp.einsum('nb,kbr->nkr', row_pick, panel.reshape(K, CELL_DEV // BLK, BLK).astype(jnp.float32))
    partial_cols = jnp.einsum('nrc,nkr->nkc', vals, picked)
    return jnp.einsum('nkc,ng->kgc', partial_cols, col_pick).reshape(K, GENE_DEV)

def reference(block_values, block_rows, block_cols, block_count, cell_factor, gene_factor):
    gene_low = gene_factor.astype(jnp.bfloat16)
    cell_low = cell_factor.astype(jnp.bfloat16)
    gene_gram = jnp.dot(gene_low, gene_low.T, preferred_element_type=jnp.float32)
    rate_cell = 1.0 / (jnp.sqrt(jnp.sum(gene_gram * gene_gram)) + 1e-06)
    n_cell = block_values.shape[0]
    n_gene = block_values.shape[1]

    def per_tile(carry, index):
        data_cell, cell_gram = carry
        cell_slab = lax.dynamic_slice_in_dim(cell_factor, index * CELL_DEV, CELL_DEV, 1)
        low_slab = lax.dynamic_slice_in_dim(cell_low, index * CELL_DEV, CELL_DEV, 1)
        data_gene = jnp.zeros((K, CELL_DEV), jnp.float32)
        for g in range(n_gene):
            data_gene = data_gene + tile_data_gene(block_values[index, g], block_rows[index, g], block_cols[index, g], block_count[index, g], gene_low[:, g * GENE_DEV:(g + 1) * GENE_DEV])
        stepped = jnp.dot(gene_gram, low_slab.astype(jnp.float32), precision=lax.Precision.HIGHEST)
        cell_new = jnp.maximum(cell_slab - rate_cell * (stepped - data_gene), 0.0)
        next_low = cell_new.astype(jnp.bfloat16)
        cell_gram = cell_gram + jnp.dot(next_low, next_low.T, preferred_element_type=jnp.float32)
        pieces = []
        for g in range(n_gene):
            pieces.append(tile_data_cell(block_values[index, g], block_rows[index, g], block_cols[index, g], block_count[index, g], next_low))
        data_cell = data_cell + jnp.concatenate(pieces, axis=1)
        return ((data_cell, cell_gram), cell_new)
    start = (jnp.zeros((K, GENE_DEV * n_gene), jnp.float32), jnp.zeros((K, K), jnp.float32))
    (data_cell, cell_gram), cell_tiles = lax.scan(per_tile, start, jnp.arange(n_cell))
    cell_next = jnp.transpose(cell_tiles, (1, 0, 2)).reshape(K, CELL_DEV * n_cell)
    rate_gene = 1.0 / (jnp.sqrt(jnp.sum(cell_gram * cell_gram)) + 1e-06)
    stepped = jnp.dot(cell_gram, gene_low.astype(jnp.float32), precision=lax.Precision.HIGHEST)
    gene_next = jnp.maximum(gene_factor - rate_gene * (stepped - data_cell), 0.0)
    return (cell_next, gene_next)
```

```python
import functools

import jax
import jax.numpy as jnp
from jax import lax
from jax.experimental import pallas as pl
from jax.experimental.pallas import tpu as pltpu
from jax.sharding import PartitionSpec as P

BLK = 128
CELL_DEV = 1024
GENE_DEV = 2048
VMEM_BYTES = 48 * 2**20

NT = (((1,), (1,)), ((), ()))
NN = (((1,), (0,)), ((), ()))
SMEM_SPEC = pl.BlockSpec(memory_space=pltpu.SMEM)
VMEM_SPEC = pl.BlockSpec(memory_space=pltpu.VMEM)


def dot(a, b, dims=NN):
    return lax.dot_general(a, b, dims, preferred_element_type=jnp.float32)


def split_dot(a, b):
    high = a.astype(jnp.bfloat16)
    rest = a - high.astype(jnp.float32)
    mid = rest.astype(jnp.bfloat16)
    low = (rest - mid.astype(jnp.float32)).astype(jnp.bfloat16)
    return dot(high, b) + (dot(mid, b) + dot(low, b))


def call(body, outs, n_smem, n_vmem, flops, traffic, scratch=()):
    return pl.pallas_call(
        body,
        out_shape=outs,
        in_specs=[SMEM_SPEC] * n_smem + [VMEM_SPEC] * n_vmem,
        out_specs=jax.tree.map(lambda _: VMEM_SPEC, outs),
        scratch_shapes=list(scratch),
        compiler_params=pltpu.CompilerParams(vmem_limit_bytes=VMEM_BYTES),
        cost_estimate=pl.CostEstimate(flops=flops, bytes_accessed=traffic, transcendentals=0),
    )


def shape(dims, dtype):
    return jax.ShapeDtypeStruct(dims, dtype)


def dense_body(rows, cols, count, values, tile):
    tile[...] = jnp.zeros_like(tile)

    def place(n, carry):
        row = pl.multiple_of(rows[n] * BLK, BLK)
        col = pl.multiple_of(cols[n] * BLK, BLK)
        tile[pl.ds(row, BLK), pl.ds(col, BLK)] = values[n]
        return carry

    lax.fori_loop(0, count[0], place, 0)


def dense_tile(values, rows, cols, count):
    return call(
        dense_body,
        shape((CELL_DEV, GENE_DEV), jnp.bfloat16),
        3,
        1,
        0,
        2 * 2**20 + 4 * 2**20,
    )(rows, cols, count, values)


def gene_body(owners, tile, *refs):
    shares, panel, message = refs[:-2], refs[-2], refs[-1]
    for n, part in enumerate(shares):
        size = part.shape[0]
        panel[pl.ds(pl.multiple_of(owners[n] * size, size), size)] = part[...]
    low = panel[...]
    message[:, :CELL_DEV] = dot(low, tile[...], NT)
    message[:, CELL_DEV:] = dot(low, low, NT)


def cell_body(picks, at, tile, mine, other, factor_mine, factor_other, cell_next, low_out, *rest):
    sends, (factor, updated, chosen) = rest[:-3], rest[-3:]
    share = factor_mine.shape[0]
    own = pl.multiple_of(at[0] * share, share)
    theirs = pl.multiple_of((1 - at[0]) * share, share)
    factor[pl.ds(own, share)] = factor_mine[...]
    factor[pl.ds(theirs, share)] = factor_other[...]
    gram = mine[:, CELL_DEV:] + other[:, CELL_DEV:]
    norm = jnp.sum(jnp.sum(gram * gram, axis=1, keepdims=True), axis=0, keepdims=True)
    rate = 1.0 / (jnp.sqrt(norm) + 1e-06)
    data = mine[:, :CELL_DEV] + other[:, :CELL_DEV]
    held = factor[...]
    stepped = split_dot(gram, held.astype(jnp.bfloat16))
    updated[...] = jnp.maximum(held - rate * (stepped - data), 0.0)
    cell_next[...] = updated[pl.ds(own, share)]
    low_out[...] = updated[...].astype(jnp.bfloat16)
    if sends:
        size = sends[0].shape[0]
        for n in range(len(sends)):
            row = pl.multiple_of(picks[n] * size, size)
            chosen[n * size : (n + 1) * size] = low_out[pl.ds(row, size)]
        product = dot(chosen[...], tile[...])
        for n, out in enumerate(sends):
            out[...] = product[n * size : (n + 1) * size].astype(out.dtype)


def keep_body(picks, low, tile, gram, *rest):
    keeps, chosen = rest[:-1], rest[-1]
    panel = low[...]
    gram[...] = dot(panel, panel, NT).astype(gram.dtype)
    size = keeps[0].shape[0]
    for n in range(len(keeps)):
        row = pl.multiple_of(picks[n] * size, size)
        chosen[n * size : (n + 1) * size] = low[pl.ds(row, size)]
    product = dot(chosen[...], tile[...])
    for n, out in enumerate(keeps):
        out[...] = product[n * size : (n + 1) * size]


def gram_body(partials, panel, stepped, square):
    size = stepped.shape[0]
    gram = partials[:size].astype(jnp.float32)
    for n in range(1, partials.shape[0] // size):
        gram = gram + partials[n * size : (n + 1) * size].astype(jnp.float32)
    stepped[...] = split_dot(gram, panel[...])
    norm = jnp.sum(jnp.sum(gram * gram, axis=1, keepdims=True), axis=0, keepdims=True)
    square[...] = jnp.broadcast_to(norm, square.shape)


def gram_of(panel):
    return dot(panel, panel, NT)


def shards(block_values, block_rows, block_cols, block_count, cell_factor, gene_factor):
    n_cell = lax.axis_size("cell")
    kdim = cell_factor.shape[0] * lax.axis_size("gene")
    size = gene_factor.shape[0]
    cell_share = cell_factor.shape[0]
    paired = size % 16 == 0 and n_cell >= 4 and n_cell & (n_cell - 1) == 0
    cell_at = lax.axis_index("cell")
    gene_at = lax.axis_index("gene")

    def swap(value, bits):
        return lax.ppermute(value, "cell", [(n, n ^ bits) for n in range(n_cell)])

    def swap_core(value):
        return lax.ppermute(value, "gene", [(0, 1), (1, 0)])

    low_share = gene_factor.astype(jnp.bfloat16)
    if paired:
        offsets = list(range(2, n_cell, 2))
        offsets.sort(key=lambda bits: -bits)
        near = swap(low_share, 1)
        far = [swap(low_share, bits) for bits in offsets]
        shares = [low_share, near] + far + [swap(part, 1) for part in far]
        owners = [0, 1] + offsets + [bits ^ 1 for bits in offsets]
        owners = jnp.stack([cell_at ^ bits for bits in owners]).astype(jnp.int32)
    else:
        shares = [lax.all_gather(low_share, "cell", axis=0, tiled=True)]
        owners = jnp.zeros((1,), jnp.int32)
    factor_other = swap_core(cell_factor)
    tile = dense_tile(block_values[0, 0], block_rows[0, 0], block_cols[0, 0], block_count[0])

    panel, message = call(
        gene_body,
        (shape((kdim, GENE_DEV), jnp.bfloat16), shape((kdim, CELL_DEV + kdim), jnp.float32)),
        1,
        1 + len(shares),
        2 * kdim * GENE_DEV * (CELL_DEV + kdim),
        8 * 2**20,
    )(owners, tile, *shares)
    other = swap_core(message)

    sent = [bits ^ 1 for bits in offsets] + [1] if paired else []
    kept = offsets + [0] if paired else []
    picks = jnp.stack([cell_at ^ bits for bits in sent or [0]]).astype(jnp.int32)
    outs = call(
        cell_body,
        (
            shape(cell_factor.shape, jnp.float32),
            shape((kdim, CELL_DEV), jnp.bfloat16),
            *[shape((size, GENE_DEV), jnp.bfloat16) for _ in sent],
        ),
        2,
        5,
        2 * kdim * CELL_DEV * 3 * kdim + kdim * CELL_DEV * GENE_DEV,
        10 * 2**20,
        [
            pltpu.VMEM((kdim, CELL_DEV), jnp.float32),
            pltpu.VMEM((kdim, CELL_DEV), jnp.float32),
            pltpu.VMEM((kdim // 2, CELL_DEV), jnp.bfloat16),
        ],
    )(picks, gene_at[None].astype(jnp.int32), tile, message, other, cell_factor, factor_other)
    cell_next, next_low, sends = outs[0], outs[1], outs[2:]

    if not paired:
        cell_gram = lax.psum(gram_of(next_low), "cell")
        own_cols = lax.psum_scatter(dot(next_low, tile), "cell", scatter_dimension=0, tiled=True)
        gram_part = lax.dynamic_slice_in_dim(cell_gram, cell_at * size, size, 0)
        rate_gene = 1.0 / (jnp.sqrt(jnp.sum(cell_gram * cell_gram)) + 1e-06)
        stepped = jnp.dot(
            gram_part, panel.astype(jnp.float32), precision=lax.Precision.HIGHEST
        )
        return (cell_next, jnp.maximum(gene_factor - rate_gene * (stepped - own_cols), 0.0))

    arrived = [swap(part, 1) for part in sends]
    picks = jnp.stack([cell_at ^ bits for bits in kept]).astype(jnp.int32)
    gram, *keeps = call(
        keep_body,
        (
            shape((kdim, kdim), jnp.bfloat16),
            *[shape((size, GENE_DEV), jnp.float32) for _ in kept],
        ),
        1,
        2,
        2 * kdim * CELL_DEV * kdim + kdim * CELL_DEV * GENE_DEV,
        6 * 2**20,
        [pltpu.VMEM((kdim // 2, CELL_DEV), jnp.bfloat16)],
    )(picks, next_low, tile)
    partials = lax.all_to_all(gram, "cell", 0, 0, tiled=True)
    stepped, square = call(
        gram_body,
        (shape((size, GENE_DEV), jnp.float32), shape((8, 128), jnp.float32)),
        0,
        2,
        2 * size * kdim * GENE_DEV * 3,
        2 * 2**20,
    )(partials, panel)
    squares = lax.all_to_all(
        jnp.broadcast_to(square[None], (n_cell, 8, 128)), "cell", 0, 0, tiled=True
    )
    rate_gene = 1.0 / (jnp.sqrt(jnp.sum(squares[:, 0, 0])) + 1e-06)
    pairs = [mine + part.astype(jnp.float32) for mine, part in zip(keeps, arrived)]
    own_cols = pairs[-1]
    for bits, pair in zip(offsets, pairs):
        own_cols = own_cols + swap(pair.astype(jnp.bfloat16), bits).astype(jnp.float32)
    return (cell_next, jnp.maximum(gene_factor - rate_gene * (stepped - own_cols), 0.0))


def solution(mesh):
    return jax.shard_map(
        shards,
        mesh=mesh,
        in_specs=(
            P(("groups", "cell"), "gene", None, None, None),
            P(("groups", "cell"), "gene", None),
            P(("groups", "cell"), "gene", None),
            P(("groups", "cell"), "gene"),
            P(("groups", "gene"), "cell"),
            P(("groups", "cell"), "gene"),
        ),
        out_specs=(P(("groups", "gene"), "cell"), P(("groups", "cell"), "gene")),
        check_vma=False,
    )
```

```python
import functools

import jax
import jax.numpy as jnp
from jax import lax
from jax.experimental import pallas as pl
from jax.experimental.pallas import tpu as pltpu
from jax.sharding import PartitionSpec as P

BLK = 128
CELL_DEV = 1024
GENE_DEV = 2048
VMEM_BYTES = 24 * 2**20

NT = (((1,), (1,)), ((), ()))
NN = (((1,), (0,)), ((), ()))
SMEM_SPEC = pl.BlockSpec(memory_space=pltpu.SMEM)
VMEM_SPEC = pl.BlockSpec(memory_space=pltpu.VMEM)


def dot(a, b, dims=NN):
    return lax.dot_general(a, b, dims, preferred_element_type=jnp.float32)


def split_dot(a, b):
    high = a.astype(jnp.bfloat16)
    low = (a - high.astype(jnp.float32)).astype(jnp.bfloat16)
    rows = a.shape[0]
    both = dot(jnp.concatenate([high, low], axis=0), b)
    return both[:rows] + both[rows:]


def call(body, outs, n_smem, n_vmem, flops, traffic, scratch=()):
    return pl.pallas_call(
        body,
        out_shape=outs,
        in_specs=[SMEM_SPEC] * n_smem + [VMEM_SPEC] * n_vmem,
        out_specs=jax.tree.map(lambda _: VMEM_SPEC, outs),
        scratch_shapes=list(scratch),
        compiler_params=pltpu.CompilerParams(vmem_limit_bytes=VMEM_BYTES),
        cost_estimate=pl.CostEstimate(flops=flops, bytes_accessed=traffic, transcendentals=0),
    )


def shape(dims, dtype):
    return jax.ShapeDtypeStruct(dims, dtype)


def dense_body(rows, cols, count, values, tile, turned):
    tile[...] = jnp.zeros_like(tile)
    turned[...] = jnp.zeros_like(turned)

    def place(n, carry):
        row = pl.multiple_of(rows[n] * BLK, BLK)
        col = pl.multiple_of(cols[n] * BLK, BLK)
        block = values[n]
        tile[pl.ds(row, BLK), pl.ds(col, BLK)] = block
        turned[pl.ds(col, BLK), pl.ds(row, BLK)] = block.T
        return carry

    lax.fori_loop(0, count[0], place, 0)


def dense_tile(values, rows, cols, count):
    return call(
        dense_body,
        (
            shape((CELL_DEV, GENE_DEV), jnp.bfloat16),
            shape((GENE_DEV, CELL_DEV), jnp.bfloat16),
        ),
        3,
        1,
        0,
        0,
    )(rows, cols, count, values)


def first_body(turned, *refs):
    shares, panel, message = refs[:-2], refs[-2], refs[-1]
    size = shares[0].shape[0]
    for n, part in enumerate(shares):
        panel[n * size : (n + 1) * size] = part[...]
    message[...] = dot(panel[...], turned[...])


def second_body(owners, turned, first, *refs):
    shares, panel, message, chosen = refs[:-3], refs[-3], refs[-2], refs[-1]
    size, half = shares[0].shape[0], first.shape[0]
    for n, part in enumerate(shares):
        chosen[n * size : (n + 1) * size] = part[...]
    for n in range(half // size):
        row = pl.multiple_of(owners[n] * size, size)
        panel[pl.ds(row, size)] = first[n * size : (n + 1) * size]
    for n, part in enumerate(shares):
        row = pl.multiple_of(owners[half // size + n] * size, size)
        panel[pl.ds(row, size)] = part[...]
    message[:, :CELL_DEV] = dot(chosen[...], turned[...])
    low = panel[...]
    gram = dot(low, low, NT)
    kdim = low.shape[0]
    message[:, CELL_DEV : CELL_DEV + kdim] = gram[:half]
    message[:, CELL_DEV + kdim :] = gram[half:]


def cell_body(
    at, owners, picks, tile, mine_first, other_first, mine, other, factor_mine, factor_other,
    cell_next, low, gram_out, *rest
):
    parts, (factor, data, updated, chosen) = rest[:-4], rest[-4:]
    share = factor_mine.shape[0]
    kdim = factor.shape[0]
    half = mine.shape[0]
    own = pl.multiple_of(at[0] * share, share)
    theirs = pl.multiple_of((1 - at[0]) * share, share)
    factor[pl.ds(own, share)] = factor_mine[...]
    factor[pl.ds(theirs, share)] = factor_other[...]
    size = kdim // owners.shape[0]
    for n in range(owners.shape[0]):
        row = pl.multiple_of(owners[n] * size, size)
        if n * size < half:
            rows = pl.ds(n * size, size)
            data[pl.ds(row, size)] = mine_first[rows] + other_first[rows]
        else:
            rows = pl.ds(n * size - half, size)
            data[pl.ds(row, size)] = mine[rows, :CELL_DEV] + other[rows, :CELL_DEV]
    gram = mine[:, CELL_DEV:] + other[:, CELL_DEV:]
    gram = jnp.concatenate([gram[:, :kdim], gram[:, kdim:]], axis=0)
    norm = jnp.sum(jnp.sum(gram * gram, axis=1, keepdims=True), axis=0, keepdims=True)
    rate = 1.0 / (jnp.sqrt(norm) + 1e-06)
    held = factor[...]
    stepped = split_dot(gram, held.astype(jnp.bfloat16))
    updated[...] = jnp.maximum(held - rate * (stepped - data[...]), 0.0)
    cell_next[...] = updated[pl.ds(own, share)]
    low[...] = updated[...].astype(jnp.bfloat16)
    if not parts:
        return
    panel = low[...]
    gram_out[...] = dot(panel, panel, NT).astype(gram_out.dtype)
    for n in range(picks.shape[0]):
        row = pl.multiple_of(picks[n] * size, size)
        chosen[n * size : (n + 1) * size] = low[pl.ds(row, size)]
    product = dot(chosen[...], tile[...])
    row = 0
    for out in parts:
        out[...] = product[row : row + out.shape[0]].astype(out.dtype)
        row += out.shape[0]


def gram_body(partials, panel, stepped, square):
    size = stepped.shape[0]
    gram = partials[:size].astype(jnp.float32)
    for n in range(1, partials.shape[0] // size):
        gram = gram + partials[n * size : (n + 1) * size].astype(jnp.float32)
    stepped[...] = split_dot(gram, panel[...])
    norm = jnp.sum(jnp.sum(gram * gram, axis=1, keepdims=True), axis=0, keepdims=True)
    square[...] = jnp.broadcast_to(norm, square.shape)


def gram_of(panel):
    return dot(panel, panel, NT)


def shards(block_values, block_rows, block_cols, block_count, cell_factor, gene_factor):
    n_cell = lax.axis_size("cell")
    kdim = cell_factor.shape[0] * lax.axis_size("gene")
    size = gene_factor.shape[0]
    paired = size % 16 == 0 and n_cell >= 4 and n_cell & (n_cell - 1) == 0
    cell_at = lax.axis_index("cell")
    gene_at = lax.axis_index("gene")

    def swap(value, bits):
        return lax.ppermute(value, "cell", [(n, n ^ bits) for n in range(n_cell)])

    def swap_core(value):
        return lax.ppermute(value, "gene", [(0, 1), (1, 0)])

    def ints(values):
        return jnp.stack(values).astype(jnp.int32)

    low_share = gene_factor.astype(jnp.bfloat16)
    factor_other = swap_core(cell_factor)
    values = block_values[0, 0]
    tile, turned = dense_tile(values, block_rows[0, 0], block_cols[0, 0], block_count[0])
    half = kdim // 2
    if paired:
        lines = [1 << bit for bit in range(1, n_cell.bit_length() - 1)][::-1]
        far = {0: low_share}
        for bits in lines + [1]:
            far[bits] = swap(low_share, bits)
        first = sorted(range(n_cell), key=lambda bits: (bits.bit_count(), bits))
        first, second = first[: n_cell // 2], first[n_cell // 2 :]
        far[lines[0]], tile, turned, factor_other = lax.optimization_barrier(
            (far[lines[0]], tile, turned, factor_other)
        )
        for at, bits in enumerate(lines):
            for held in sorted(far):
                if held and held not in (1, bits) and held ^ bits not in far and held % (2 * bits) == 0:
                    far[held ^ bits] = swap(far[held], bits)
        for bits in range(2, n_cell, 2):
            far[bits ^ 1] = swap(far[bits], 1)
        owners = ints([cell_at ^ bits for bits in first + second])
        twice = [bits for bits in second if bits % 2 == 0]
        first_shares = [far[bits] for bits in first]
        first_shares[0], *ahead = lax.optimization_barrier((low_share, *[far[bits] for bits in twice]))
        far.update(zip(twice, ahead))
        second_shares = [far[bits] for bits in second]
    else:
        whole = lax.all_gather(low_share, "cell", axis=0, tiled=True)
        owners = jnp.arange(2, dtype=jnp.int32)
        first_shares, second_shares = [whole[:half]], [whole[half:]]

    panel_first, message_first = call(
        first_body,
        (shape((half, GENE_DEV), jnp.bfloat16), shape((half, CELL_DEV), jnp.float32)),
        0,
        1 + len(first_shares),
        0,
        0,
    )(turned, *first_shares)
    other_first = swap_core(message_first)
    if paired:
        other_first, *second_shares = lax.optimization_barrier((other_first, *second_shares))
    panel, message = call(
        second_body,
        (
            shape((kdim, GENE_DEV), jnp.bfloat16),
            shape((half, CELL_DEV + 2 * kdim), jnp.float32),
        ),
        1,
        2 + len(second_shares),
        2 * half * GENE_DEV * (CELL_DEV + 2 * kdim),
        8 * 2**20,
        [pltpu.VMEM((half, GENE_DEV), jnp.bfloat16)],
    )(owners, turned, panel_first, *second_shares)
    other = swap_core(message)

    through = list(range(n_cell - 2, 2, -2)) if paired else []
    order = [bits ^ 1 for bits in through] + [2, 3] + through + [1, 0] if paired else [0]
    rows = [size] * len(through) + [2 * size] if paired else []
    keeps = [size] * (len(through) + 2) if paired else []
    cell_next, next_low, gram, *parts = call(
        cell_body,
        (
            shape(cell_factor.shape, jnp.float32),
            shape((kdim, CELL_DEV), jnp.bfloat16),
            shape((kdim, kdim), jnp.bfloat16),
            *[shape((count, GENE_DEV), jnp.bfloat16) for count in rows],
            *[shape((count, GENE_DEV), jnp.float32) for count in keeps],
        ),
        3,
        7,
        2 * kdim * CELL_DEV * 3 * kdim + 2 * kdim * CELL_DEV * GENE_DEV,
        14 * 2**20,
        [
            pltpu.VMEM((kdim, CELL_DEV), jnp.float32),
            pltpu.VMEM((kdim, CELL_DEV), jnp.float32),
            pltpu.VMEM((kdim, CELL_DEV), jnp.float32),
            pltpu.VMEM((kdim, CELL_DEV), jnp.bfloat16),
        ],
    )(
        ints([gene_at]), owners, ints([cell_at ^ bits for bits in order]),
        tile, message_first, other_first, message, other, cell_factor, factor_other,
    )

    if not paired:
        cell_gram = lax.psum(gram_of(next_low), "cell")
        own_cols = lax.psum_scatter(dot(next_low, tile), "cell", scatter_dimension=0, tiled=True)
        gram_part = lax.dynamic_slice_in_dim(cell_gram, cell_at * size, size, 0)
        rate_gene = 1.0 / (jnp.sqrt(jnp.sum(cell_gram * cell_gram)) + 1e-06)
        stepped = jnp.dot(
            gram_part, panel.astype(jnp.float32), precision=lax.Precision.HIGHEST
        )
        return (cell_next, jnp.maximum(gene_factor - rate_gene * (stepped - own_cols), 0.0))

    sends, keeps = parts[: len(rows)], parts[len(rows) :]
    arrived = [swap(part, 1) for part in sends[:-1]]
    beside = swap(sends[-1], 2).astype(jnp.float32)
    moved = [(mine + part.astype(jnp.float32)).astype(jnp.bfloat16) for mine, part in zip(keeps, arrived)]
    near = (keeps[-2] + beside[size:]).astype(jnp.bfloat16)
    moved[0], gram = lax.optimization_barrier((moved[0], gram))
    partials = lax.all_to_all(gram, "cell", 0, 0, tiled=True)
    stepped, square = call(
        gram_body,
        (shape((size, GENE_DEV), jnp.float32), shape((8, 128), jnp.float32)),
        0,
        2,
        2 * size * kdim * GENE_DEV * 3,
        2 * 2**20,
    )(partials, panel)
    squares = lax.all_to_all(
        jnp.broadcast_to(square[None], (n_cell, 8, 128)), "cell", 0, 0, tiled=True
    )
    rate_gene = 1.0 / (jnp.sqrt(jnp.sum(squares[:, 0, 0])) + 1e-06)
    own_cols = keeps[-1] + beside[:size]
    for part, bits in zip(moved + [near], through + [1]):
        own_cols = own_cols + swap(part, bits).astype(jnp.float32)
    return (cell_next, jnp.maximum(gene_factor - rate_gene * (stepped - own_cols), 0.0))


def solution(mesh):
    return jax.shard_map(
        shards,
        mesh=mesh,
        in_specs=(
            P(("groups", "cell"), "gene", None, None, None),
            P(("groups", "cell"), "gene", None),
            P(("groups", "cell"), "gene", None),
            P(("groups", "cell"), "gene"),
            P(("groups", "gene"), "cell"),
            P(("groups", "cell"), "gene"),
        ),
        out_specs=(P(("groups", "gene"), "cell"), P(("groups", "cell"), "gene")),
        check_vma=False,
    )
```

```python
import functools

import jax
import jax.numpy as jnp
from jax import lax
from jax.experimental import pallas as pl
from jax.experimental.pallas import tpu as pltpu
from jax.sharding import PartitionSpec as P

BLK = 128
CELL_DEV = 1024
GENE_DEV = 2048
VMEM_BYTES = 24 * 2**20

NT = (((1,), (1,)), ((), ()))
NN = (((1,), (0,)), ((), ()))
SMEM_SPEC = pl.BlockSpec(memory_space=pltpu.SMEM)
VMEM_SPEC = pl.BlockSpec(memory_space=pltpu.VMEM)


def dot(a, b, dims=NN):
    return lax.dot_general(a, b, dims, preferred_element_type=jnp.float32)


def split_dot(a, b):
    high = a.astype(jnp.bfloat16)
    low = (a - high.astype(jnp.float32)).astype(jnp.bfloat16)
    rows = a.shape[0]
    both = dot(jnp.concatenate([high, low], axis=0), b)
    return both[:rows] + both[rows:]


def call(body, outs, n_smem, n_vmem, flops, traffic, scratch=()):
    return pl.pallas_call(
        body,
        out_shape=outs,
        in_specs=[SMEM_SPEC] * n_smem + [VMEM_SPEC] * n_vmem,
        out_specs=jax.tree.map(lambda _: VMEM_SPEC, outs),
        scratch_shapes=list(scratch),
        compiler_params=pltpu.CompilerParams(vmem_limit_bytes=VMEM_BYTES),
        cost_estimate=pl.CostEstimate(flops=flops, bytes_accessed=traffic, transcendentals=0),
    )


def shape(dims, dtype):
    return jax.ShapeDtypeStruct(dims, dtype)


def dense_body(turn, rows, cols, count, values, tile):
    tile[...] = jnp.zeros_like(tile)

    def place(n, carry):
        row = pl.multiple_of(rows[n] * BLK, BLK)
        col = pl.multiple_of(cols[n] * BLK, BLK)
        if turn:
            tile[pl.ds(col, BLK), pl.ds(row, BLK)] = values[n].T
        else:
            tile[pl.ds(row, BLK), pl.ds(col, BLK)] = values[n]
        return carry

    lax.fori_loop(0, count[0], place, 0)


def dense_tile(turn, values, rows, cols, count):
    dims = (GENE_DEV, CELL_DEV) if turn else (CELL_DEV, GENE_DEV)
    body = functools.partial(dense_body, turn)
    return call(body, shape(dims, jnp.bfloat16), 3, 1, 0, 0)(rows, cols, count, values)


def first_body(turned, *refs):
    shares, panel, message = refs[:-2], refs[-2], refs[-1]
    size = shares[0].shape[0]
    for n, part in enumerate(shares):
        panel[n * size : (n + 1) * size] = part[...]
    message[...] = dot(panel[...], turned[...])


def owned(bits, size):
    return pl.ds(pl.multiple_of((lax.axis_index("cell") ^ bits) * size, size), size)


def second_body(order, turned, first, *refs):
    shares, panel, message, chosen = refs[:-3], refs[-3], refs[-2], refs[-1]
    size, half = shares[0].shape[0], first.shape[0]
    for n, part in enumerate(shares):
        chosen[n * size : (n + 1) * size] = part[...]
    if order is None:
        panel[:half] = first[...]
        panel[half:] = chosen[...]
    else:
        for n, bits in enumerate(order):
            source = first if n * size < half else chosen
            panel[owned(bits, size)] = source[n * size % half : n * size % half + size]
    message[:, :CELL_DEV] = dot(chosen[...], turned[...])
    low = panel[...]
    gram = dot(low, low, NT)
    kdim = low.shape[0]
    message[:, CELL_DEV : CELL_DEV + kdim] = gram[:half]
    message[:, CELL_DEV + kdim :] = gram[half:]


def cell_body(
    order, picks, tile, mine_first, other_first, mine, other, factor_mine, factor_other,
    cell_next, low, gram_out, *rest
):
    parts, (factor, data, updated, chosen) = rest[:-4], rest[-4:]
    share = factor_mine.shape[0]
    kdim = factor.shape[0]
    half = mine.shape[0]
    core = lax.axis_index("gene")
    own = pl.ds(pl.multiple_of(core * share, share), share)
    theirs = pl.ds(pl.multiple_of((1 - core) * share, share), share)
    factor[own] = factor_mine[...]
    factor[theirs] = factor_other[...]
    if order is None:
        data[:half] = mine_first[...] + other_first[...]
        data[half:] = mine[:, :CELL_DEV] + other[:, :CELL_DEV]
    else:
        size = kdim // len(order)
        for n, bits in enumerate(order):
            rows = slice(n * size % half, n * size % half + size)
            if n * size < half:
                data[owned(bits, size)] = mine_first[rows] + other_first[rows]
            else:
                data[owned(bits, size)] = mine[rows, :CELL_DEV] + other[rows, :CELL_DEV]
    gram = mine[:, CELL_DEV:] + other[:, CELL_DEV:]
    gram = jnp.concatenate([gram[:, :kdim], gram[:, kdim:]], axis=0)
    norm = jnp.sum(jnp.sum(gram * gram, axis=1, keepdims=True), axis=0, keepdims=True)
    rate = 1.0 / (jnp.sqrt(norm) + 1e-06)
    held = factor[...]
    stepped = split_dot(gram, held.astype(jnp.bfloat16))
    updated[...] = jnp.maximum(held - rate * (stepped - data[...]), 0.0)
    cell_next[...] = updated[own]
    low[...] = updated[...].astype(jnp.bfloat16)
    gram_out[...] = dot(low[own], low[...], NT).astype(gram_out.dtype)
    if not parts:
        return
    for n, bits in enumerate(picks):
        chosen[n * size : (n + 1) * size] = low[owned(bits, size)]
    product = dot(chosen[...], tile[...])
    row = 0
    for out in parts:
        out[...] = product[row : row + out.shape[0]].astype(out.dtype)
        row += out.shape[0]


def gram_body(mine, other, panel, factor, base, rate_out, gram):
    share = mine.shape[0]
    core = lax.axis_index("gene")
    gram[pl.ds(pl.multiple_of(core * share, share), share)] = mine[...]
    gram[pl.ds(pl.multiple_of((1 - core) * share, share), share)] = other[...]
    whole = gram[...]
    norm = jnp.sum(jnp.sum(whole * whole, axis=1, keepdims=True), axis=0, keepdims=True)
    rate = 1.0 / (jnp.sqrt(norm) + 1e-06)
    base[...] = factor[...] - rate * split_dot(gram[owned(0, factor.shape[0])], panel[...])
    rate_out[...] = jnp.broadcast_to(rate, rate_out.shape)


def last_body(rate, base, own, beside, *refs):
    size = own.shape[0]
    total = own[...] + beside[:size].astype(jnp.float32)
    for part in refs[:-1]:
        total = total + part[...].astype(jnp.float32)
    refs[-1][...] = jnp.maximum(base[...] + rate[0:1, 0:1] * total, 0.0)


def gram_of(panel):
    return dot(panel, panel, NT)


def shards(block_values, block_rows, block_cols, block_count, cell_factor, gene_factor):
    n_cell = lax.axis_size("cell")
    kdim = cell_factor.shape[0] * lax.axis_size("gene")
    size = gene_factor.shape[0]
    half = kdim // 2
    paired = size % 16 == 0 and n_cell >= 4 and n_cell & (n_cell - 1) == 0

    def swap(value, bits):
        return lax.ppermute(value, "cell", [(n, n ^ bits) for n in range(n_cell)])

    def swap_core(value):
        return lax.ppermute(value, "gene", [(0, 1), (1, 0)])

    low_share = gene_factor.astype(jnp.bfloat16)
    factor_other = swap_core(cell_factor)
    blocks = (block_values[0, 0], block_rows[0, 0], block_cols[0, 0], block_count[0])
    turned = dense_tile(True, *blocks)
    tile = dense_tile(False, *blocks)
    if paired:
        lines = [1 << bit for bit in range(1, n_cell.bit_length() - 1)][::-1]
        far = {0: low_share}
        for bits in lines + [1]:
            far[bits] = swap(low_share, bits)
        first = sorted(range(n_cell), key=lambda bits: (bits.bit_count(), bits))
        first, second = first[: n_cell // 2], first[n_cell // 2 :]
        far[lines[0]], turned, factor_other = lax.optimization_barrier(
            (far[lines[0]], turned, factor_other)
        )
        for at, bits in enumerate(lines):
            for held in sorted(far):
                if held and held not in (1, bits) and held ^ bits not in far and held % (2 * bits) == 0:
                    far[held ^ bits] = swap(far[held], bits)
        for bits in range(2, n_cell, 2):
            far[bits ^ 1] = swap(far[bits], 1)
        order = first + second
        first_shares = [far[bits] for bits in first]
        second_shares = [far[bits] for bits in second]
    else:
        whole = lax.all_gather(low_share, "cell", axis=0, tiled=True)
        order = None
        first_shares, second_shares = [whole[:half]], [whole[half:]]

    panel_first, message_first = call(
        first_body,
        (shape((half, GENE_DEV), jnp.bfloat16), shape((half, CELL_DEV), jnp.float32)),
        0,
        1 + len(first_shares),
        0,
        0,
    )(turned, *first_shares)
    other_first = swap_core(message_first)
    if paired:
        other_first, tile, *second_shares = lax.optimization_barrier(
            (other_first, tile, *second_shares)
        )
    panel, message = call(
        functools.partial(second_body, order),
        (
            shape((kdim, GENE_DEV), jnp.bfloat16),
            shape((half, CELL_DEV + 2 * kdim), jnp.float32),
        ),
        0,
        2 + len(second_shares),
        2 * half * GENE_DEV * (CELL_DEV + 2 * kdim),
        8 * 2**20,
        [pltpu.VMEM((half, GENE_DEV), jnp.bfloat16)],
    )(turned, panel_first, *second_shares)
    other = swap_core(message)

    through = list(range(n_cell - 2, 2, -2)) if paired else []
    picks = [bits ^ 1 for bits in through] + [2, 3] + through + [1, 0]
    rows = [size] * len(through) + [2 * size] if paired else []
    keeps = [size] * (len(through) + 2) if paired else []
    cell_next, next_low, gram, *parts = call(
        functools.partial(cell_body, order, picks),
        (
            shape(cell_factor.shape, jnp.float32),
            shape((kdim, CELL_DEV), jnp.bfloat16),
            shape((half, kdim), jnp.bfloat16),
            *[shape((count, GENE_DEV), jnp.bfloat16) for count in rows],
            *[shape((count, GENE_DEV), jnp.float32) for count in keeps],
        ),
        0,
        7,
        2 * kdim * CELL_DEV * 3 * kdim + 2 * kdim * CELL_DEV * GENE_DEV,
        14 * 2**20,
        [
            pltpu.VMEM((kdim, CELL_DEV), jnp.float32),
            pltpu.VMEM((kdim, CELL_DEV), jnp.float32),
            pltpu.VMEM((kdim, CELL_DEV), jnp.float32),
            pltpu.VMEM((kdim, CELL_DEV), jnp.bfloat16),
        ],
    )(tile, message_first, other_first, message, other, cell_factor, factor_other)

    if not paired:
        cell_gram = lax.psum(gram_of(next_low), "cell")
        own_cols = lax.psum_scatter(dot(next_low, tile), "cell", scatter_dimension=0, tiled=True)
        gram_part = lax.dynamic_slice_in_dim(cell_gram, lax.axis_index("cell") * size, size, 0)
        rate_gene = 1.0 / (jnp.sqrt(jnp.sum(cell_gram * cell_gram)) + 1e-06)
        stepped = jnp.dot(
            gram_part, panel.astype(jnp.float32), precision=lax.Precision.HIGHEST
        )
        return (cell_next, jnp.maximum(gene_factor - rate_gene * (stepped - own_cols), 0.0))

    sends, keeps = parts[: len(rows)], parts[len(rows) :]
    arrived = [swap(part, 1) for part in sends[:-1]]
    beside = swap(sends[-1], 2)
    moved = [(mine + part.astype(jnp.float32)).astype(jnp.bfloat16) for mine, part in zip(keeps, arrived)]
    near = (keeps[-2] + beside[size:].astype(jnp.float32)).astype(jnp.bfloat16)
    for bits in [1] + lines[::-1]:
        gram = gram.astype(jnp.bfloat16)
        partner = swap(gram, bits)
        if bits == 1:
            partner, moved[0] = lax.optimization_barrier((partner, moved[0]))
        gram = gram.astype(jnp.float32) + partner.astype(jnp.float32)
    base, rate = call(
        gram_body,
        (shape((size, GENE_DEV), jnp.float32), shape((8, 128), jnp.float32)),
        0,
        4,
        0,
        0,
        [pltpu.VMEM((kdim, kdim), jnp.float32)],
    )(gram, swap_core(gram), panel, gene_factor)
    sums = [swap(part, bits) for part, bits in zip(moved + [near], through + [1])]
    gene_next = call(
        last_body, shape((size, GENE_DEV), jnp.float32), 0, 4 + len(sums), 0, 0
    )(rate, base, keeps[-1], beside, *sums)
    return (cell_next, gene_next)


def solution(mesh):
    return jax.shard_map(
        shards,
        mesh=mesh,
        in_specs=(
            P(("groups", "cell"), "gene", None, None, None),
            P(("groups", "cell"), "gene", None),
            P(("groups", "cell"), "gene", None),
            P(("groups", "cell"), "gene"),
            P(("groups", "gene"), "cell"),
            P(("groups", "cell"), "gene"),
        ),
        out_specs=(P(("groups", "gene"), "cell"), P(("groups", "cell"), "gene")),
        check_vma=False,
    )
```

```python
import functools

import jax
import jax.numpy as jnp
from jax import lax
from jax.experimental import pallas as pl
from jax.experimental.pallas import tpu as pltpu
from jax.sharding import PartitionSpec as P

BLK = 128
CELL_DEV = 1024
GENE_DEV = 2048
VMEM_BYTES = 24 * 2**20

NT = (((1,), (1,)), ((), ()))
NN = (((1,), (0,)), ((), ()))
SMEM_SPEC = pl.BlockSpec(memory_space=pltpu.SMEM)
VMEM_SPEC = pl.BlockSpec(memory_space=pltpu.VMEM)


def dot(a, b, dims=NN):
    return lax.dot_general(a, b, dims, preferred_element_type=jnp.float32)


def split_dot(a, b):
    high = a.astype(jnp.bfloat16)
    low = (a - high.astype(jnp.float32)).astype(jnp.bfloat16)
    rows = a.shape[0]
    both = dot(jnp.concatenate([high, low], axis=0), b)
    return both[:rows] + both[rows:]


def call(body, outs, n_smem, n_vmem, flops, traffic, scratch=()):
    return pl.pallas_call(
        body,
        out_shape=outs,
        in_specs=[SMEM_SPEC] * n_smem + [VMEM_SPEC] * n_vmem,
        out_specs=jax.tree.map(lambda _: VMEM_SPEC, outs),
        scratch_shapes=list(scratch),
        compiler_params=pltpu.CompilerParams(vmem_limit_bytes=VMEM_BYTES),
        cost_estimate=pl.CostEstimate(flops=flops, bytes_accessed=traffic, transcendentals=0),
    )


def shape(dims, dtype):
    return jax.ShapeDtypeStruct(dims, dtype)


def dense_body(rows_in, cols_in, count, values, tile, rows, cols, sems, index_sems):
    copies = [
        pltpu.make_async_copy(rows_in, rows, index_sems.at[0]),
        pltpu.make_async_copy(cols_in, cols, index_sems.at[1]),
    ]
    for copy in copies:
        copy.start()
    tile[...] = jnp.zeros_like(tile)
    for copy in copies:
        copy.wait()

    def block(n):
        row = pl.multiple_of(rows[n] * BLK, BLK)
        col = pl.multiple_of(cols[n] * BLK, BLK)
        place = tile.at[pl.ds(row, BLK), pl.ds(col, BLK)]
        return pltpu.make_async_copy(values.at[n], place, sems.at[n])

    def start(n, carry):
        block(n).start()
        return carry

    def wait(n, carry):
        block(n).wait()
        return carry

    lax.fori_loop(0, count[0], start, 0)
    lax.fori_loop(0, count[0], wait, 0)


def dense_tile(values, rows, cols, count):
    anywhere = pl.BlockSpec(memory_space=pl.ANY)
    n_blocks = values.shape[0]
    return pl.pallas_call(
        dense_body,
        out_shape=shape((CELL_DEV, GENE_DEV), jnp.bfloat16),
        in_specs=[anywhere, anywhere, SMEM_SPEC, anywhere],
        out_specs=VMEM_SPEC,
        scratch_shapes=[
            pltpu.SMEM((n_blocks,), jnp.int32),
            pltpu.SMEM((n_blocks,), jnp.int32),
            pltpu.SemaphoreType.DMA((n_blocks,)),
            pltpu.SemaphoreType.DMA((2,)),
        ],
        compiler_params=pltpu.CompilerParams(vmem_limit_bytes=VMEM_BYTES),
        cost_estimate=pl.CostEstimate(flops=0, bytes_accessed=0, transcendentals=0),
    )(rows, cols, count, values)


def owned(bits, size):
    return pl.ds(pl.multiple_of((lax.axis_index("cell") ^ bits) * size, size), size)


def join_body(*refs):
    row = 0
    for part in refs[:-1]:
        refs[-1][row : row + part.shape[0]] = part[...]
        row += part.shape[0]


def gene_body(order, tile, *refs):
    shares, (panel, mine, message) = refs[:-3], refs[-3:]
    if order is None:
        panel[...] = shares[0][...]
    else:
        size = panel.shape[0] // len(order)
        row = 0
        for part in shares:
            for at in range(0, part.shape[0], size):
                panel[owned(order[row], size)] = part[at : at + size]
                row += 1
    low = panel[...]
    mine[:, :CELL_DEV] = dot(low, tile[...], NT)
    mine[:, CELL_DEV:] = dot(low, low, NT)
    message[...] = mine[...].astype(message.dtype)


def cell_body(picks, tile, mine, other, factor_mine, factor_other, cell_next, low, *rest):
    (first, *sends, gram_out), (factor, updated, chosen) = rest[:-3] or (None, None), rest[-3:]
    share = factor_mine.shape[0]
    core = lax.axis_index("gene")
    own = pl.ds(pl.multiple_of(core * share, share), share)
    theirs = pl.ds(pl.multiple_of((1 - core) * share, share), share)
    factor[own] = factor_mine[...]
    factor[theirs] = factor_other[...]
    gram = mine[:, CELL_DEV:] + other[:, CELL_DEV:].astype(jnp.float32)
    norm = jnp.sum(jnp.sum(gram * gram, axis=1, keepdims=True), axis=0, keepdims=True)
    rate = 1.0 / (jnp.sqrt(norm) + 1e-06)
    held = factor[...]
    stepped = split_dot(gram, held.astype(jnp.bfloat16))
    data = mine[:, :CELL_DEV] + other[:, :CELL_DEV].astype(jnp.float32)
    updated[...] = jnp.maximum(held - rate * (stepped - data), 0.0)
    cell_next[...] = updated[own]
    low[...] = updated[...].astype(jnp.bfloat16)
    if not sends:
        return
    size = chosen.shape[0] // len(picks)
    picked_product(picks, low, tile, chosen, [first.at[:size], *sends])
    own_gram = dot(low[own], low[...], NT)
    rows, width = gram_out.shape[0], own_gram.shape[1]
    for n in range(share // rows):
        gram_out[:, n * width : (n + 1) * width] = own_gram[n * rows : (n + 1) * rows]
    first[size:] = gram_out[...].astype(first.dtype)


def picked_product(picks, low, tile, chosen, parts):
    size = chosen.shape[0] // len(picks)
    for n, bits in enumerate(picks):
        chosen[n * size : (n + 1) * size] = low[owned(bits, size)]
    product = dot(chosen[...], tile[...])
    row = 0
    for out in parts:
        out[...] = product[row : row + out.shape[0]].astype(out.dtype)
        row += out.shape[0]


def keep_body(picks, low, tile, *rest):
    picked_product(picks, low, tile, rest[-1], rest[:-1])


def pass_body(keep, arrived, gram, gram_arrived, out):
    size = keep.shape[0]
    out[:size] = (keep[...] + arrived[...].astype(jnp.float32)).astype(out.dtype)
    gram_sum = gram[...].astype(jnp.float32) + gram_arrived[...].astype(jnp.float32)
    out[size:] = gram_sum.astype(out.dtype)


def gram_body(mine, other, panel, factor, base, rate_out, gram):
    rows, width = mine.shape[0], gram.shape[1]
    core = lax.axis_index("gene")
    for half, part in ((core, mine), (1 - core, other)):
        for n in range(part.shape[1] // width):
            row = pl.multiple_of(half * (gram.shape[0] // 2) + n * rows, rows)
            gram[pl.ds(row, rows)] = part[:, n * width : (n + 1) * width]
    whole = gram[...]
    norm = jnp.sum(jnp.sum(whole * whole, axis=1, keepdims=True), axis=0, keepdims=True)
    rate = 1.0 / (jnp.sqrt(norm) + 1e-06)
    base[...] = factor[...] - rate * split_dot(gram[owned(0, factor.shape[0])], panel[...])
    rate_out[...] = jnp.broadcast_to(rate, rate_out.shape)


def last_body(rate, base, own, beside, third, second, last, out):
    size = own.shape[0]
    total = own[...]
    for part in (beside, third, second, last):
        total = total + part[:size].astype(jnp.float32)
    out[...] = jnp.maximum(base[...] + rate[0:1, 0:1] * total, 0.0)


def gram_of(panel):
    return dot(panel, panel, NT)


def shards(block_values, block_rows, block_cols, block_count, cell_factor, gene_factor):
    n_cell = lax.axis_size("cell")
    kdim = cell_factor.shape[0] * lax.axis_size("gene")
    size = gene_factor.shape[0]
    half = kdim // 2
    gram_rows = half * kdim // GENE_DEV
    paired = n_cell == 8 and size % 16 == 0 and gram_rows % 16 == 0

    def swap(value, bits):
        return lax.ppermute(value, "cell", [(n, n ^ bits) for n in range(n_cell)])

    def swap_core(value):
        return lax.ppermute(value, "gene", [(0, 1), (1, 0)])

    def wide(rows, dtype):
        return shape((rows, GENE_DEV), dtype)

    low_share = gene_factor.astype(jnp.bfloat16)
    factor_other = swap_core(cell_factor)
    tile = dense_tile(block_values[0, 0], block_rows[0, 0], block_cols[0, 0], block_count[0])
    if paired:
        near = [swap(low_share, bits) for bits in (1, 2, 4)]
        beside, second, fourth, tile, factor_other = lax.optimization_barrier((*near, tile, factor_other))
        sixth = swap(fourth, 2)
        both = call(join_body, wide(2 * size, jnp.bfloat16), 0, 2, 0, 0)(second, fourth)
        shares = [low_share, beside, both, swap(both, 1), sixth, swap(sixth, 1)]
        order = [0, 1, 2, 4, 3, 5, 6, 7]
    else:
        shares = [lax.all_gather(low_share, "cell", axis=0, tiled=True)]
        order = None

    panel, mine, message = call(
        functools.partial(gene_body, order),
        (
            wide(kdim, jnp.bfloat16),
            shape((kdim, CELL_DEV + kdim), jnp.float32),
            shape((kdim, CELL_DEV + kdim), jnp.bfloat16),
        ),
        0,
        1 + len(shares),
        0,
        0,
    )(tile, *shares)
    other = swap_core(message)

    sent = [7, 5, 2, 3]
    kept = [6, 4, 1, 0]
    cell_next, next_low, *sends = call(
        functools.partial(cell_body, sent),
        (
            shape(cell_factor.shape, jnp.float32),
            shape((kdim, CELL_DEV), jnp.bfloat16),
            *(
                [
                    wide(size + gram_rows, jnp.bfloat16),
                    wide(size, jnp.bfloat16),
                    wide(2 * size, jnp.bfloat16),
                    wide(gram_rows, jnp.float32),
                ]
                if paired
                else []
            ),
        ),
        0,
        5,
        0,
        0,
        [
            pltpu.VMEM((kdim, CELL_DEV), jnp.float32),
            pltpu.VMEM((kdim, CELL_DEV), jnp.float32),
            pltpu.VMEM((half, CELL_DEV), jnp.bfloat16),
        ],
    )(tile, mine, other, cell_factor, factor_other)

    if not paired:
        cell_gram = lax.psum(gram_of(next_low), "cell")
        own_cols = lax.psum_scatter(dot(next_low, tile), "cell", scatter_dimension=0, tiled=True)
        gram_part = lax.dynamic_slice_in_dim(cell_gram, lax.axis_index("cell") * size, size, 0)
        rate_gene = 1.0 / (jnp.sqrt(jnp.sum(cell_gram * cell_gram)) + 1e-06)
        stepped = jnp.dot(
            gram_part, panel.astype(jnp.float32), precision=lax.Precision.HIGHEST
        )
        return (cell_next, jnp.maximum(gene_factor - rate_gene * (stepped - own_cols), 0.0))

    arrived_third, arrived_second = swap(sends[0], 1), swap(sends[1], 1)
    beside = swap(sends[2], 2)
    keeps = call(
        functools.partial(keep_body, kept),
        tuple(wide(size, jnp.float32) for _ in kept),
        0,
        2,
        0,
        0,
        [pltpu.VMEM((half, CELL_DEV), jnp.bfloat16)],
    )(next_low, tile)
    third = swap((keeps[0] + arrived_third[:size].astype(jnp.float32)).astype(jnp.bfloat16), 6)
    gram = (sends[3] + arrived_third[size:].astype(jnp.float32)).astype(jnp.bfloat16)
    message = call(pass_body, wide(size + gram_rows, jnp.bfloat16), 0, 4, 0, 0)(
        keeps[1], arrived_second, gram, swap(gram, 2)
    )
    second = swap(message, 4)
    last = swap((keeps[2] + beside[size:].astype(jnp.float32)).astype(jnp.bfloat16), 1)
    last, second, third = lax.optimization_barrier((last, second, third))
    gram = message[size:].astype(jnp.float32) + second[size:].astype(jnp.float32)
    base, rate = call(
        gram_body,
        (wide(size, jnp.float32), shape((8, 128), jnp.float32)),
        0,
        4,
        0,
        0,
        [pltpu.VMEM((kdim, kdim), jnp.float32)],
    )(gram, swap_core(gram), panel, gene_factor)
    gene_next = call(last_body, wide(size, jnp.float32), 0, 7, 0, 0)(
        rate, base, keeps[3], beside, third, second, last
    )
    return (cell_next, gene_next)


def solution(mesh):
    return jax.shard_map(
        shards,
        mesh=mesh,
        in_specs=(
            P(("groups", "cell"), "gene", None, None, None),
            P(("groups", "cell"), "gene", None),
            P(("groups", "cell"), "gene", None),
            P(("groups", "cell"), "gene"),
            P(("groups", "gene"), "cell"),
            P(("groups", "cell"), "gene"),
        ),
        out_specs=(P(("groups", "gene"), "cell"), P(("groups", "cell"), "gene")),
        check_vma=False,
    )
```

```python
import functools

import jax
import jax.numpy as jnp
from jax import lax
from jax.experimental import pallas as pl
from jax.experimental.pallas import tpu as pltpu
from jax.sharding import PartitionSpec as P

BLK = 128
CELL_DEV = 1024
GENE_DEV = 2048
VMEM_BYTES = 24 * 2**20

NT = (((1,), (1,)), ((), ()))
NN = (((1,), (0,)), ((), ()))
SMEM_SPEC = pl.BlockSpec(memory_space=pltpu.SMEM)
VMEM_SPEC = pl.BlockSpec(memory_space=pltpu.VMEM)


def dot(a, b, dims=NN):
    return lax.dot_general(a, b, dims, preferred_element_type=jnp.float32)


def split_dot(a, b):
    high = a.astype(jnp.bfloat16)
    low = (a - high.astype(jnp.float32)).astype(jnp.bfloat16)
    rows = a.shape[0]
    both = dot(jnp.concatenate([high, low], axis=0), b)
    return both[:rows] + both[rows:]


def call(body, outs, n_smem, n_vmem, flops, traffic, scratch=()):
    return pl.pallas_call(
        body,
        out_shape=outs,
        in_specs=[SMEM_SPEC] * n_smem + [VMEM_SPEC] * n_vmem,
        out_specs=jax.tree.map(lambda _: VMEM_SPEC, outs),
        scratch_shapes=list(scratch),
        compiler_params=pltpu.CompilerParams(vmem_limit_bytes=VMEM_BYTES),
        cost_estimate=pl.CostEstimate(flops=flops, bytes_accessed=traffic, transcendentals=0),
    )


def shape(dims, dtype):
    return jax.ShapeDtypeStruct(dims, dtype)


def dense_body(rows_in, cols_in, count, values, tile, rows, cols, sems, index_sems):
    copies = [
        pltpu.make_async_copy(rows_in, rows, index_sems.at[0]),
        pltpu.make_async_copy(cols_in, cols, index_sems.at[1]),
    ]
    for copy in copies:
        copy.start()
    tile[...] = jnp.zeros_like(tile)
    for copy in copies:
        copy.wait()

    def block(n):
        row = pl.multiple_of(rows[n] * BLK, BLK)
        col = pl.multiple_of(cols[n] * BLK, BLK)
        place = tile.at[pl.ds(row, BLK), pl.ds(col, BLK)]
        return pltpu.make_async_copy(values.at[n], place, sems.at[n])

    def start(n, carry):
        block(n).start()
        return carry

    def wait(n, carry):
        block(n).wait()
        return carry

    lax.fori_loop(0, count[0], start, 0)
    lax.fori_loop(0, count[0], wait, 0)


def dense_tile(values, rows, cols, count):
    anywhere = pl.BlockSpec(memory_space=pl.ANY)
    n_blocks = values.shape[0]
    return pl.pallas_call(
        dense_body,
        out_shape=shape((CELL_DEV, GENE_DEV), jnp.bfloat16),
        in_specs=[anywhere, anywhere, SMEM_SPEC, anywhere],
        out_specs=VMEM_SPEC,
        scratch_shapes=[
            pltpu.SMEM((n_blocks,), jnp.int32),
            pltpu.SMEM((n_blocks,), jnp.int32),
            pltpu.SemaphoreType.DMA((n_blocks,)),
            pltpu.SemaphoreType.DMA((2,)),
        ],
        compiler_params=pltpu.CompilerParams(vmem_limit_bytes=VMEM_BYTES),
        cost_estimate=pl.CostEstimate(flops=0, bytes_accessed=0, transcendentals=0),
    )(rows, cols, count, values)


def owned(bits, size):
    return pl.ds(pl.multiple_of((lax.axis_index("cell") ^ bits) * size, size), size)


def join_body(*refs):
    row = 0
    for part in refs[:-1]:
        refs[-1][row : row + part.shape[0]] = part[...]
        row += part.shape[0]


def gene_body(order, tile, *refs):
    shares, (panel, mine, message) = refs[:-3], refs[-3:]
    if order is None:
        panel[...] = shares[0][...]
    else:
        size = panel.shape[0] // len(order)
        row = 0
        for part in shares:
            for at in range(0, part.shape[0], size):
                panel[owned(order[row], size)] = part[at : at + size]
                row += 1
    low = panel[...]
    mine[:, :CELL_DEV] = dot(low, tile[...], NT)
    mine[:, CELL_DEV:] = dot(low, low, NT)
    message[...] = mine[...].astype(message.dtype)


def cell_body(picks, tile, mine, other, factor_mine, factor_other, cell_next, low, *rest):
    sends, (factor, updated, chosen) = rest[:-3], rest[-3:]
    share = factor_mine.shape[0]
    core = lax.axis_index("gene")
    own = pl.ds(pl.multiple_of(core * share, share), share)
    theirs = pl.ds(pl.multiple_of((1 - core) * share, share), share)
    factor[own] = factor_mine[...]
    factor[theirs] = factor_other[...]
    gram = mine[:, CELL_DEV:] + other[:, CELL_DEV:].astype(jnp.float32)
    norm = jnp.sum(jnp.sum(gram * gram, axis=1, keepdims=True), axis=0, keepdims=True)
    rate = 1.0 / (jnp.sqrt(norm) + 1e-06)
    held = factor[...]
    stepped = split_dot(gram, held.astype(jnp.bfloat16))
    data = mine[:, :CELL_DEV] + other[:, :CELL_DEV].astype(jnp.float32)
    updated[...] = jnp.maximum(held - rate * (stepped - data), 0.0)
    cell_next[...] = updated[own]
    low[...] = updated[...].astype(jnp.bfloat16)
    if not sends:
        return
    picked_product(picks, low, tile, chosen, sends)


def picked_product(picks, low, tile, chosen, parts):
    size = chosen.shape[0] // len(picks)
    for n, bits in enumerate(picks):
        chosen[n * size : (n + 1) * size] = low[owned(bits, size)]
    product = dot(chosen[...], tile[...])
    row = 0
    for out in parts:
        out[...] = product[row : row + out.shape[0]].astype(out.dtype)
        row += out.shape[0]


def keep_body(picks, low, tile, gram, *rest):
    picked_product(picks, low, tile, rest[-1], rest[:-1])
    share = low.shape[0] // 2
    own = pl.ds(pl.multiple_of(lax.axis_index("gene") * share, share), share)
    half = dot(low[own], low[...], NT).astype(gram.dtype)
    rows, width = gram.shape[0], half.shape[1]
    for n in range(share // rows):
        gram[:, n * width : (n + 1) * width] = half[n * rows : (n + 1) * rows]


def sum_body(keep, arrived, out):
    out[...] = (keep[...] + arrived[...].astype(jnp.float32)).astype(out.dtype)


def turn_body(keep, own, beside, third, out, partial):
    size = own.shape[0]
    out[...] = (keep[...] + beside[size:].astype(jnp.float32)).astype(out.dtype)
    partial[...] = own[...] + beside[:size].astype(jnp.float32) + third[...].astype(jnp.float32)


def last_body(mine, other, panel, factor, partial, second, last, out, gram):
    rows, width = mine.shape[0], gram.shape[1]
    core = lax.axis_index("gene")
    for half, part in ((core, mine), (1 - core, other)):
        for n in range(part.shape[1] // width):
            row = pl.multiple_of(half * (gram.shape[0] // 2) + n * rows, rows)
            gram[pl.ds(row, rows)] = part[:, n * width : (n + 1) * width]
    whole = gram[...]
    norm = jnp.sum(jnp.sum(whole * whole, axis=1, keepdims=True), axis=0, keepdims=True)
    rate = 1.0 / (jnp.sqrt(norm) + 1e-06)
    stepped = split_dot(gram[owned(0, factor.shape[0])], panel[...])
    data = partial[...] + second[...].astype(jnp.float32) + last[...].astype(jnp.float32)
    out[...] = jnp.maximum(factor[...] - rate * (stepped - data), 0.0)


def gram_of(panel):
    return dot(panel, panel, NT)


def shards(block_values, block_rows, block_cols, block_count, cell_factor, gene_factor):
    n_cell = lax.axis_size("cell")
    kdim = cell_factor.shape[0] * lax.axis_size("gene")
    size = gene_factor.shape[0]
    half = kdim // 2
    gram_rows = half * kdim // GENE_DEV
    paired = n_cell == 8 and size % 16 == 0 and gram_rows % 16 == 0

    def swap(value, bits):
        return lax.ppermute(value, "cell", [(n, n ^ bits) for n in range(n_cell)])

    def swap_core(value):
        return lax.ppermute(value, "gene", [(0, 1), (1, 0)])

    def wide(rows, dtype):
        return shape((rows, GENE_DEV), dtype)

    low_share = gene_factor.astype(jnp.bfloat16)
    tile = dense_tile(block_values[0, 0], block_rows[0, 0], block_cols[0, 0], block_count[0])
    if paired:
        near = [swap(low_share, bits) for bits in (1, 2, 4)]
        beside, second, fourth = lax.optimization_barrier(near)
        sixth = swap(fourth, 2)
        both = call(join_body, wide(2 * size, jnp.bfloat16), 0, 2, 0, 0)(second, fourth)
        both, factor = lax.optimization_barrier((both, cell_factor))
        shares = [low_share, beside, both, swap(both, 1), sixth, swap(sixth, 1)]
        order = [0, 1, 2, 4, 3, 5, 6, 7]
    else:
        shares = [lax.all_gather(low_share, "cell", axis=0, tiled=True)]
        order, factor = None, cell_factor
    factor_other = swap_core(factor)

    shares[0], factor_other = lax.optimization_barrier((shares[0], factor_other))
    panel, mine, message = call(
        functools.partial(gene_body, order),
        (
            wide(kdim, jnp.bfloat16),
            shape((kdim, CELL_DEV + kdim), jnp.float32),
            shape((kdim, CELL_DEV + kdim), jnp.bfloat16),
        ),
        0,
        1 + len(shares),
        0,
        0,
    )(tile, *shares)
    other = swap_core(message)

    sent = [7, 5, 2, 3]
    kept = [6, 4, 1, 0]
    cell_next, next_low, *sends = call(
        functools.partial(cell_body, sent),
        (
            shape(cell_factor.shape, jnp.float32),
            shape((kdim, CELL_DEV), jnp.bfloat16),
            *(
                [
                    wide(size, jnp.bfloat16),
                    wide(size, jnp.bfloat16),
                    wide(2 * size, jnp.bfloat16),
                ]
                if paired
                else []
            ),
        ),
        0,
        5,
        0,
        0,
        [
            pltpu.VMEM((kdim, CELL_DEV), jnp.float32),
            pltpu.VMEM((kdim, CELL_DEV), jnp.float32),
            pltpu.VMEM((half, CELL_DEV), jnp.bfloat16),
        ],
    )(tile, mine, other, cell_factor, factor_other)

    if not paired:
        cell_gram = lax.psum(gram_of(next_low), "cell")
        own_cols = lax.psum_scatter(dot(next_low, tile), "cell", scatter_dimension=0, tiled=True)
        gram_part = lax.dynamic_slice_in_dim(cell_gram, lax.axis_index("cell") * size, size, 0)
        rate_gene = 1.0 / (jnp.sqrt(jnp.sum(cell_gram * cell_gram)) + 1e-06)
        stepped = jnp.dot(
            gram_part, panel.astype(jnp.float32), precision=lax.Precision.HIGHEST
        )
        return (cell_next, jnp.maximum(gene_factor - rate_gene * (stepped - own_cols), 0.0))

    arrived_third, arrived_second = swap(sends[0], 1), swap(sends[1], 1)
    beside = swap(sends[2], 2)
    gram, *keeps = call(
        functools.partial(keep_body, kept),
        (wide(gram_rows, jnp.bfloat16), *[wide(size, jnp.float32) for _ in kept]),
        0,
        2,
        0,
        16 * 2**20,
        [pltpu.VMEM((half, CELL_DEV), jnp.bfloat16)],
    )(next_low, tile)
    gram_arrived = swap(gram, 4)
    third = call(sum_body, wide(size, jnp.bfloat16), 0, 2, 0, 16 * 2**20)(keeps[0], arrived_third)
    gram_arrived, third = lax.optimization_barrier((gram_arrived, third))
    third = swap(third, 6)
    gram = (gram.astype(jnp.float32) + gram_arrived.astype(jnp.float32)).astype(jnp.bfloat16)
    gram_arrived = swap(gram, 2)
    beside, arrived_second = lax.optimization_barrier((beside, arrived_second))
    second = call(sum_body, wide(size, jnp.bfloat16), 0, 2, 0, 16 * 2**20)(keeps[1], arrived_second)
    gram_arrived, second = lax.optimization_barrier((gram_arrived, second))
    second = swap(second, 4)
    gram = (gram.astype(jnp.float32) + gram_arrived.astype(jnp.float32)).astype(jnp.bfloat16)
    message, partial = call(
        turn_body, (wide(size, jnp.bfloat16), wide(size, jnp.float32)), 0, 4, 0, 16 * 2**20
    )(keeps[2], keeps[3], beside, third)
    last = swap(message, 1)
    gram_arrived, second = lax.optimization_barrier((swap(gram, 1), second))
    gram = gram.astype(jnp.float32) + gram_arrived.astype(jnp.float32)
    gene_next = call(
        last_body,
        wide(size, jnp.float32),
        0,
        7,
        0,
        0,
        [pltpu.VMEM((kdim, kdim), jnp.float32)],
    )(gram, swap_core(gram), panel, gene_factor, partial, second, last)
    return (cell_next, gene_next)


def solution(mesh):
    return jax.shard_map(
        shards,
        mesh=mesh,
        in_specs=(
            P(("groups", "cell"), "gene", None, None, None),
            P(("groups", "cell"), "gene", None),
            P(("groups", "cell"), "gene", None),
            P(("groups", "cell"), "gene"),
            P(("groups", "gene"), "cell"),
            P(("groups", "cell"), "gene"),
        ),
        out_specs=(P(("groups", "gene"), "cell"), P(("groups", "cell"), "gene")),
        check_vma=False,
    )
```

```python
import functools

import jax
import jax.numpy as jnp
from jax import lax
from jax.experimental import pallas as pl
from jax.experimental.pallas import tpu as pltpu
from jax.sharding import PartitionSpec as P

BLK = 128
CELL_DEV = 1024
GENE_DEV = 2048
VMEM_BYTES = 24 * 2**20
AHEAD = 16 * 2**20

NT = (((1,), (1,)), ((), ()))
NN = (((1,), (0,)), ((), ()))
SMEM_SPEC = pl.BlockSpec(memory_space=pltpu.SMEM)
VMEM_SPEC = pl.BlockSpec(memory_space=pltpu.VMEM)


def dot(a, b, dims=NN):
    return lax.dot_general(a, b, dims, preferred_element_type=jnp.float32)


def split_dot(a, b):
    high = a.astype(jnp.bfloat16)
    low = (a - high.astype(jnp.float32)).astype(jnp.bfloat16)
    rows = a.shape[0]
    both = dot(jnp.concatenate([high, low], axis=0), b)
    return both[:rows] + both[rows:]


def call(body, outs, n_smem, n_vmem, flops, traffic, scratch=()):
    return pl.pallas_call(
        body,
        out_shape=outs,
        in_specs=[SMEM_SPEC] * n_smem + [VMEM_SPEC] * n_vmem,
        out_specs=jax.tree.map(lambda _: VMEM_SPEC, outs),
        scratch_shapes=list(scratch),
        compiler_params=pltpu.CompilerParams(vmem_limit_bytes=VMEM_BYTES),
        cost_estimate=pl.CostEstimate(flops=flops, bytes_accessed=traffic, transcendentals=0),
    )


def shape(dims, dtype):
    return jax.ShapeDtypeStruct(dims, dtype)


def dense_body(rows_in, cols_in, count, values, tile, rows, cols, sems, index_sems):
    copies = [
        pltpu.make_async_copy(rows_in, rows, index_sems.at[0]),
        pltpu.make_async_copy(cols_in, cols, index_sems.at[1]),
    ]
    for copy in copies:
        copy.start()
    tile[...] = jnp.zeros_like(tile)
    for copy in copies:
        copy.wait()

    def block(n):
        row = pl.multiple_of(rows[n] * BLK, BLK)
        col = pl.multiple_of(cols[n] * BLK, BLK)
        place = tile.at[pl.ds(row, BLK), pl.ds(col, BLK)]
        return pltpu.make_async_copy(values.at[n], place, sems.at[n])

    def start(n, carry):
        block(n).start()
        return carry

    def wait(n, carry):
        block(n).wait()
        return carry

    lax.fori_loop(0, count[0], start, 0)
    lax.fori_loop(0, count[0], wait, 0)


def pinned(array):
    return pltpu.with_memory_space_constraint(array, pltpu.HBM)


def dense_tile(values, rows, cols, count):
    anywhere = pl.BlockSpec(memory_space=pltpu.HBM)
    n_blocks = values.shape[0]
    return pl.pallas_call(
        dense_body,
        out_shape=shape((CELL_DEV, GENE_DEV), jnp.bfloat16),
        in_specs=[anywhere, anywhere, SMEM_SPEC, anywhere],
        out_specs=VMEM_SPEC,
        scratch_shapes=[
            pltpu.SMEM((n_blocks,), jnp.int32),
            pltpu.SMEM((n_blocks,), jnp.int32),
            pltpu.SemaphoreType.DMA((n_blocks,)),
            pltpu.SemaphoreType.DMA((2,)),
        ],
        compiler_params=pltpu.CompilerParams(vmem_limit_bytes=VMEM_BYTES),
        cost_estimate=pl.CostEstimate(flops=0, bytes_accessed=AHEAD, transcendentals=0),
    )(pinned(rows), pinned(cols), count, pinned(values))


def owned(bits, size):
    return pl.ds(pl.multiple_of((lax.axis_index("cell") ^ bits) * size, size), size)


def join_body(*refs):
    row = 0
    for part in refs[:-1]:
        refs[-1][row : row + part.shape[0]] = part[...]
        row += part.shape[0]


def gene_body(order, tile, *refs):
    shares, (panel, mine, message) = refs[:-3], refs[-3:]
    if order is None:
        panel[...] = shares[0][...]
    else:
        size = panel.shape[0] // len(order)
        row = 0
        for part in shares:
            for at in range(0, part.shape[0], size):
                panel[owned(order[row], size)] = part[at : at + size]
                row += 1
    low = panel[...]
    mine[:, :CELL_DEV] = dot(low, tile[...], NT)
    mine[:, CELL_DEV:] = dot(low, low, NT)
    message[...] = mine[...].astype(message.dtype)


def cell_body(picks, tile, mine, other, factor_mine, factor_other, cell_next, low, *rest):
    sends, (factor, updated, chosen) = rest[:-3], rest[-3:]
    share = factor_mine.shape[0]
    core = lax.axis_index("gene")
    own = pl.ds(pl.multiple_of(core * share, share), share)
    theirs = pl.ds(pl.multiple_of((1 - core) * share, share), share)
    factor[own] = factor_mine[...]
    factor[theirs] = factor_other[...]
    gram = mine[:, CELL_DEV:] + other[:, CELL_DEV:].astype(jnp.float32)
    norm = jnp.sum(jnp.sum(gram * gram, axis=1, keepdims=True), axis=0, keepdims=True)
    rate = 1.0 / (jnp.sqrt(norm) + 1e-06)
    held = factor[...]
    stepped = split_dot(gram, held.astype(jnp.bfloat16))
    data = mine[:, :CELL_DEV] + other[:, :CELL_DEV].astype(jnp.float32)
    updated[...] = jnp.maximum(held - rate * (stepped - data), 0.0)
    cell_next[...] = updated[own]
    low[...] = updated[...].astype(jnp.bfloat16)
    if not sends:
        return
    picked_product(picks, low, tile, chosen, sends)


def picked_product(picks, low, tile, chosen, parts):
    size = chosen.shape[0] // len(picks)
    for n, bits in enumerate(picks):
        chosen[n * size : (n + 1) * size] = low[owned(bits, size)]
    product = dot(chosen[...], tile[...])
    row = 0
    for out in parts:
        out[...] = product[row : row + out.shape[0]].astype(out.dtype)
        row += out.shape[0]


def keep_body(picks, low, tile, gram, *rest):
    picked_product(picks, low, tile, rest[-1], rest[:-1])
    share = low.shape[0] // 2
    own = pl.ds(pl.multiple_of(lax.axis_index("gene") * share, share), share)
    half = dot(low[own], low[...], NT).astype(gram.dtype)
    rows, width = gram.shape[0], half.shape[1]
    for n in range(share // rows):
        gram[:, n * width : (n + 1) * width] = half[n * rows : (n + 1) * rows]


def sum_body(keep, arrived, out):
    out[...] = (keep[...] + arrived[...].astype(jnp.float32)).astype(out.dtype)


def turn_body(keep, own, arrived, third, out, partial):
    size = own.shape[0]
    out[...] = (keep[...] + arrived[:size].astype(jnp.float32)).astype(out.dtype)
    partial[...] = own[...] + arrived[size:].astype(jnp.float32) + third[...].astype(jnp.float32)


def add_body(partial, arrived, out):
    out[...] = partial[...] + arrived[...].astype(jnp.float32)


def last_body(mine, other, panel, factor, partial, last, out, gram):
    rows, width = mine.shape[0], gram.shape[1]
    core = lax.axis_index("gene")
    for half, part in ((core, mine), (1 - core, other)):
        for n in range(part.shape[1] // width):
            row = pl.multiple_of(half * (gram.shape[0] // 2) + n * rows, rows)
            gram[pl.ds(row, rows)] = part[:, n * width : (n + 1) * width]
    whole = gram[...]
    norm = jnp.sum(jnp.sum(whole * whole, axis=1, keepdims=True), axis=0, keepdims=True)
    rate = 1.0 / (jnp.sqrt(norm) + 1e-06)
    stepped = split_dot(gram[owned(0, factor.shape[0])], panel[...])
    data = partial[...] + last[...].astype(jnp.float32)
    out[...] = jnp.maximum(factor[...] - rate * (stepped - data), 0.0)


def gram_of(panel):
    return dot(panel, panel, NT)


def shards(block_values, block_rows, block_cols, block_count, cell_factor, gene_factor):
    n_cell = lax.axis_size("cell")
    kdim = cell_factor.shape[0] * lax.axis_size("gene")
    size = gene_factor.shape[0]
    half = kdim // 2
    gram_rows = half * kdim // GENE_DEV
    paired = n_cell == 8 and size % 16 == 0 and gram_rows % 16 == 0

    def swap(value, bits):
        return lax.ppermute(value, "cell", [(n, n ^ bits) for n in range(n_cell)])

    def swap_core(value):
        return lax.ppermute(value, "gene", [(0, 1), (1, 0)])

    def wide(rows, dtype):
        return shape((rows, GENE_DEV), dtype)

    low_share = gene_factor.astype(jnp.bfloat16)
    values = block_values[0, 0]
    if paired:
        near = [swap(low_share, bits) for bits in (1, 2, 4)]
        beside, second, fourth = lax.optimization_barrier(near)
        sixth = swap(fourth, 2)
        both = call(join_body, wide(2 * size, jnp.bfloat16), 0, 2, 0, 0)(second, fourth)
        both, factor = lax.optimization_barrier((both, cell_factor))
        both_beside, values = lax.optimization_barrier((swap(both, 1), values))
        shares = [low_share, beside, both, both_beside, sixth, swap(sixth, 1)]
        order = [0, 1, 2, 4, 3, 5, 6, 7]
    else:
        shares = [lax.all_gather(low_share, "cell", axis=0, tiled=True)]
        order, factor = None, cell_factor
    factor_other = swap_core(factor)
    tile = dense_tile(values, block_rows[0, 0], block_cols[0, 0], block_count[0])

    shares[0], factor_other = lax.optimization_barrier((shares[0], factor_other))
    panel, mine, message = call(
        functools.partial(gene_body, order),
        (
            wide(kdim, jnp.bfloat16),
            shape((kdim, CELL_DEV + kdim), jnp.float32),
            shape((kdim, CELL_DEV + kdim), jnp.bfloat16),
        ),
        0,
        1 + len(shares),
        0,
        0,
    )(tile, *shares)
    other = swap_core(message)

    sent = [7, 5, 3, 1]
    kept = [6, 4, 2, 0]
    cell_next, next_low, *sends = call(
        functools.partial(cell_body, sent),
        (
            shape(cell_factor.shape, jnp.float32),
            shape((kdim, CELL_DEV), jnp.bfloat16),
            *(
                [
                    wide(size, jnp.bfloat16),
                    wide(size, jnp.bfloat16),
                    wide(2 * size, jnp.bfloat16),
                ]
                if paired
                else []
            ),
        ),
        0,
        5,
        0,
        0,
        [
            pltpu.VMEM((kdim, CELL_DEV), jnp.float32),
            pltpu.VMEM((kdim, CELL_DEV), jnp.float32),
            pltpu.VMEM((half, CELL_DEV), jnp.bfloat16),
        ],
    )(tile, mine, other, cell_factor, factor_other)

    if not paired:
        cell_gram = lax.psum(gram_of(next_low), "cell")
        own_cols = lax.psum_scatter(dot(next_low, tile), "cell", scatter_dimension=0, tiled=True)
        gram_part = lax.dynamic_slice_in_dim(cell_gram, lax.axis_index("cell") * size, size, 0)
        rate_gene = 1.0 / (jnp.sqrt(jnp.sum(cell_gram * cell_gram)) + 1e-06)
        stepped = jnp.dot(
            gram_part, panel.astype(jnp.float32), precision=lax.Precision.HIGHEST
        )
        return (cell_next, jnp.maximum(gene_factor - rate_gene * (stepped - own_cols), 0.0))

    arrived = [swap(part, 1) for part in sends]
    gram, *keeps = call(
        functools.partial(keep_body, kept),
        (wide(gram_rows, jnp.bfloat16), *[wide(size, jnp.float32) for _ in kept]),
        0,
        2,
        0,
        AHEAD,
        [pltpu.VMEM((half, CELL_DEV), jnp.bfloat16)],
    )(next_low, tile)
    gram_arrived = swap(gram, 4)
    third = call(sum_body, wide(size, jnp.bfloat16), 0, 2, 0, AHEAD)(keeps[0], arrived[0])
    second = call(sum_body, wide(size, jnp.bfloat16), 0, 2, 0, AHEAD)(keeps[1], arrived[1])
    gram_arrived, second, third = lax.optimization_barrier((gram_arrived, second, third))
    third = swap(third, 6)
    second = swap(second, 4)
    gram = (gram.astype(jnp.float32) + gram_arrived.astype(jnp.float32)).astype(jnp.bfloat16)
    gram_arrived = swap(gram, 2)
    message, partial = call(
        turn_body, (wide(size, jnp.bfloat16), wide(size, jnp.float32)), 0, 4, 0, 0
    )(keeps[2], keeps[3], arrived[2], third)
    last = swap(message, 2)
    gram_arrived, partial = lax.optimization_barrier((gram_arrived, partial))
    gram = (gram.astype(jnp.float32) + gram_arrived.astype(jnp.float32)).astype(jnp.bfloat16)
    gram_arrived = swap(gram, 1)
    partial = call(add_body, wide(size, jnp.float32), 0, 2, 0, AHEAD)(partial, second)
    gram_arrived, partial = lax.optimization_barrier((gram_arrived, partial))
    gram = gram.astype(jnp.float32) + gram_arrived.astype(jnp.float32)
    gene_next = call(
        last_body,
        wide(size, jnp.float32),
        0,
        6,
        0,
        0,
        [pltpu.VMEM((kdim, kdim), jnp.float32)],
    )(gram, swap_core(gram), panel, gene_factor, partial, last)
    return (cell_next, gene_next)


def solution(mesh):
    return jax.shard_map(
        shards,
        mesh=mesh,
        in_specs=(
            P(("groups", "cell"), "gene", None, None, None),
            P(("groups", "cell"), "gene", None),
            P(("groups", "cell"), "gene", None),
            P(("groups", "cell"), "gene"),
            P(("groups", "gene"), "cell"),
            P(("groups", "cell"), "gene"),
        ),
        out_specs=(P(("groups", "gene"), "cell"), P(("groups", "cell"), "gene")),
        check_vma=False,
    )
```

```python
import functools

import jax
import jax.numpy as jnp
from jax import lax
from jax.experimental import pallas as pl
from jax.experimental.pallas import tpu as pltpu
from jax.sharding import PartitionSpec as P

BLK = 128
CELL_DEV = 1024
GENE_DEV = 2048
VMEM_BYTES = 24 * 2**20
AHEAD = 16 * 2**20

NT = (((1,), (1,)), ((), ()))
NN = (((1,), (0,)), ((), ()))
SMEM_SPEC = pl.BlockSpec(memory_space=pltpu.SMEM)
VMEM_SPEC = pl.BlockSpec(memory_space=pltpu.VMEM)


def dot(a, b, dims=NN):
    return lax.dot_general(a, b, dims, preferred_element_type=jnp.float32)


def split_dot(a, b):
    high = a.astype(jnp.bfloat16)
    low = (a - high.astype(jnp.float32)).astype(jnp.bfloat16)
    rows = a.shape[0]
    both = dot(jnp.concatenate([high, low], axis=0), b)
    return both[:rows] + both[rows:]


def call(body, outs, n_smem, n_vmem, flops, traffic, scratch=()):
    return pl.pallas_call(
        body,
        out_shape=outs,
        in_specs=[SMEM_SPEC] * n_smem + [VMEM_SPEC] * n_vmem,
        out_specs=jax.tree.map(lambda _: VMEM_SPEC, outs),
        scratch_shapes=list(scratch),
        compiler_params=pltpu.CompilerParams(vmem_limit_bytes=VMEM_BYTES),
        cost_estimate=pl.CostEstimate(flops=flops, bytes_accessed=traffic, transcendentals=0),
    )


def shape(dims, dtype):
    return jax.ShapeDtypeStruct(dims, dtype)


def dense_body(rows_in, cols_in, count, values, tile, rows, cols, sems, index_sems):
    copies = [
        pltpu.make_async_copy(rows_in, rows, index_sems.at[0]),
        pltpu.make_async_copy(cols_in, cols, index_sems.at[1]),
    ]
    for copy in copies:
        copy.start()
    tile[...] = jnp.zeros_like(tile)
    for copy in copies:
        copy.wait()

    def block(n):
        row = pl.multiple_of(rows[n] * BLK, BLK)
        col = pl.multiple_of(cols[n] * BLK, BLK)
        place = tile.at[pl.ds(row, BLK), pl.ds(col, BLK)]
        return pltpu.make_async_copy(values.at[n], place, sems.at[n])

    def start(n, carry):
        block(n).start()
        return carry

    def wait(n, carry):
        block(n).wait()
        return carry

    lax.fori_loop(0, count[0], start, 0)
    lax.fori_loop(0, count[0], wait, 0)


def pinned(array):
    return pltpu.with_memory_space_constraint(array, pltpu.HBM)


def dense_tile(values, rows, cols, count):
    anywhere = pl.BlockSpec(memory_space=pltpu.HBM)
    n_blocks = values.shape[0]
    return pl.pallas_call(
        dense_body,
        out_shape=shape((CELL_DEV, GENE_DEV), jnp.bfloat16),
        in_specs=[anywhere, anywhere, SMEM_SPEC, anywhere],
        out_specs=VMEM_SPEC,
        scratch_shapes=[
            pltpu.SMEM((n_blocks,), jnp.int32),
            pltpu.SMEM((n_blocks,), jnp.int32),
            pltpu.SemaphoreType.DMA((n_blocks,)),
            pltpu.SemaphoreType.DMA((2,)),
        ],
        compiler_params=pltpu.CompilerParams(vmem_limit_bytes=VMEM_BYTES),
        cost_estimate=pl.CostEstimate(flops=0, bytes_accessed=AHEAD, transcendentals=0),
    )(pinned(rows), pinned(cols), count, pinned(values))


def owned(bits, size):
    return pl.ds(pl.multiple_of((lax.axis_index("cell") ^ bits) * size, size), size)


def gene_body(order, tile, *refs):
    shares, (panel, mine, message) = refs[:-3], refs[-3:]
    if order is None:
        panel[...] = shares[0][...]
    else:
        size = panel.shape[0] // len(order)
        row = 0
        for part in shares:
            for at in range(0, part.shape[0], size):
                panel[owned(order[row], size)] = part[at : at + size]
                row += 1
    low = panel[...]
    mine[:, :CELL_DEV] = dot(low, tile[...], NT)
    mine[:, CELL_DEV:] = dot(low, low, NT)
    message[...] = mine[...].astype(message.dtype)


def cell_body(picks, tile, mine, other, factor_mine, factor_other, cell_next, low, *rest):
    sends, (factor, updated, chosen) = rest[:-3], rest[-3:]
    share = factor_mine.shape[0]
    core = lax.axis_index("gene")
    own = pl.ds(pl.multiple_of(core * share, share), share)
    theirs = pl.ds(pl.multiple_of((1 - core) * share, share), share)
    factor[own] = factor_mine[...]
    factor[theirs] = factor_other[...]
    gram = mine[:, CELL_DEV:] + other[:, CELL_DEV:].astype(jnp.float32)
    norm = jnp.sum(jnp.sum(gram * gram, axis=1, keepdims=True), axis=0, keepdims=True)
    rate = 1.0 / (jnp.sqrt(norm) + 1e-06)
    held = factor[...]
    stepped = split_dot(gram, held.astype(jnp.bfloat16))
    data = mine[:, :CELL_DEV] + other[:, :CELL_DEV].astype(jnp.float32)
    updated[...] = jnp.maximum(held - rate * (stepped - data), 0.0)
    cell_next[...] = updated[own]
    low[...] = updated[...].astype(jnp.bfloat16)
    if not sends:
        return
    picked_product(picks, low, tile, chosen, sends)


def picked_product(picks, low, tile, chosen, parts):
    size = chosen.shape[0] // len(picks)
    for n, bits in enumerate(picks):
        chosen[n * size : (n + 1) * size] = low[owned(bits, size)]
    product = dot(chosen[...], tile[...])
    row = 0
    for out in parts:
        out[...] = product[row : row + out.shape[0]].astype(out.dtype)
        row += out.shape[0]


def keep_body(picks, low, tile, gram, *rest):
    picked_product(picks, low, tile, rest[-1], rest[:-1])
    share = low.shape[0] // 2
    own = pl.ds(pl.multiple_of(lax.axis_index("gene") * share, share), share)
    half = dot(low[own], low[...], NT).astype(gram.dtype)
    rows, width = gram.shape[0], half.shape[1]
    for n in range(share // rows):
        gram[:, n * width : (n + 1) * width] = half[n * rows : (n + 1) * rows]


def sum_body(keep, arrived, out):
    out[...] = (keep[...] + arrived[: keep.shape[0]].astype(jnp.float32)).astype(out.dtype)


def total_body(own, arrived, third, second, last, out):
    total = own[...] + arrived[own.shape[0] :].astype(jnp.float32)
    for part in (third, second, last):
        total = total + part[...].astype(jnp.float32)
    out[...] = total


def last_body(mine, other, panel, factor, data, out, gram):
    rows, width = mine.shape[0], gram.shape[1]
    core = lax.axis_index("gene")
    for half, part in ((core, mine), (1 - core, other)):
        for n in range(part.shape[1] // width):
            row = pl.multiple_of(half * (gram.shape[0] // 2) + n * rows, rows)
            gram[pl.ds(row, rows)] = part[:, n * width : (n + 1) * width]
    whole = gram[...]
    norm = jnp.sum(jnp.sum(whole * whole, axis=1, keepdims=True), axis=0, keepdims=True)
    rate = 1.0 / (jnp.sqrt(norm) + 1e-06)
    stepped = split_dot(gram[owned(0, factor.shape[0])], panel[...])
    out[...] = jnp.maximum(factor[...] - rate * (stepped - data[...]), 0.0)


def gram_of(panel):
    return dot(panel, panel, NT)


def shards(block_values, block_rows, block_cols, block_count, cell_factor, gene_factor):
    n_cell = lax.axis_size("cell")
    kdim = cell_factor.shape[0] * lax.axis_size("gene")
    size = gene_factor.shape[0]
    half = kdim // 2
    gram_rows = half * kdim // GENE_DEV
    paired = n_cell == 8 and size % 16 == 0 and gram_rows % 16 == 0

    def swap(value, bits):
        return lax.ppermute(value, "cell", [(n, n ^ bits) for n in range(n_cell)])

    def swap_core(value):
        return lax.ppermute(value, "gene", [(0, 1), (1, 0)])

    def wide(rows, dtype):
        return shape((rows, GENE_DEV), dtype)

    low_share = gene_factor.astype(jnp.bfloat16)
    values = block_values[0, 0]
    if paired:
        near = [swap(low_share, bits) for bits in (1, 2, 4)]
        beside, second, fourth, factor = lax.optimization_barrier((*near, cell_factor))
        sixth, third, fifth = swap(fourth, 2), swap(beside, 2), swap(fourth, 1)
        seventh = swap(sixth, 1)
        fifth, values = lax.optimization_barrier((fifth, values))
        shares = [low_share, beside, second, third, fourth, fifth, sixth, seventh]
        order = range(n_cell)
    else:
        shares = [lax.all_gather(low_share, "cell", axis=0, tiled=True)]
        order, factor = None, cell_factor
    factor_other = swap_core(factor)
    tile = dense_tile(values, block_rows[0, 0], block_cols[0, 0], block_count[0])

    shares[0], factor_other = lax.optimization_barrier((shares[0], factor_other))
    panel, mine, message = call(
        functools.partial(gene_body, order),
        (
            wide(kdim, jnp.bfloat16),
            shape((kdim, CELL_DEV + kdim), jnp.float32),
            shape((kdim, CELL_DEV + kdim), jnp.bfloat16),
        ),
        0,
        1 + len(shares),
        0,
        0,
    )(tile, *shares)
    other = swap_core(message)

    sent = [7, 5, 3, 1]
    kept = [6, 4, 2, 0]
    cell_next, next_low, *sends = call(
        functools.partial(cell_body, sent),
        (
            shape(cell_factor.shape, jnp.float32),
            shape((kdim, CELL_DEV), jnp.bfloat16),
            *(
                [
                    wide(size, jnp.bfloat16),
                    wide(size, jnp.bfloat16),
                    wide(2 * size, jnp.bfloat16),
                ]
                if paired
                else []
            ),
        ),
        0,
        5,
        0,
        0,
        [
            pltpu.VMEM((kdim, CELL_DEV), jnp.float32),
            pltpu.VMEM((kdim, CELL_DEV), jnp.float32),
            pltpu.VMEM((half, CELL_DEV), jnp.bfloat16),
        ],
    )(tile, mine, other, cell_factor, factor_other)

    if not paired:
        cell_gram = lax.psum(gram_of(next_low), "cell")
        own_cols = lax.psum_scatter(dot(next_low, tile), "cell", scatter_dimension=0, tiled=True)
        gram_part = lax.dynamic_slice_in_dim(cell_gram, lax.axis_index("cell") * size, size, 0)
        rate_gene = 1.0 / (jnp.sqrt(jnp.sum(cell_gram * cell_gram)) + 1e-06)
        stepped = jnp.dot(
            gram_part, panel.astype(jnp.float32), precision=lax.Precision.HIGHEST
        )
        return (cell_next, jnp.maximum(gene_factor - rate_gene * (stepped - own_cols), 0.0))

    arrived = [swap(part, 1) for part in sends]
    gram, *keeps = call(
        functools.partial(keep_body, kept),
        (wide(gram_rows, jnp.bfloat16), *[wide(size, jnp.float32) for _ in kept]),
        0,
        2,
        0,
        AHEAD,
        [pltpu.VMEM((half, CELL_DEV), jnp.bfloat16)],
    )(next_low, tile)
    gram_arrived = swap(gram, 4)
    third = call(sum_body, wide(size, jnp.bfloat16), 0, 2, 0, AHEAD)(keeps[0], arrived[0])
    second = call(sum_body, wide(size, jnp.bfloat16), 0, 2, 0, AHEAD)(keeps[1], arrived[1])
    gram_arrived, second, third = lax.optimization_barrier((gram_arrived, second, third))
    third = swap(third, 6)
    second = swap(second, 4)
    last = swap(call(sum_body, wide(size, jnp.bfloat16), 0, 2, 0, 0)(keeps[2], arrived[2]), 2)
    gram = (gram.astype(jnp.float32) + gram_arrived.astype(jnp.float32)).astype(jnp.bfloat16)
    gram = (gram.astype(jnp.float32) + swap(gram, 2).astype(jnp.float32)).astype(jnp.bfloat16)
    total = call(total_body, wide(size, jnp.float32), 0, 5, 0, AHEAD)(keeps[3], arrived[2], third, second, last)
    gram_arrived, total = lax.optimization_barrier((swap(gram, 1), total))
    gram = gram.astype(jnp.float32) + gram_arrived.astype(jnp.float32)
    gene_next = call(
        last_body,
        wide(size, jnp.float32),
        0,
        5,
        0,
        0,
        [pltpu.VMEM((kdim, kdim), jnp.float32)],
    )(gram, swap_core(gram), panel, gene_factor, total)
    return (cell_next, gene_next)


def solution(mesh):
    return jax.shard_map(
        shards,
        mesh=mesh,
        in_specs=(
            P(("groups", "cell"), "gene", None, None, None),
            P(("groups", "cell"), "gene", None),
            P(("groups", "cell"), "gene", None),
            P(("groups", "cell"), "gene"),
            P(("groups", "gene"), "cell"),
            P(("groups", "cell"), "gene"),
        ),
        out_specs=(P(("groups", "gene"), "cell"), P(("groups", "cell"), "gene")),
        check_vma=False,
    )
```

```python
import functools

import jax
import jax.numpy as jnp
from jax import lax
from jax.experimental import pallas as pl
from jax.experimental.pallas import tpu as pltpu
from jax.sharding import PartitionSpec as P

BLK = 128
CELL_DEV = 1024
GENE_DEV = 2048
VMEM_BYTES = 24 * 2**20
AHEAD = 16 * 2**20

NT = (((1,), (1,)), ((), ()))
NN = (((1,), (0,)), ((), ()))
SMEM_SPEC = pl.BlockSpec(memory_space=pltpu.SMEM)
VMEM_SPEC = pl.BlockSpec(memory_space=pltpu.VMEM)


def dot(a, b, dims=NN):
    return lax.dot_general(a, b, dims, preferred_element_type=jnp.float32)


def split_dot(a, b):
    high = a.astype(jnp.bfloat16)
    low = (a - high.astype(jnp.float32)).astype(jnp.bfloat16)
    rows = a.shape[0]
    both = dot(jnp.concatenate([high, low], axis=0), b)
    return both[:rows] + both[rows:]


def call(body, outs, n_smem, n_vmem, flops, traffic, scratch=()):
    return pl.pallas_call(
        body,
        out_shape=outs,
        in_specs=[SMEM_SPEC] * n_smem + [VMEM_SPEC] * n_vmem,
        out_specs=jax.tree.map(lambda _: VMEM_SPEC, outs),
        scratch_shapes=list(scratch),
        compiler_params=pltpu.CompilerParams(vmem_limit_bytes=VMEM_BYTES),
        cost_estimate=pl.CostEstimate(flops=flops, bytes_accessed=traffic, transcendentals=0),
    )


def shape(dims, dtype):
    return jax.ShapeDtypeStruct(dims, dtype)


def dense_body(rows_in, cols_in, count, values, tile, rows, cols, sems, index_sems):
    copies = [
        pltpu.make_async_copy(rows_in, rows, index_sems.at[0]),
        pltpu.make_async_copy(cols_in, cols, index_sems.at[1]),
    ]
    for copy in copies:
        copy.start()
    tile[...] = jnp.zeros_like(tile)
    for copy in copies:
        copy.wait()

    def block(n):
        row = pl.multiple_of(rows[n] * BLK, BLK)
        col = pl.multiple_of(cols[n] * BLK, BLK)
        place = tile.at[pl.ds(row, BLK), pl.ds(col, BLK)]
        return pltpu.make_async_copy(values.at[n], place, sems.at[n])

    def start(n, carry):
        block(n).start()
        return carry

    def wait(n, carry):
        block(n).wait()
        return carry

    lax.fori_loop(0, count[0], start, 0)
    lax.fori_loop(0, count[0], wait, 0)


def pinned(array):
    return pltpu.with_memory_space_constraint(array, pltpu.HBM)


def dense_tile(values, rows, cols, count):
    anywhere = pl.BlockSpec(memory_space=pltpu.HBM)
    n_blocks = values.shape[0]
    return pl.pallas_call(
        dense_body,
        out_shape=shape((CELL_DEV, GENE_DEV), jnp.bfloat16),
        in_specs=[anywhere, anywhere, SMEM_SPEC, anywhere],
        out_specs=VMEM_SPEC,
        scratch_shapes=[
            pltpu.SMEM((n_blocks,), jnp.int32),
            pltpu.SMEM((n_blocks,), jnp.int32),
            pltpu.SemaphoreType.DMA((n_blocks,)),
            pltpu.SemaphoreType.DMA((2,)),
        ],
        compiler_params=pltpu.CompilerParams(vmem_limit_bytes=VMEM_BYTES),
        cost_estimate=pl.CostEstimate(flops=0, bytes_accessed=0, transcendentals=0),
    )(pinned(rows), pinned(cols), count, pinned(values))


def owned(bits, size):
    return pl.ds(pl.multiple_of((lax.axis_index("cell") ^ bits) * size, size), size)


STEP = 8
PARTS = 2


def coded(rows):
    above, parts = None, []
    for n in range(0, rows.shape[0], STEP):
        part = rows[n : n + STEP]
        part = (part if above is None else part - above).astype(jnp.bfloat16).astype(jnp.float32)
        above = part if above is None else above + part
        parts.append(part)
    return jnp.concatenate(parts, axis=0).astype(jnp.bfloat16)


def decoded(rows):
    rows, above, parts = rows.astype(jnp.float32), None, []
    for n in range(0, rows.shape[0], STEP):
        above = rows[n : n + STEP] if above is None else above + rows[n : n + STEP]
        parts.append(above)
    return jnp.concatenate(parts, axis=0)


def first_body(count, tile, *refs):
    shares, (panel, mine), messages = refs[: -2 - count], refs[-2 - count : -count], refs[-count:]
    row = 0
    for part in shares:
        panel[row : row + part.shape[0]] = part[...]
        row += part.shape[0]
    mine[...] = dot(panel[...], tile[...], NT)
    row = 0
    for out in messages:
        out[...] = mine[row : row + out.shape[0]].astype(out.dtype)
        row += out.shape[0]


def second_body(order, tile, first, share, panel, mine, message):
    size = share.shape[0]
    if order is None:
        panel[: first.shape[0]] = first[...]
        panel[first.shape[0] :] = share[...]
    else:
        for n, bits in enumerate(order[:-1]):
            panel[owned(bits, size)] = first[n * size : (n + 1) * size]
        panel[owned(order[-1], size)] = share[...]
    mine[:size] = dot(share[...], tile[...], NT)
    low = panel[...]
    gram = dot(low, low, NT)
    rows, width = mine.shape[0] - size, gram.shape[1]
    for n in range(gram.shape[0] // rows):
        mine[size:, n * width : (n + 1) * width] = gram[n * rows : (n + 1) * rows]
    message[...] = mine[...].astype(message.dtype)


def cell_body(
    order, picks, count, tile, mine_first, mine, other, factor_mine, factor_other, *refs
):
    others, (cell_next, low), sends = refs[:count], refs[count : count + 2], refs[count + 2 : -5]
    other_first, factor, data, updated, chosen = refs[-5:]
    for n, part in enumerate(others):
        other_first[n * part.shape[0] : (n + 1) * part.shape[0]] = part[...]
    share = factor_mine.shape[0]
    kdim = factor.shape[0]
    core = lax.axis_index("gene")
    own = pl.ds(pl.multiple_of(core * share, share), share)
    theirs = pl.ds(pl.multiple_of((1 - core) * share, share), share)
    factor[own] = factor_mine[...]
    factor[theirs] = factor_other[...]
    both = mine[...] + other[...].astype(jnp.float32)
    size = kdim - mine_first.shape[0]
    gram = jnp.concatenate([both[size:, n : n + kdim] for n in range(0, CELL_DEV, kdim)], axis=0)
    if order is None:
        data[:-size] = mine_first[...] + other_first[...].astype(jnp.float32)
        data[-size:] = both[:size]
    else:
        for n, bits in enumerate(order[:-1]):
            rows = slice(n * size, (n + 1) * size)
            data[owned(bits, size)] = mine_first[rows] + other_first[rows].astype(jnp.float32)
        data[owned(order[-1], size)] = both[:size]
    norm = jnp.sum(jnp.sum(gram * gram, axis=1, keepdims=True), axis=0, keepdims=True)
    rate = 1.0 / (jnp.sqrt(norm) + 1e-06)
    held = factor[...]
    stepped = split_dot(gram, held.astype(jnp.bfloat16))
    updated[...] = jnp.maximum(held - rate * (stepped - data[...]), 0.0)
    cell_next[...] = updated[own]
    low[...] = updated[...].astype(jnp.bfloat16)
    if sends:
        send, gram_out = sends
        send[...] = coded(picked_product(picks, low, tile, chosen)[0])
        half_gram(low, gram_out)


def half_gram(low, out):
    share = low.shape[0] // 2
    own = pl.ds(pl.multiple_of(lax.axis_index("gene") * share, share), share)
    half = dot(low[own], low[...], NT).astype(out.dtype)
    rows, width = out.shape[0], half.shape[1]
    for n in range(share // rows):
        out[:, n * width : (n + 1) * width] = half[n * rows : (n + 1) * rows]


def picked_product(picks, low, tile, chosen):
    size = chosen.shape[0] // len(picks)
    for n, bits in enumerate(picks):
        chosen[n * size : (n + 1) * size] = low[owned(bits, size)]
    product = dot(chosen[...], tile[...])
    return [product[n * size : (n + 1) * size] for n in range(len(picks))]


def keep_body(picks, low, tile, send, send_pair, *rest):
    first, second, third, *kept = picked_product(picks, low, tile, rest[-1])
    send[...] = coded(first)
    size = first.shape[0]
    send_pair[:size] = coded(second)
    send_pair[size:] = coded(third)
    for out, part in zip(rest[:-1], kept):
        out[...] = part


def pair_body(keep, other, arrived, out, total):
    size = keep.shape[0]
    out[...] = coded(keep[...] + decoded(arrived[:size]))
    total[...] = other[...] + decoded(arrived[size:])


def sum_body(keep, *refs):
    total = keep[...]
    for part in refs[:-1]:
        total = total + decoded(part[...])
    refs[-1][...] = coded(total)


def total_body(keep, *refs):
    total = keep[...]
    for part in refs[:-1]:
        total = total + decoded(part[...])
    refs[-1][...] = total


def last_body(mine, other, panel, factor, data, out, gram):
    rows, width = mine.shape[0], gram.shape[1]
    core = lax.axis_index("gene")
    for half, part in ((core, mine), (1 - core, other)):
        for n in range(part.shape[1] // width):
            row = pl.multiple_of(half * (gram.shape[0] // 2) + n * rows, rows)
            gram[pl.ds(row, rows)] = part[:, n * width : (n + 1) * width]
    whole = gram[...]
    norm = jnp.sum(jnp.sum(whole * whole, axis=1, keepdims=True), axis=0, keepdims=True)
    rate = 1.0 / (jnp.sqrt(norm) + 1e-06)
    stepped = split_dot(gram[owned(0, factor.shape[0])], panel[...])
    out[...] = jnp.maximum(factor[...] - rate * (stepped - data[...]), 0.0)


def gram_of(panel):
    return dot(panel, panel, NT)


def shards(block_values, block_rows, block_cols, block_count, cell_factor, gene_factor):
    n_cell = lax.axis_size("cell")
    kdim = cell_factor.shape[0] * lax.axis_size("gene")
    size = gene_factor.shape[0]
    gram_rows = kdim // 2 * kdim // GENE_DEV
    paired = n_cell == 8 and size % 16 == 0 and gram_rows % 16 == 0

    def swap(value, bits):
        return lax.ppermute(value, "cell", [(n, n ^ bits) for n in range(n_cell)])

    def swap_core(value):
        return lax.ppermute(value, "gene", [(0, 1), (1, 0)])

    def wide(rows, dtype):
        return shape((rows, GENE_DEV), dtype)

    low_share = gene_factor.astype(jnp.bfloat16)
    factor_other = swap_core(cell_factor)
    tile = dense_tile(block_values[0, 0], block_rows[0, 0], block_cols[0, 0], block_count[0])
    if paired:
        near = [swap(low_share, bits) for bits in (1, 2, 4)]
        beside, second, fourth, tile, factor_other = lax.optimization_barrier((*near, tile, factor_other))
        sixth, third, fifth = swap(fourth, 2), swap(beside, 2), swap(fourth, 1)
        seventh = swap(sixth, 1)
        shares = [low_share, beside, second, third, fourth, fifth, sixth]
        order = range(n_cell)
    else:
        whole = lax.all_gather(low_share, "cell", axis=0, tiled=True)
        shares, seventh, order = [whole[: -kdim // 8]], whole[-kdim // 8 :], None
    last_rows = seventh.shape[0]

    first_rows = kdim - last_rows
    part_rows = first_rows // PARTS if first_rows % (16 * PARTS) == 0 else first_rows
    n_parts = first_rows // part_rows
    panel_first, mine_first, *messages = call(
        functools.partial(first_body, n_parts),
        (
            wide(first_rows, jnp.bfloat16),
            shape((first_rows, CELL_DEV), jnp.float32),
            *[shape((part_rows, CELL_DEV), jnp.bfloat16) for _ in range(n_parts)],
        ),
        0,
        1 + len(shares),
        0,
        AHEAD,
    )(tile, *shares)
    others = [swap_core(part) for part in messages]
    rows = last_rows + kdim * kdim // CELL_DEV
    panel, mine, message = call(
        functools.partial(second_body, order),
        (
            wide(kdim, jnp.bfloat16),
            shape((rows, CELL_DEV), jnp.float32),
            shape((rows, CELL_DEV), jnp.bfloat16),
        ),
        0,
        3,
        0,
        0,
    )(tile, panel_first, seventh)
    other = swap_core(message)

    sent = [5, 3, 1]
    kept = [6, 4, 2, 0]
    cell_next, next_low, *sends = call(
        functools.partial(cell_body, order, [7], n_parts),
        (
            shape(cell_factor.shape, jnp.float32),
            shape((kdim, CELL_DEV), jnp.bfloat16),
            *([wide(size, jnp.bfloat16), wide(gram_rows, jnp.bfloat16)] if paired else []),
        ),
        0,
        6 + n_parts,
        0,
        0,
        [
            pltpu.VMEM((first_rows, CELL_DEV), jnp.bfloat16),
            pltpu.VMEM((kdim, CELL_DEV), jnp.float32),
            pltpu.VMEM((kdim, CELL_DEV), jnp.float32),
            pltpu.VMEM((kdim, CELL_DEV), jnp.float32),
            pltpu.VMEM((size, CELL_DEV), jnp.bfloat16),
        ],
    )(tile, mine_first, mine, other, cell_factor, factor_other, *others)

    if not paired:
        cell_gram = lax.psum(gram_of(next_low), "cell")
        own_cols = lax.psum_scatter(dot(next_low, tile), "cell", scatter_dimension=0, tiled=True)
        gram_part = lax.dynamic_slice_in_dim(cell_gram, lax.axis_index("cell") * size, size, 0)
        rate_gene = 1.0 / (jnp.sqrt(jnp.sum(cell_gram * cell_gram)) + 1e-06)
        stepped = jnp.dot(
            gram_part, panel.astype(jnp.float32), precision=lax.Precision.HIGHEST
        )
        return (cell_next, jnp.maximum(gene_factor - rate_gene * (stepped - own_cols), 0.0))

    arrived = [swap(sends[0], 1)]
    send, send_pair, *keeps = call(
        functools.partial(keep_body, sent + kept),
        (
            wide(size, jnp.bfloat16),
            wide(2 * size, jnp.bfloat16),
            *[wide(size, jnp.float32) for _ in kept],
        ),
        0,
        2,
        0,
        AHEAD,
        [pltpu.VMEM((kdim - size, CELL_DEV), jnp.bfloat16)],
    )(next_low, tile)
    gram = sends[1]
    arrived += [swap(send, 1), swap(send_pair, 1)]

    def add_up(cost, keep, *parts):
        body = call(sum_body, wide(size, jnp.bfloat16), 0, 1 + len(parts), 0, cost)
        return body(keep, *parts)

    through = add_up(AHEAD, keeps[0], arrived[0])
    gram_arrived = swap(gram, 4)
    through = swap(through, 2)
    beside, total = call(
        pair_body, (wide(size, jnp.bfloat16), wide(size, jnp.float32)), 0, 3, 0, AHEAD
    )(keeps[2], keeps[3], arrived[2])
    across = add_up(AHEAD, keeps[1], arrived[1], through)

    gram = (gram.astype(jnp.float32) + gram_arrived.astype(jnp.float32)).astype(jnp.bfloat16)
    gram_arrived = swap(gram, 2)
    gram_arrived, across = lax.optimization_barrier((gram_arrived, across))
    across = swap(across, 4)
    beside = swap(beside, 2)
    gram = (gram.astype(jnp.float32) + gram_arrived.astype(jnp.float32)).astype(jnp.bfloat16)

    partner = swap(gram, 1)
    total = call(total_body, wide(size, jnp.float32), 0, 3, 0, AHEAD)(total, beside, across)

    gram = gram.astype(jnp.float32) + partner.astype(jnp.float32)
    gene_next = call(
        last_body,
        wide(size, jnp.float32),
        0,
        5,
        0,
        0,
        [pltpu.VMEM((kdim, kdim), jnp.float32)],
    )(gram, swap_core(gram), panel, gene_factor, total)
    return (cell_next, gene_next)


def solution(mesh):
    return jax.shard_map(
        shards,
        mesh=mesh,
        in_specs=(
            P(("groups", "cell"), "gene", None, None, None),
            P(("groups", "cell"), "gene", None),
            P(("groups", "cell"), "gene", None),
            P(("groups", "cell"), "gene"),
            P(("groups", "gene"), "cell"),
            P(("groups", "cell"), "gene"),
        ),
        out_specs=(P(("groups", "gene"), "cell"), P(("groups", "cell"), "gene")),
        check_vma=False,
    )
```

```python
import functools

import jax
import jax.numpy as jnp
from jax import lax
from jax.experimental import pallas as pl
from jax.experimental.pallas import tpu as pltpu
from jax.sharding import PartitionSpec as P

BLK = 128
CELL_DEV = 1024
GENE_DEV = 2048
VMEM_BYTES = 24 * 2**20
AHEAD = 16 * 2**20

NT = (((1,), (1,)), ((), ()))
NN = (((1,), (0,)), ((), ()))
SMEM_SPEC = pl.BlockSpec(memory_space=pltpu.SMEM)
VMEM_SPEC = pl.BlockSpec(memory_space=pltpu.VMEM)


def dot(a, b, dims=NN):
    return lax.dot_general(a, b, dims, preferred_element_type=jnp.float32)


def split_dot(a, b):
    high = a.astype(jnp.bfloat16)
    low = (a - high.astype(jnp.float32)).astype(jnp.bfloat16)
    rows = a.shape[0]
    both = dot(jnp.concatenate([high, low], axis=0), b)
    return both[:rows] + both[rows:]


def call(body, outs, n_smem, n_vmem, flops, traffic, scratch=()):
    return pl.pallas_call(
        body,
        out_shape=outs,
        in_specs=[SMEM_SPEC] * n_smem + [VMEM_SPEC] * n_vmem,
        out_specs=jax.tree.map(lambda _: VMEM_SPEC, outs),
        scratch_shapes=list(scratch),
        compiler_params=pltpu.CompilerParams(vmem_limit_bytes=VMEM_BYTES),
        cost_estimate=pl.CostEstimate(flops=flops, bytes_accessed=traffic, transcendentals=0),
    )


def shape(dims, dtype):
    return jax.ShapeDtypeStruct(dims, dtype)


def dense_body(rows_in, cols_in, count, values, tile, rows, cols, sems, index_sems):
    copies = [
        pltpu.make_async_copy(rows_in, rows, index_sems.at[0]),
        pltpu.make_async_copy(cols_in, cols, index_sems.at[1]),
    ]
    for copy in copies:
        copy.start()
    tile[...] = jnp.zeros_like(tile)
    for copy in copies:
        copy.wait()

    def block(n):
        row = pl.multiple_of(rows[n] * BLK, BLK)
        col = pl.multiple_of(cols[n] * BLK, BLK)
        place = tile.at[pl.ds(row, BLK), pl.ds(col, BLK)]
        return pltpu.make_async_copy(values.at[n], place, sems.at[n])

    def start(n, carry):
        block(n).start()
        return carry

    def wait(n, carry):
        block(n).wait()
        return carry

    lax.fori_loop(0, count[0], start, 0)
    lax.fori_loop(0, count[0], wait, 0)


def pinned(array):
    return pltpu.with_memory_space_constraint(array, pltpu.HBM)


def dense_tile(values, rows, cols, count):
    anywhere = pl.BlockSpec(memory_space=pltpu.HBM)
    n_blocks = values.shape[0]
    return pl.pallas_call(
        dense_body,
        out_shape=shape((CELL_DEV, GENE_DEV), jnp.bfloat16),
        in_specs=[anywhere, anywhere, SMEM_SPEC, anywhere],
        out_specs=VMEM_SPEC,
        scratch_shapes=[
            pltpu.SMEM((n_blocks,), jnp.int32),
            pltpu.SMEM((n_blocks,), jnp.int32),
            pltpu.SemaphoreType.DMA((n_blocks,)),
            pltpu.SemaphoreType.DMA((2,)),
        ],
        compiler_params=pltpu.CompilerParams(vmem_limit_bytes=VMEM_BYTES),
        cost_estimate=pl.CostEstimate(flops=0, bytes_accessed=0, transcendentals=0),
    )(pinned(rows), pinned(cols), count, pinned(values))


def owned(bits, size):
    return pl.ds(pl.multiple_of((lax.axis_index("cell") ^ bits) * size, size), size)


STEP = 8
PARTS = 2


def coded(rows):
    above, parts = None, []
    for n in range(0, rows.shape[0], STEP):
        part = rows[n : n + STEP]
        part = (part if above is None else part - above).astype(jnp.bfloat16).astype(jnp.float32)
        above = part if above is None else above + part
        parts.append(part)
    return jnp.concatenate(parts, axis=0).astype(jnp.bfloat16)


def decoded(rows):
    rows, above, parts = rows.astype(jnp.float32), None, []
    for n in range(0, rows.shape[0], STEP):
        above = rows[n : n + STEP] if above is None else above + rows[n : n + STEP]
        parts.append(above)
    return jnp.concatenate(parts, axis=0)


def first_body(count, tile, *refs):
    shares, (panel, mine), messages = refs[: -2 - count], refs[-2 - count : -count], refs[-count:]
    row = 0
    for part in shares:
        panel[row : row + part.shape[0]] = part[...]
        row += part.shape[0]
    mine[...] = dot(panel[...], tile[...], NT)
    row = 0
    for out in messages:
        out[...] = mine[row : row + out.shape[0]].astype(out.dtype)
        row += out.shape[0]


def second_body(order, tile, first, share, panel, mine, message):
    size = share.shape[0]
    if order is None:
        panel[: first.shape[0]] = first[...]
        panel[first.shape[0] :] = share[...]
    else:
        for n, bits in enumerate(order[:-1]):
            panel[owned(bits, size)] = first[n * size : (n + 1) * size]
        panel[owned(order[-1], size)] = share[...]
    mine[:size] = dot(share[...], tile[...], NT)
    low = panel[...]
    gram = dot(low, low, NT)
    rows, width = mine.shape[0] - size, gram.shape[1]
    for n in range(gram.shape[0] // rows):
        mine[size:, n * width : (n + 1) * width] = gram[n * rows : (n + 1) * rows]
    message[...] = mine[...].astype(message.dtype)


def cell_body(
    order, picks, count, tile, mine_first, mine, other, factor_mine, factor_other, *refs
):
    others, (cell_next, low), sends = refs[:count], refs[count : count + 2], refs[count + 2 : -5]
    other_first, factor, data, updated, chosen = refs[-5:]
    for n, part in enumerate(others):
        other_first[n * part.shape[0] : (n + 1) * part.shape[0]] = part[...]
    share = factor_mine.shape[0]
    kdim = factor.shape[0]
    core = lax.axis_index("gene")
    own = pl.ds(pl.multiple_of(core * share, share), share)
    theirs = pl.ds(pl.multiple_of((1 - core) * share, share), share)
    factor[own] = factor_mine[...]
    factor[theirs] = factor_other[...]
    both = mine[...] + other[...].astype(jnp.float32)
    size = kdim - mine_first.shape[0]
    gram = jnp.concatenate([both[size:, n : n + kdim] for n in range(0, CELL_DEV, kdim)], axis=0)
    if order is None:
        data[:-size] = mine_first[...] + other_first[...].astype(jnp.float32)
        data[-size:] = both[:size]
    else:
        for n, bits in enumerate(order[:-1]):
            rows = slice(n * size, (n + 1) * size)
            data[owned(bits, size)] = mine_first[rows] + other_first[rows].astype(jnp.float32)
        data[owned(order[-1], size)] = both[:size]
    norm = jnp.sum(jnp.sum(gram * gram, axis=1, keepdims=True), axis=0, keepdims=True)
    rate = 1.0 / (jnp.sqrt(norm) + 1e-06)
    held = factor[...]
    stepped = split_dot(gram, held.astype(jnp.bfloat16))
    updated[...] = jnp.maximum(held - rate * (stepped - data[...]), 0.0)
    cell_next[...] = updated[own]
    low[...] = updated[...].astype(jnp.bfloat16)
    if sends:
        send, gram_out = sends
        send[...] = coded(picked_product(picks, low, tile, chosen)[0])
        gram_blocks(low, gram_out)


def gram_blocks(low, out):
    half = low.shape[0] // 2
    panel = low[...]
    gram = dot(panel, panel, NT)
    out[:half] = gram[:half, :half].astype(out.dtype)
    out[half : 2 * half] = gram[:half, half:].astype(out.dtype)
    out[2 * half :] = gram[half:, half:].astype(out.dtype)


def picked_product(picks, low, tile, chosen):
    size = chosen.shape[0] // len(picks)
    for n, bits in enumerate(picks):
        chosen[n * size : (n + 1) * size] = low[owned(bits, size)]
    product = dot(chosen[...], tile[...])
    return [product[n * size : (n + 1) * size] for n in range(len(picks))]


def keep_body(picks, low, tile, *rest):
    for out, part in zip(rest[:-1], picked_product(picks, low, tile, rest[-1])):
        out[...] = coded(part) if out.dtype == jnp.bfloat16 else part


def sum_body(keep, *refs):
    total = keep[...]
    for part in refs[:-1]:
        total = total + decoded(part[...])
    refs[-1][...] = coded(total)


def total_body(keep, *refs):
    total = keep[...]
    for part in refs[:-1]:
        total = total + decoded(part[...])
    refs[-1][...] = total


def last_body(mine, other, panel, factor, data, out, gram):
    half = mine.shape[0] // 3
    quarters = mine[...].astype(jnp.float32) + other[...].astype(jnp.float32)
    upper, side, lower = quarters[:half], quarters[half : 2 * half], quarters[2 * half :]
    gram[:half, :half] = upper
    gram[:half, half:] = side
    gram[half:, :half] = side.T
    gram[half:, half:] = lower
    squares = upper * upper + 2.0 * (side * side) + lower * lower
    norm = jnp.sum(jnp.sum(squares, axis=1, keepdims=True), axis=0, keepdims=True)
    rate = 1.0 / (jnp.sqrt(norm) + 1e-06)
    stepped = split_dot(gram[owned(0, factor.shape[0])], panel[...])
    out[...] = jnp.maximum(factor[...] - rate * (stepped - data[...]), 0.0)


def gram_of(panel):
    return dot(panel, panel, NT)


def shards(block_values, block_rows, block_cols, block_count, cell_factor, gene_factor):
    n_cell = lax.axis_size("cell")
    kdim = cell_factor.shape[0] * lax.axis_size("gene")
    size = gene_factor.shape[0]
    paired = n_cell == 8 and size % 16 == 0 and kdim % (2 * BLK) == 0

    def swap(value, bits):
        return lax.ppermute(value, "cell", [(n, n ^ bits) for n in range(n_cell)])

    def swap_core(value):
        return lax.ppermute(value, "gene", [(0, 1), (1, 0)])

    def wide(rows, dtype):
        return shape((rows, GENE_DEV), dtype)

    low_share = gene_factor.astype(jnp.bfloat16)
    factor_other = swap_core(cell_factor)
    tile = dense_tile(block_values[0, 0], block_rows[0, 0], block_cols[0, 0], block_count[0])
    if paired:
        near = [swap(low_share, bits) for bits in (1, 2, 4)]
        beside, second, fourth, tile, factor_other = lax.optimization_barrier((*near, tile, factor_other))
        sixth, third, fifth = swap(fourth, 2), swap(beside, 2), swap(fourth, 1)
        seventh = swap(sixth, 1)
        shares = [low_share, beside, second, third, fourth, fifth, sixth]
        order = range(n_cell)
    else:
        whole = lax.all_gather(low_share, "cell", axis=0, tiled=True)
        shares, seventh, order = [whole[: -kdim // 8]], whole[-kdim // 8 :], None
    last_rows = seventh.shape[0]

    first_rows = kdim - last_rows
    part_rows = first_rows // PARTS if first_rows % (16 * PARTS) == 0 else first_rows
    n_parts = first_rows // part_rows
    panel_first, mine_first, *messages = call(
        functools.partial(first_body, n_parts),
        (
            wide(first_rows, jnp.bfloat16),
            shape((first_rows, CELL_DEV), jnp.float32),
            *[shape((part_rows, CELL_DEV), jnp.bfloat16) for _ in range(n_parts)],
        ),
        0,
        1 + len(shares),
        0,
        AHEAD,
    )(tile, *shares)
    others = [swap_core(part) for part in messages]
    rows = last_rows + kdim * kdim // CELL_DEV
    panel, mine, message = call(
        functools.partial(second_body, order),
        (
            wide(kdim, jnp.bfloat16),
            shape((rows, CELL_DEV), jnp.float32),
            shape((rows, CELL_DEV), jnp.bfloat16),
        ),
        0,
        3,
        0,
        0,
    )(tile, panel_first, seventh)
    other = swap_core(message)

    sent = [5, 3, 1]
    kept = [6, 4, 2, 0]
    cell_next, next_low, *sends = call(
        functools.partial(cell_body, order, [7], n_parts),
        (
            shape(cell_factor.shape, jnp.float32),
            shape((kdim, CELL_DEV), jnp.bfloat16),
            *([wide(size, jnp.bfloat16), shape((3 * kdim // 2, kdim // 2), jnp.bfloat16)] if paired else []),
        ),
        0,
        6 + n_parts,
        0,
        0,
        [
            pltpu.VMEM((first_rows, CELL_DEV), jnp.bfloat16),
            pltpu.VMEM((kdim, CELL_DEV), jnp.float32),
            pltpu.VMEM((kdim, CELL_DEV), jnp.float32),
            pltpu.VMEM((kdim, CELL_DEV), jnp.float32),
            pltpu.VMEM((size, CELL_DEV), jnp.bfloat16),
        ],
    )(tile, mine_first, mine, other, cell_factor, factor_other, *others)

    if not paired:
        cell_gram = lax.psum(gram_of(next_low), "cell")
        own_cols = lax.psum_scatter(dot(next_low, tile), "cell", scatter_dimension=0, tiled=True)
        gram_part = lax.dynamic_slice_in_dim(cell_gram, lax.axis_index("cell") * size, size, 0)
        rate_gene = 1.0 / (jnp.sqrt(jnp.sum(cell_gram * cell_gram)) + 1e-06)
        stepped = jnp.dot(
            gram_part, panel.astype(jnp.float32), precision=lax.Precision.HIGHEST
        )
        return (cell_next, jnp.maximum(gene_factor - rate_gene * (stepped - own_cols), 0.0))

    arrived = [swap(sends[0], 1)]
    *parts, keep_third, keep_second, keep_near, own = call(
        functools.partial(keep_body, sent + kept),
        (
            *[wide(size, jnp.bfloat16) for _ in sent],
            *[wide(size, jnp.float32) for _ in kept],
        ),
        0,
        2,
        0,
        AHEAD,
        [pltpu.VMEM((kdim - size, CELL_DEV), jnp.bfloat16)],
    )(next_low, tile)
    gram = sends[1]
    arrived += [swap(part, 1) for part in parts]

    def add_up(cost, keep, *parts):
        body = call(sum_body, wide(size, jnp.bfloat16), 0, 1 + len(parts), 0, cost)
        return body(keep, *parts)

    through = swap(add_up(AHEAD, keep_third, arrived[0]), 2)
    gram_arrived = swap(gram, 4)
    beside = swap(add_up(AHEAD, keep_near, arrived[2]), 2)
    across = add_up(AHEAD, keep_second, arrived[1], through)
    gram = (gram.astype(jnp.float32) + gram_arrived.astype(jnp.float32)).astype(jnp.bfloat16)
    gram_arrived = swap(gram, 2)
    across = swap(across, 4)
    gram = (gram.astype(jnp.float32) + gram_arrived.astype(jnp.float32)).astype(jnp.bfloat16)
    partner = swap(gram, 1)
    total = call(total_body, wide(size, jnp.float32), 0, 4, 0, AHEAD)(own, arrived[3], beside, across)
    partner, total = lax.optimization_barrier((partner, total))
    gene_next = call(
        last_body,
        wide(size, jnp.float32),
        0,
        5,
        0,
        0,
        [pltpu.VMEM((kdim, kdim), jnp.float32)],
    )(gram, partner, panel, gene_factor, total)
    return (cell_next, gene_next)


def solution(mesh):
    return jax.shard_map(
        shards,
        mesh=mesh,
        in_specs=(
            P(("groups", "cell"), "gene", None, None, None),
            P(("groups", "cell"), "gene", None),
            P(("groups", "cell"), "gene", None),
            P(("groups", "cell"), "gene"),
            P(("groups", "gene"), "cell"),
            P(("groups", "cell"), "gene"),
        ),
        out_specs=(P(("groups", "gene"), "cell"), P(("groups", "cell"), "gene")),
        check_vma=False,
    )
```

```python
import functools

import jax
import jax.numpy as jnp
from jax import lax
from jax.experimental import pallas as pl
from jax.experimental.pallas import tpu as pltpu
from jax.sharding import PartitionSpec as P

BLK = 128
CELL_DEV = 1024
GENE_DEV = 2048
VMEM_BYTES = 24 * 2**20
AHEAD = 16 * 2**20

NT = (((1,), (1,)), ((), ()))
NN = (((1,), (0,)), ((), ()))
SMEM_SPEC = pl.BlockSpec(memory_space=pltpu.SMEM)
VMEM_SPEC = pl.BlockSpec(memory_space=pltpu.VMEM)


def dot(a, b, dims=NN):
    return lax.dot_general(a, b, dims, preferred_element_type=jnp.float32)


def split_dot(a, b):
    high = a.astype(jnp.bfloat16)
    low = (a - high.astype(jnp.float32)).astype(jnp.bfloat16)
    rows = a.shape[0]
    both = dot(jnp.concatenate([high, low], axis=0), b)
    return both[:rows] + both[rows:]


def call(body, outs, n_smem, n_vmem, flops, traffic, scratch=()):
    return pl.pallas_call(
        body,
        out_shape=outs,
        in_specs=[SMEM_SPEC] * n_smem + [VMEM_SPEC] * n_vmem,
        out_specs=jax.tree.map(lambda _: VMEM_SPEC, outs),
        scratch_shapes=list(scratch),
        compiler_params=pltpu.CompilerParams(vmem_limit_bytes=VMEM_BYTES),
        cost_estimate=pl.CostEstimate(flops=flops, bytes_accessed=traffic, transcendentals=0),
    )


def shape(dims, dtype):
    return jax.ShapeDtypeStruct(dims, dtype)


def dense_body(rows_in, cols_in, count, values, tile, turned, rows, cols, sems, index_sems):
    copies = [
        pltpu.make_async_copy(rows_in, rows, index_sems.at[0]),
        pltpu.make_async_copy(cols_in, cols, index_sems.at[1]),
    ]
    for copy in copies:
        copy.start()
    tile[...] = jnp.zeros_like(tile)
    for copy in copies:
        copy.wait()

    def block(n):
        row = pl.multiple_of(rows[n] * BLK, BLK)
        col = pl.multiple_of(cols[n] * BLK, BLK)
        place = tile.at[pl.ds(row, BLK), pl.ds(col, BLK)]
        return pltpu.make_async_copy(values.at[n], place, sems.at[n])

    def start(n, carry):
        block(n).start()
        return carry

    def wait(n, carry):
        block(n).wait()
        return carry

    lax.fori_loop(0, count[0], start, 0)
    lax.fori_loop(0, count[0], wait, 0)
    for row in range(0, tile.shape[0], TURN):
        turned[:, row : row + TURN] = tile[row : row + TURN].T


def pinned(array):
    return pltpu.with_memory_space_constraint(array, pltpu.HBM)


def dense_tile(values, rows, cols, count):
    anywhere = pl.BlockSpec(memory_space=pltpu.HBM)
    n_blocks = values.shape[0]
    return pl.pallas_call(
        dense_body,
        out_shape=(shape((CELL_DEV, GENE_DEV), jnp.bfloat16), shape((GENE_DEV, CELL_DEV), jnp.bfloat16)),
        in_specs=[anywhere, anywhere, SMEM_SPEC, anywhere],
        out_specs=(VMEM_SPEC, VMEM_SPEC),
        scratch_shapes=[
            pltpu.SMEM((n_blocks,), jnp.int32),
            pltpu.SMEM((n_blocks,), jnp.int32),
            pltpu.SemaphoreType.DMA((n_blocks,)),
            pltpu.SemaphoreType.DMA((2,)),
        ],
        compiler_params=pltpu.CompilerParams(vmem_limit_bytes=VMEM_BYTES),
        cost_estimate=pl.CostEstimate(flops=0, bytes_accessed=0, transcendentals=0),
    )(pinned(rows), pinned(cols), count, pinned(values))


def owned(bits, size):
    return pl.ds(pl.multiple_of((lax.axis_index("cell") ^ bits) * size, size), size)


STEP = 8
TURN = 256
PARTS = 2


def coded(rows):
    above, parts = None, []
    for n in range(0, rows.shape[0], STEP):
        part = rows[n : n + STEP]
        part = (part if above is None else part - above).astype(jnp.bfloat16).astype(jnp.float32)
        above = part if above is None else above + part
        parts.append(part)
    return jnp.concatenate(parts, axis=0).astype(jnp.bfloat16)


def decoded(rows):
    rows, above, parts = rows.astype(jnp.float32), None, []
    for n in range(0, rows.shape[0], STEP):
        above = rows[n : n + STEP] if above is None else above + rows[n : n + STEP]
        parts.append(above)
    return jnp.concatenate(parts, axis=0)


def first_body(count, turned, *refs):
    shares, (panel, mine), messages = refs[: -2 - count], refs[-2 - count : -count], refs[-count:]
    row = 0
    for part in shares:
        panel[row : row + part.shape[0]] = part[...]
        row += part.shape[0]
    mine[...] = dot(panel[...], turned[...])
    row = 0
    for out in messages:
        out[...] = mine[row : row + out.shape[0]].astype(out.dtype)
        row += out.shape[0]


def second_body(order, turned, first, share, panel, mine, message):
    size = share.shape[0]
    if order is None:
        panel[: first.shape[0]] = first[...]
        panel[first.shape[0] :] = share[...]
    else:
        for n, bits in enumerate(order[:-1]):
            panel[owned(bits, size)] = first[n * size : (n + 1) * size]
        panel[owned(order[-1], size)] = share[...]
    mine[:size] = dot(share[...], turned[...])
    low = panel[...]
    gram = dot(low, low, NT)
    rows, width = mine.shape[0] - size, gram.shape[1]
    for n in range(gram.shape[0] // rows):
        mine[size:, n * width : (n + 1) * width] = gram[n * rows : (n + 1) * rows]
    message[...] = mine[...].astype(message.dtype)


def cell_body(
    order, picks, count, tile, mine_first, mine, other, factor_mine, factor_other, *refs
):
    others, (cell_next, low), sends = refs[:count], refs[count : count + 2], refs[count + 2 : -5]
    other_first, factor, data, updated, chosen = refs[-5:]
    for n, part in enumerate(others):
        other_first[n * part.shape[0] : (n + 1) * part.shape[0]] = part[...]
    share = factor_mine.shape[0]
    kdim = factor.shape[0]
    core = lax.axis_index("gene")
    own = pl.ds(pl.multiple_of(core * share, share), share)
    theirs = pl.ds(pl.multiple_of((1 - core) * share, share), share)
    factor[own] = factor_mine[...]
    factor[theirs] = factor_other[...]
    both = mine[...] + other[...].astype(jnp.float32)
    size = kdim - mine_first.shape[0]
    gram = jnp.concatenate([both[size:, n : n + kdim] for n in range(0, CELL_DEV, kdim)], axis=0)
    if order is None:
        data[:-size] = mine_first[...] + other_first[...].astype(jnp.float32)
        data[-size:] = both[:size]
    else:
        for n, bits in enumerate(order[:-1]):
            rows = slice(n * size, (n + 1) * size)
            data[owned(bits, size)] = mine_first[rows] + other_first[rows].astype(jnp.float32)
        data[owned(order[-1], size)] = both[:size]
    norm = jnp.sum(jnp.sum(gram * gram, axis=1, keepdims=True), axis=0, keepdims=True)
    rate = 1.0 / (jnp.sqrt(norm) + 1e-06)
    held = factor[...]
    stepped = split_dot(gram, held.astype(jnp.bfloat16))
    updated[...] = jnp.maximum(held - rate * (stepped - data[...]), 0.0)
    cell_next[...] = updated[own]
    low[...] = updated[...].astype(jnp.bfloat16)
    if sends:
        send, gram_out = sends
        send[...] = coded(picked_product(picks, low, tile, chosen)[0])
        gram_blocks(low, gram_out)


def gram_blocks(low, out):
    half = low.shape[0] // 2
    panel = low[...]
    gram = dot(panel, panel, NT)
    out[:half] = gram[:half, :half].astype(out.dtype)
    out[half : 2 * half] = gram[:half, half:].astype(out.dtype)
    out[2 * half :] = gram[half:, half:].astype(out.dtype)


def picked_product(picks, low, tile, chosen):
    size = chosen.shape[0] // len(picks)
    for n, bits in enumerate(picks):
        chosen[n * size : (n + 1) * size] = low[owned(bits, size)]
    product = dot(chosen[...], tile[...])
    return [product[n * size : (n + 1) * size] for n in range(len(picks))]


def keep_body(picks, low, tile, *rest):
    for out, part in zip(rest[:-1], picked_product(picks, low, tile, rest[-1])):
        out[...] = coded(part) if out.dtype == jnp.bfloat16 else part


def sum_body(keep, *refs):
    total = keep[...]
    for part in refs[:-1]:
        total = total + decoded(part[...])
    refs[-1][...] = coded(total)


def total_body(keep, *refs):
    total = keep[...]
    for part in refs[:-1]:
        total = total + decoded(part[...])
    refs[-1][...] = total


def last_body(mine, other, panel, factor, data, out, gram):
    half = mine.shape[0] // 3
    quarters = mine[...].astype(jnp.float32) + other[...].astype(jnp.float32)
    upper, side, lower = quarters[:half], quarters[half : 2 * half], quarters[2 * half :]
    gram[:half, :half] = upper
    gram[:half, half:] = side
    gram[half:, :half] = side.T
    gram[half:, half:] = lower
    squares = upper * upper + 2.0 * (side * side) + lower * lower
    norm = jnp.sum(jnp.sum(squares, axis=1, keepdims=True), axis=0, keepdims=True)
    rate = 1.0 / (jnp.sqrt(norm) + 1e-06)
    stepped = split_dot(gram[owned(0, factor.shape[0])], panel[...])
    out[...] = jnp.maximum(factor[...] - rate * (stepped - data[...]), 0.0)


def gram_of(panel):
    return dot(panel, panel, NT)


def shards(block_values, block_rows, block_cols, block_count, cell_factor, gene_factor):
    n_cell = lax.axis_size("cell")
    kdim = cell_factor.shape[0] * lax.axis_size("gene")
    size = gene_factor.shape[0]
    paired = n_cell == 8 and size % 16 == 0 and kdim % (2 * BLK) == 0

    def swap(value, bits):
        return lax.ppermute(value, "cell", [(n, n ^ bits) for n in range(n_cell)])

    def swap_core(value):
        return lax.ppermute(value, "gene", [(0, 1), (1, 0)])

    def wide(rows, dtype):
        return shape((rows, GENE_DEV), dtype)

    low_share = gene_factor.astype(jnp.bfloat16)
    factor_other = swap_core(cell_factor)
    tile, turned = dense_tile(block_values[0, 0], block_rows[0, 0], block_cols[0, 0], block_count[0])
    if paired:
        near = [swap(low_share, bits) for bits in (1, 2, 4)]
        beside, second, fourth, tile, turned, factor_other = lax.optimization_barrier(
            (*near, tile, turned, factor_other)
        )
        sixth, third, fifth = swap(fourth, 2), swap(beside, 2), swap(fourth, 1)
        seventh = swap(sixth, 1)
        shares = [low_share, beside, second, third, fourth, fifth, sixth]
        order = range(n_cell)
    else:
        whole = lax.all_gather(low_share, "cell", axis=0, tiled=True)
        shares, seventh, order = [whole[: -kdim // 8]], whole[-kdim // 8 :], None
    last_rows = seventh.shape[0]

    first_rows = kdim - last_rows
    part_rows = first_rows // PARTS if first_rows % (16 * PARTS) == 0 else first_rows
    n_parts = first_rows // part_rows
    panel_first, mine_first, *messages = call(
        functools.partial(first_body, n_parts),
        (
            wide(first_rows, jnp.bfloat16),
            shape((first_rows, CELL_DEV), jnp.float32),
            *[shape((part_rows, CELL_DEV), jnp.bfloat16) for _ in range(n_parts)],
        ),
        0,
        1 + len(shares),
        0,
        AHEAD,
    )(turned, *shares)
    others = [swap_core(part) for part in messages]
    rows = last_rows + kdim * kdim // CELL_DEV
    panel, mine, message = call(
        functools.partial(second_body, order),
        (
            wide(kdim, jnp.bfloat16),
            shape((rows, CELL_DEV), jnp.float32),
            shape((rows, CELL_DEV), jnp.bfloat16),
        ),
        0,
        3,
        0,
        0,
    )(turned, panel_first, seventh)
    other = swap_core(message)

    sent = [5, 3, 1]
    kept = [6, 4, 2, 0]
    cell_next, next_low, *sends = call(
        functools.partial(cell_body, order, [7], n_parts),
        (
            shape(cell_factor.shape, jnp.float32),
            shape((kdim, CELL_DEV), jnp.bfloat16),
            *([wide(size, jnp.bfloat16), shape((3 * kdim // 2, kdim // 2), jnp.bfloat16)] if paired else []),
        ),
        0,
        6 + n_parts,
        0,
        0,
        [
            pltpu.VMEM((first_rows, CELL_DEV), jnp.bfloat16),
            pltpu.VMEM((kdim, CELL_DEV), jnp.float32),
            pltpu.VMEM((kdim, CELL_DEV), jnp.float32),
            pltpu.VMEM((kdim, CELL_DEV), jnp.float32),
            pltpu.VMEM((size, CELL_DEV), jnp.bfloat16),
        ],
    )(tile, mine_first, mine, other, cell_factor, factor_other, *others)

    if not paired:
        cell_gram = lax.psum(gram_of(next_low), "cell")
        own_cols = lax.psum_scatter(dot(next_low, tile), "cell", scatter_dimension=0, tiled=True)
        gram_part = lax.dynamic_slice_in_dim(cell_gram, lax.axis_index("cell") * size, size, 0)
        rate_gene = 1.0 / (jnp.sqrt(jnp.sum(cell_gram * cell_gram)) + 1e-06)
        stepped = jnp.dot(
            gram_part, panel.astype(jnp.float32), precision=lax.Precision.HIGHEST
        )
        return (cell_next, jnp.maximum(gene_factor - rate_gene * (stepped - own_cols), 0.0))

    arrived = [swap(sends[0], 1)]
    *parts, keep_third, keep_second, keep_near, own = call(
        functools.partial(keep_body, sent + kept),
        (
            *[wide(size, jnp.bfloat16) for _ in sent],
            *[wide(size, jnp.float32) for _ in kept],
        ),
        0,
        2,
        0,
        AHEAD,
        [pltpu.VMEM((kdim - size, CELL_DEV), jnp.bfloat16)],
    )(next_low, tile)
    gram = sends[1]
    arrived += [swap(part, 1) for part in parts]

    def add_up(cost, keep, *parts):
        body = call(sum_body, wide(size, jnp.bfloat16), 0, 1 + len(parts), 0, cost)
        return body(keep, *parts)

    through = swap(add_up(AHEAD, keep_third, arrived[0]), 2)
    gram_arrived = swap(gram, 4)
    beside = swap(add_up(AHEAD, keep_near, arrived[2]), 2)
    across = add_up(AHEAD, keep_second, arrived[1], through)
    gram = (gram.astype(jnp.float32) + gram_arrived.astype(jnp.float32)).astype(jnp.bfloat16)
    gram_arrived = swap(gram, 2)
    across = swap(across, 4)
    gram = (gram.astype(jnp.float32) + gram_arrived.astype(jnp.float32)).astype(jnp.bfloat16)
    partner = swap(gram, 1)
    total = call(total_body, wide(size, jnp.float32), 0, 4, 0, AHEAD)(own, arrived[3], beside, across)
    partner, total = lax.optimization_barrier((partner, total))
    gene_next = call(
        last_body,
        wide(size, jnp.float32),
        0,
        5,
        0,
        0,
        [pltpu.VMEM((kdim, kdim), jnp.float32)],
    )(gram, partner, panel, gene_factor, total)
    return (cell_next, gene_next)


def solution(mesh):
    return jax.shard_map(
        shards,
        mesh=mesh,
        in_specs=(
            P(("groups", "cell"), "gene", None, None, None),
            P(("groups", "cell"), "gene", None),
            P(("groups", "cell"), "gene", None),
            P(("groups", "cell"), "gene"),
            P(("groups", "gene"), "cell"),
            P(("groups", "cell"), "gene"),
        ),
        out_specs=(P(("groups", "gene"), "cell"), P(("groups", "cell"), "gene")),
        check_vma=False,
    )
```

```python
import functools

import jax
import jax.numpy as jnp
from jax import lax
from jax.experimental import pallas as pl
from jax.experimental.pallas import tpu as pltpu
from jax.sharding import PartitionSpec as P

BLK = 128
CELL_DEV = 1024
GENE_DEV = 2048
VMEM_BYTES = 24 * 2**20
AHEAD = 16 * 2**20

NT = (((1,), (1,)), ((), ()))
NN = (((1,), (0,)), ((), ()))
SMEM_SPEC = pl.BlockSpec(memory_space=pltpu.SMEM)
VMEM_SPEC = pl.BlockSpec(memory_space=pltpu.VMEM)


def dot(a, b, dims=NN):
    return lax.dot_general(a, b, dims, preferred_element_type=jnp.float32)


def split_dot(a, b):
    high = a.astype(jnp.bfloat16)
    low = (a - high.astype(jnp.float32)).astype(jnp.bfloat16)
    rows = a.shape[0]
    both = dot(jnp.concatenate([high, low], axis=0), b)
    return both[:rows] + both[rows:]


def call(body, outs, n_smem, n_vmem, flops, traffic, scratch=()):
    return pl.pallas_call(
        body,
        out_shape=outs,
        in_specs=[SMEM_SPEC] * n_smem + [VMEM_SPEC] * n_vmem,
        out_specs=jax.tree.map(lambda _: VMEM_SPEC, outs),
        scratch_shapes=list(scratch),
        compiler_params=pltpu.CompilerParams(vmem_limit_bytes=VMEM_BYTES),
        cost_estimate=pl.CostEstimate(flops=flops, bytes_accessed=traffic, transcendentals=0),
    )


def shape(dims, dtype):
    return jax.ShapeDtypeStruct(dims, dtype)


def dense_body(rows_in, cols_in, count, values, tile, turned, rows, cols, sems, index_sems):
    copies = [
        pltpu.make_async_copy(rows_in, rows, index_sems.at[0]),
        pltpu.make_async_copy(cols_in, cols, index_sems.at[1]),
    ]
    for copy in copies:
        copy.start()
    tile[...] = jnp.zeros_like(tile)
    for copy in copies:
        copy.wait()

    def block(n):
        row = pl.multiple_of(rows[n] * BLK, BLK)
        col = pl.multiple_of(cols[n] * BLK, BLK)
        place = tile.at[pl.ds(row, BLK), pl.ds(col, BLK)]
        return pltpu.make_async_copy(values.at[n], place, sems.at[n])

    def start(n, carry):
        block(n).start()
        return carry

    def wait(n, carry):
        block(n).wait()
        return carry

    lax.fori_loop(0, count[0], start, 0)
    lax.fori_loop(0, count[0], wait, 0)
    for row in range(0, tile.shape[0], TURN):
        turned[:, row : row + TURN] = tile[row : row + TURN].T


def pinned(array):
    return pltpu.with_memory_space_constraint(array, pltpu.HBM)


def dense_tile(values, rows, cols, count):
    anywhere = pl.BlockSpec(memory_space=pltpu.HBM)
    n_blocks = values.shape[0]
    return pl.pallas_call(
        dense_body,
        out_shape=(shape((CELL_DEV, GENE_DEV), jnp.bfloat16), shape((GENE_DEV, CELL_DEV), jnp.bfloat16)),
        in_specs=[anywhere, anywhere, SMEM_SPEC, anywhere],
        out_specs=(VMEM_SPEC, VMEM_SPEC),
        scratch_shapes=[
            pltpu.SMEM((n_blocks,), jnp.int32),
            pltpu.SMEM((n_blocks,), jnp.int32),
            pltpu.SemaphoreType.DMA((n_blocks,)),
            pltpu.SemaphoreType.DMA((2,)),
        ],
        compiler_params=pltpu.CompilerParams(vmem_limit_bytes=VMEM_BYTES),
        cost_estimate=pl.CostEstimate(flops=0, bytes_accessed=0, transcendentals=0),
    )(pinned(rows), pinned(cols), count, pinned(values))


def owned(bits, size):
    return pl.ds(pl.multiple_of((lax.axis_index("cell") ^ bits) * size, size), size)


STEP = 8
TURN = 256
PARTS = 2


def coded(rows):
    above, parts = None, []
    for n in range(0, rows.shape[0], STEP):
        part = rows[n : n + STEP]
        part = (part if above is None else part - above).astype(jnp.bfloat16).astype(jnp.float32)
        above = part if above is None else above + part
        parts.append(part)
    return jnp.concatenate(parts, axis=0).astype(jnp.bfloat16)


def decoded(rows):
    rows, above, parts = rows.astype(jnp.float32), None, []
    for n in range(0, rows.shape[0], STEP):
        above = rows[n : n + STEP] if above is None else above + rows[n : n + STEP]
        parts.append(above)
    return jnp.concatenate(parts, axis=0)


def first_body(count, turned, *refs):
    shares, (panel, mine), messages = refs[: -2 - count], refs[-2 - count : -count], refs[-count:]
    row = 0
    for part in shares:
        panel[row : row + part.shape[0]] = part[...]
        row += part.shape[0]
    mine[...] = dot(panel[...], turned[...])
    row = 0
    for out in messages:
        out[...] = mine[row : row + out.shape[0]].astype(out.dtype)
        row += out.shape[0]


def second_body(order, turned, first, share, panel, mine, message):
    size = share.shape[0]
    if order is None:
        panel[: first.shape[0]] = first[...]
        panel[first.shape[0] :] = share[...]
    else:
        for n, bits in enumerate(order[:-1]):
            panel[owned(bits, size)] = first[n * size : (n + 1) * size]
        panel[owned(order[-1], size)] = share[...]
    mine[:size] = dot(share[...], turned[...])
    low = panel[...]
    gram = dot(low, low, NT)
    rows, width = mine.shape[0] - size, gram.shape[1]
    for n in range(gram.shape[0] // rows):
        mine[size:, n * width : (n + 1) * width] = gram[n * rows : (n + 1) * rows]
    message[...] = mine[...].astype(message.dtype)


def cell_body(
    order, picks, count, tile, mine_first, mine, other, factor_mine, factor_other, *refs
):
    others, (cell_next, low), sends = refs[:count], refs[count : count + 2], refs[count + 2 : -5]
    other_first, factor, data, updated, chosen = refs[-5:]
    for n, part in enumerate(others):
        other_first[n * part.shape[0] : (n + 1) * part.shape[0]] = part[...]
    share = factor_mine.shape[0]
    kdim = factor.shape[0]
    core = lax.axis_index("gene")
    own = pl.ds(pl.multiple_of(core * share, share), share)
    theirs = pl.ds(pl.multiple_of((1 - core) * share, share), share)
    factor[own] = factor_mine[...]
    factor[theirs] = factor_other[...]
    both = mine[...] + other[...].astype(jnp.float32)
    size = kdim - mine_first.shape[0]
    gram = jnp.concatenate([both[size:, n : n + kdim] for n in range(0, CELL_DEV, kdim)], axis=0)
    if order is None:
        data[:-size] = mine_first[...] + other_first[...].astype(jnp.float32)
        data[-size:] = both[:size]
    else:
        for n, bits in enumerate(order[:-1]):
            rows = slice(n * size, (n + 1) * size)
            data[owned(bits, size)] = mine_first[rows] + other_first[rows].astype(jnp.float32)
        data[owned(order[-1], size)] = both[:size]
    norm = jnp.sum(jnp.sum(gram * gram, axis=1, keepdims=True), axis=0, keepdims=True)
    rate = 1.0 / (jnp.sqrt(norm) + 1e-06)
    held = factor[...]
    stepped = split_dot(gram, held.astype(jnp.bfloat16))
    updated[...] = jnp.maximum(held - rate * (stepped - data[...]), 0.0)
    cell_next[...] = updated[own]
    low[...] = updated[...].astype(jnp.bfloat16)
    if sends:
        send, gram_out = sends
        send[...] = coded(picked_product(picks, low, tile, chosen)[0])
        gram_blocks(low, gram_out)


def gram_blocks(low, out):
    half = low.shape[0] // 2
    panel = low[...]
    gram = dot(panel, panel, NT)
    out[:half] = gram[:half, :half].astype(out.dtype)
    out[half : 2 * half] = gram[:half, half:].astype(out.dtype)
    out[2 * half :] = gram[half:, half:].astype(out.dtype)


def picked_product(picks, low, tile, chosen):
    size = chosen.shape[0] // len(picks)
    for n, bits in enumerate(picks):
        chosen[n * size : (n + 1) * size] = low[owned(bits, size)]
    product = dot(chosen[...], tile[...])
    return [product[n * size : (n + 1) * size] for n in range(len(picks))]


def keep_body(picks, low, tile, *rest):
    for out, part in zip(rest[:-1], picked_product(picks, low, tile, rest[-1])):
        out[...] = coded(part) if out.dtype == jnp.bfloat16 else part


def copy_body(source, out):
    out[...] = source[...]


def sum_body(keep, *refs):
    total = keep[...]
    for part in refs[:-1]:
        total = total + decoded(part[...])
    refs[-1][...] = coded(total)


def base_body(mine, other, panel, factor, base, rate_out, gram):
    half = mine.shape[0] // 3
    quarters = mine[...].astype(jnp.float32) + other[...].astype(jnp.float32)
    upper, side, lower = quarters[:half], quarters[half : 2 * half], quarters[2 * half :]
    gram[:half, :half] = upper
    gram[:half, half:] = side
    gram[half:, :half] = side.T
    gram[half:, half:] = lower
    squares = upper * upper + 2.0 * (side * side) + lower * lower
    norm = jnp.sum(jnp.sum(squares, axis=1, keepdims=True), axis=0, keepdims=True)
    rate = 1.0 / (jnp.sqrt(norm) + 1e-06)
    base[...] = factor[...] - rate * split_dot(gram[owned(0, factor.shape[0])], panel[...])
    rate_out[...] = jnp.broadcast_to(rate, rate_out.shape)


def last_body(rate, base, own, *refs):
    total = own[...]
    for part in refs[:-1]:
        total = total + decoded(part[...])
    refs[-1][...] = jnp.maximum(base[...] + rate[0:1, 0:1] * total, 0.0)


def gram_of(panel):
    return dot(panel, panel, NT)


def shards(block_values, block_rows, block_cols, block_count, cell_factor, gene_factor):
    n_cell = lax.axis_size("cell")
    kdim = cell_factor.shape[0] * lax.axis_size("gene")
    size = gene_factor.shape[0]
    paired = n_cell == 8 and size % 16 == 0 and kdim % (2 * BLK) == 0

    def swap(value, bits):
        return lax.ppermute(value, "cell", [(n, n ^ bits) for n in range(n_cell)])

    def swap_core(value):
        return lax.ppermute(value, "gene", [(0, 1), (1, 0)])

    def wide(rows, dtype):
        return shape((rows, GENE_DEV), dtype)

    low_share = gene_factor.astype(jnp.bfloat16)
    factor_other = swap_core(cell_factor)
    tile, turned = dense_tile(block_values[0, 0], block_rows[0, 0], block_cols[0, 0], block_count[0])
    if paired:
        near = [swap(low_share, bits) for bits in (1, 2, 4)]
        sixth = swap(low_share, 6)
        beside, second, fourth, tile, turned, factor_other = lax.optimization_barrier(
            (*near, tile, turned, factor_other)
        )
        third, fifth = swap(beside, 2), swap(fourth, 1)
        seventh = swap(sixth, 1)
        shares = [low_share, beside, second, third, fourth, fifth, sixth]
        order = range(n_cell)
    else:
        whole = lax.all_gather(low_share, "cell", axis=0, tiled=True)
        shares, seventh, order = [whole[: -kdim // 8]], whole[-kdim // 8 :], None
    last_rows = seventh.shape[0]

    first_rows = kdim - last_rows
    part_rows = first_rows // PARTS if first_rows % (16 * PARTS) == 0 else first_rows
    n_parts = first_rows // part_rows
    panel_first, mine_first, *messages = call(
        functools.partial(first_body, n_parts),
        (
            wide(first_rows, jnp.bfloat16),
            shape((first_rows, CELL_DEV), jnp.float32),
            *[shape((part_rows, CELL_DEV), jnp.bfloat16) for _ in range(n_parts)],
        ),
        0,
        1 + len(shares),
        0,
        AHEAD,
    )(turned, *shares)
    others = [swap_core(part) for part in messages]
    rows = last_rows + kdim * kdim // CELL_DEV
    panel, mine, message = call(
        functools.partial(second_body, order),
        (
            wide(kdim, jnp.bfloat16),
            shape((rows, CELL_DEV), jnp.float32),
            shape((rows, CELL_DEV), jnp.bfloat16),
        ),
        0,
        3,
        0,
        0,
    )(turned, panel_first, seventh)
    other = swap_core(message)

    sent = [5, 3, 1]
    kept = [6, 4, 2, 0]
    updated, next_low, *sends = call(
        functools.partial(cell_body, order, [7], n_parts),
        (
            shape(cell_factor.shape, jnp.float32),
            shape((kdim, CELL_DEV), jnp.bfloat16),
            *([wide(size, jnp.bfloat16), shape((3 * kdim // 2, kdim // 2), jnp.bfloat16)] if paired else []),
        ),
        0,
        6 + n_parts,
        0,
        0,
        [
            pltpu.VMEM((first_rows, CELL_DEV), jnp.bfloat16),
            pltpu.VMEM((kdim, CELL_DEV), jnp.float32),
            pltpu.VMEM((kdim, CELL_DEV), jnp.float32),
            pltpu.VMEM((kdim, CELL_DEV), jnp.float32),
            pltpu.VMEM((size, CELL_DEV), jnp.bfloat16),
        ],
    )(tile, mine_first, mine, other, cell_factor, factor_other, *others)

    if not paired:
        cell_gram = lax.psum(gram_of(next_low), "cell")
        own_cols = lax.psum_scatter(dot(next_low, tile), "cell", scatter_dimension=0, tiled=True)
        gram_part = lax.dynamic_slice_in_dim(cell_gram, lax.axis_index("cell") * size, size, 0)
        rate_gene = 1.0 / (jnp.sqrt(jnp.sum(cell_gram * cell_gram)) + 1e-06)
        stepped = jnp.dot(
            gram_part, panel.astype(jnp.float32), precision=lax.Precision.HIGHEST
        )
        return (updated, jnp.maximum(gene_factor - rate_gene * (stepped - own_cols), 0.0))

    arrived = [swap(sends[0], 1)]
    *parts, keep_third, keep_second, keep_near, own = call(
        functools.partial(keep_body, sent + kept),
        (
            *[wide(size, jnp.bfloat16) for _ in sent],
            *[wide(size, jnp.float32) for _ in kept],
        ),
        0,
        2,
        0,
        AHEAD,
        [pltpu.VMEM((kdim - size, CELL_DEV), jnp.bfloat16)],
    )(next_low, tile)
    gram = sends[1]
    arrived += [swap(part, 1) for part in parts]

    def add_up(cost, keep, *parts):
        body = call(sum_body, wide(size, jnp.bfloat16), 0, 1 + len(parts), 0, cost)
        return body(keep, *parts)

    through = swap(add_up(AHEAD, keep_third, arrived[0]), 2)
    gram_arrived = swap(gram, 4)
    beside = swap(add_up(AHEAD, keep_near, arrived[2]), 2)
    across = add_up(AHEAD, keep_second, arrived[1], through)
    gram = (gram.astype(jnp.float32) + gram_arrived.astype(jnp.float32)).astype(jnp.bfloat16)
    gram_arrived = swap(gram, 2)
    across = swap(across, 4)
    gram = (gram.astype(jnp.float32) + gram_arrived.astype(jnp.float32)).astype(jnp.bfloat16)
    partner = swap(gram, 1)
    gram, updated = lax.optimization_barrier((gram, updated))
    cell_next = call(copy_body, shape(cell_factor.shape, jnp.float32), 0, 1, 0, 0)(updated)
    own, cell_next = lax.optimization_barrier((own, cell_next))
    base, rate = call(
        base_body,
        (wide(size, jnp.float32), shape((8, 128), jnp.float32)),
        0,
        4,
        0,
        0,
        [pltpu.VMEM((kdim, kdim), jnp.float32)],
    )(gram, partner, panel, gene_factor)
    gene_next = call(last_body, wide(size, jnp.float32), 0, 6, 0, AHEAD)(
        rate, base, own, arrived[3], beside, across
    )
    return (cell_next, gene_next)


def solution(mesh):
    return jax.shard_map(
        shards,
        mesh=mesh,
        in_specs=(
            P(("groups", "cell"), "gene", None, None, None),
            P(("groups", "cell"), "gene", None),
            P(("groups", "cell"), "gene", None),
            P(("groups", "cell"), "gene"),
            P(("groups", "gene"), "cell"),
            P(("groups", "cell"), "gene"),
        ),
        out_specs=(P(("groups", "gene"), "cell"), P(("groups", "cell"), "gene")),
        check_vma=False,
    )
```

```python
import functools

import jax
import jax.numpy as jnp
from jax import lax
from jax.experimental import pallas as pl
from jax.experimental.pallas import tpu as pltpu
from jax.sharding import PartitionSpec as P

BLK = 128
CELL_DEV = 1024
GENE_DEV = 2048
VMEM_BYTES = 24 * 2**20
AHEAD = 16 * 2**20

NT = (((1,), (1,)), ((), ()))
NN = (((1,), (0,)), ((), ()))
SMEM_SPEC = pl.BlockSpec(memory_space=pltpu.SMEM)
VMEM_SPEC = pl.BlockSpec(memory_space=pltpu.VMEM)


def dot(a, b, dims=NN):
    return lax.dot_general(a, b, dims, preferred_element_type=jnp.float32)


def split_dot(a, b):
    high = a.astype(jnp.bfloat16)
    low = (a - high.astype(jnp.float32)).astype(jnp.bfloat16)
    rows = a.shape[0]
    both = dot(jnp.concatenate([high, low], axis=0), b)
    return both[:rows] + both[rows:]


def call(body, outs, n_smem, n_vmem, flops, traffic, scratch=()):
    return pl.pallas_call(
        body,
        out_shape=outs,
        in_specs=[SMEM_SPEC] * n_smem + [VMEM_SPEC] * n_vmem,
        out_specs=jax.tree.map(lambda _: VMEM_SPEC, outs),
        scratch_shapes=list(scratch),
        compiler_params=pltpu.CompilerParams(vmem_limit_bytes=VMEM_BYTES),
        cost_estimate=pl.CostEstimate(flops=flops, bytes_accessed=traffic, transcendentals=0),
    )


def shape(dims, dtype):
    return jax.ShapeDtypeStruct(dims, dtype)


def dense_body(rows_in, cols_in, count, values, tile, turned, rows, cols, sems, index_sems):
    copies = [
        pltpu.make_async_copy(rows_in, rows, index_sems.at[0]),
        pltpu.make_async_copy(cols_in, cols, index_sems.at[1]),
    ]
    for copy in copies:
        copy.start()
    tile[...] = jnp.zeros_like(tile)
    for copy in copies:
        copy.wait()

    def block(n):
        row = pl.multiple_of(rows[n] * BLK, BLK)
        col = pl.multiple_of(cols[n] * BLK, BLK)
        place = tile.at[pl.ds(row, BLK), pl.ds(col, BLK)]
        return pltpu.make_async_copy(values.at[n], place, sems.at[n])

    def start(n, carry):
        block(n).start()
        return carry

    def wait(n, carry):
        block(n).wait()
        return carry

    lax.fori_loop(0, count[0], start, 0)
    lax.fori_loop(0, count[0], wait, 0)
    for row in range(0, tile.shape[0], TURN):
        turned[:, row : row + TURN] = tile[row : row + TURN].T


def pinned(array):
    return pltpu.with_memory_space_constraint(array, pltpu.HBM)


def dense_tile(values, rows, cols, count):
    anywhere = pl.BlockSpec(memory_space=pltpu.HBM)
    n_blocks = values.shape[0]
    return pl.pallas_call(
        dense_body,
        out_shape=(shape((CELL_DEV, GENE_DEV), jnp.bfloat16), shape((GENE_DEV, CELL_DEV), jnp.bfloat16)),
        in_specs=[anywhere, anywhere, SMEM_SPEC, anywhere],
        out_specs=(VMEM_SPEC, VMEM_SPEC),
        scratch_shapes=[
            pltpu.SMEM((n_blocks,), jnp.int32),
            pltpu.SMEM((n_blocks,), jnp.int32),
            pltpu.SemaphoreType.DMA((n_blocks,)),
            pltpu.SemaphoreType.DMA((2,)),
        ],
        compiler_params=pltpu.CompilerParams(vmem_limit_bytes=VMEM_BYTES),
        cost_estimate=pl.CostEstimate(flops=0, bytes_accessed=0, transcendentals=0),
    )(pinned(rows), pinned(cols), count, pinned(values))


def owned(bits, size):
    return pl.ds(pl.multiple_of((lax.axis_index("cell") ^ bits) * size, size), size)


STEP = 8
TURN = 256
PARTS = 2


def coded(rows):
    above, parts = None, []
    for n in range(0, rows.shape[0], STEP):
        part = rows[n : n + STEP]
        part = (part if above is None else part - above).astype(jnp.bfloat16).astype(jnp.float32)
        above = part if above is None else above + part
        parts.append(part)
    return jnp.concatenate(parts, axis=0).astype(jnp.bfloat16)


def decoded(rows):
    rows, above, parts = rows.astype(jnp.float32), None, []
    for n in range(0, rows.shape[0], STEP):
        above = rows[n : n + STEP] if above is None else above + rows[n : n + STEP]
        parts.append(above)
    return jnp.concatenate(parts, axis=0)


def first_body(count, turned, *refs):
    shares, (panel, mine), messages = refs[: -2 - count], refs[-2 - count : -count], refs[-count:]
    row = 0
    for part in shares:
        panel[row : row + part.shape[0]] = part[...]
        row += part.shape[0]
    mine[...] = dot(panel[...], turned[...])
    row = 0
    for out in messages:
        out[...] = mine[row : row + out.shape[0]].astype(out.dtype)
        row += out.shape[0]


def second_body(order, turned, first, share, panel, mine, message):
    size = share.shape[0]
    if order is None:
        panel[: first.shape[0]] = first[...]
        panel[first.shape[0] :] = share[...]
    else:
        for n, bits in enumerate(order[:-1]):
            panel[owned(bits, size)] = first[n * size : (n + 1) * size]
        panel[owned(order[-1], size)] = share[...]
    mine[:size] = dot(share[...], turned[...])
    low = panel[...]
    gram = dot(low, low, NT)
    rows, width = mine.shape[0] - size, gram.shape[1]
    for n in range(gram.shape[0] // rows):
        mine[size:, n * width : (n + 1) * width] = gram[n * rows : (n + 1) * rows]
    message[...] = mine[...].astype(message.dtype)


def cell_body(
    order, picks, count, tile, mine_first, mine, other, factor_mine, factor_other, *refs
):
    others, (cell_next, low), sends = refs[:count], refs[count : count + 2], refs[count + 2 : -5]
    other_first, factor, data, updated, chosen = refs[-5:]
    for n, part in enumerate(others):
        other_first[n * part.shape[0] : (n + 1) * part.shape[0]] = part[...]
    share = factor_mine.shape[0]
    kdim = factor.shape[0]
    core = lax.axis_index("gene")
    own = pl.ds(pl.multiple_of(core * share, share), share)
    theirs = pl.ds(pl.multiple_of((1 - core) * share, share), share)
    factor[own] = factor_mine[...]
    factor[theirs] = factor_other[...]
    both = mine[...] + other[...].astype(jnp.float32)
    size = kdim - mine_first.shape[0]
    gram = jnp.concatenate([both[size:, n : n + kdim] for n in range(0, CELL_DEV, kdim)], axis=0)
    if order is None:
        data[:-size] = mine_first[...] + other_first[...].astype(jnp.float32)
        data[-size:] = both[:size]
    else:
        for n, bits in enumerate(order[:-1]):
            rows = slice(n * size, (n + 1) * size)
            data[owned(bits, size)] = mine_first[rows] + other_first[rows].astype(jnp.float32)
        data[owned(order[-1], size)] = both[:size]
    norm = jnp.sum(jnp.sum(gram * gram, axis=1, keepdims=True), axis=0, keepdims=True)
    rate = 1.0 / (jnp.sqrt(norm) + 1e-06)
    held = factor[...]
    stepped = split_dot(gram, held.astype(jnp.bfloat16))
    updated[...] = jnp.maximum(held - rate * (stepped - data[...]), 0.0)
    cell_next[...] = updated[own]
    low[...] = updated[...].astype(jnp.bfloat16)
    if sends:
        send, gram_out = sends
        send[...] = coded(picked_product(picks, low, tile, chosen)[0])
        gram_blocks(low, gram_out)


def gram_blocks(low, out):
    half = low.shape[0] // 2

    @pl.when(lax.axis_index("gene") == 1)
    def _():
        panel = low[...]
        gram = dot(panel, panel, NT)
        out[:half] = gram[:half, :half].astype(out.dtype)
        out[half : 2 * half] = gram[:half, half:].astype(out.dtype)
        out[2 * half :] = gram[half:, half:].astype(out.dtype)

    @pl.when(lax.axis_index("gene") == 0)
    def _():
        out[...] = jnp.zeros_like(out)


def picked_product(picks, low, tile, chosen):
    size = chosen.shape[0] // len(picks)
    for n, bits in enumerate(picks):
        chosen[n * size : (n + 1) * size] = low[owned(bits, size)]
    product = dot(chosen[...], tile[...])
    return [product[n * size : (n + 1) * size] for n in range(len(picks))]


def keep_body(picks, low, tile, *rest):
    for out, part in zip(rest[:-1], picked_product(picks, low, tile, rest[-1])):
        out[...] = coded(part) if out.dtype == jnp.bfloat16 else part


def copy_body(source, out):
    out[...] = source[...]


def sum_body(keep, *refs):
    total = keep[...]
    for part in refs[:-1]:
        total = total + decoded(part[...])
    refs[-1][...] = coded(total)


def base_body(mine, other_1, other_0, given, panel, factor, base, rate_out, gram):
    half = mine.shape[0] // 3
    first = jnp.where(lax.axis_index("gene") == 1, mine[...].astype(jnp.float32), given[...].astype(jnp.float32))
    last = jnp.where(lax.axis_index("gene") == 1, other_1[...].astype(jnp.float32), other_0[...].astype(jnp.float32))
    quarters = first + last
    upper, side, lower = quarters[:half], quarters[half : 2 * half], quarters[2 * half :]
    gram[:half, :half] = upper
    gram[:half, half:] = side
    gram[half:, :half] = side.T
    gram[half:, half:] = lower
    squares = upper * upper + 2.0 * (side * side) + lower * lower
    norm = jnp.sum(jnp.sum(squares, axis=1, keepdims=True), axis=0, keepdims=True)
    rate = 1.0 / (jnp.sqrt(norm) + 1e-06)
    base[...] = factor[...] - rate * split_dot(gram[owned(0, factor.shape[0])], panel[...])
    rate_out[...] = jnp.broadcast_to(rate, rate_out.shape)


def last_body(rate, base, own, *refs):
    total = own[...]
    for part in refs[:-1]:
        total = total + decoded(part[...])
    refs[-1][...] = jnp.maximum(base[...] + rate[0:1, 0:1] * total, 0.0)


def gram_of(panel):
    return dot(panel, panel, NT)


def shards(block_values, block_rows, block_cols, block_count, cell_factor, gene_factor):
    n_cell = lax.axis_size("cell")
    kdim = cell_factor.shape[0] * lax.axis_size("gene")
    size = gene_factor.shape[0]
    paired = n_cell == 8 and size % 16 == 0 and kdim % (2 * BLK) == 0

    def swap(value, bits):
        return lax.ppermute(value, "cell", [(n, n ^ bits) for n in range(n_cell)])

    def from_core_1(value, bits, core):
        n_gene = lax.axis_size("gene")
        pairs = [(n * n_gene + 1, (n ^ bits) * n_gene + core) for n in range(n_cell)]
        return lax.ppermute(value, ("cell", "gene"), pairs)

    def swap_core(value):
        return lax.ppermute(value, "gene", [(0, 1), (1, 0)])

    def wide(rows, dtype):
        return shape((rows, GENE_DEV), dtype)

    low_share = gene_factor.astype(jnp.bfloat16)
    factor_other = swap_core(cell_factor)
    tile, turned = dense_tile(block_values[0, 0], block_rows[0, 0], block_cols[0, 0], block_count[0])
    if paired:
        near = [swap(low_share, bits) for bits in (1, 2, 4)]
        sixth = swap(low_share, 6)
        beside, second, fourth, tile, turned, factor_other = lax.optimization_barrier(
            (*near, tile, turned, factor_other)
        )
        third, fifth = swap(beside, 2), swap(fourth, 1)
        seventh = swap(sixth, 1)
        shares = [low_share, beside, second, third, fourth, fifth, sixth]
        order = range(n_cell)
    else:
        whole = lax.all_gather(low_share, "cell", axis=0, tiled=True)
        shares, seventh, order = [whole[: -kdim // 8]], whole[-kdim // 8 :], None
    last_rows = seventh.shape[0]

    first_rows = kdim - last_rows
    part_rows = first_rows // PARTS if first_rows % (16 * PARTS) == 0 else first_rows
    n_parts = first_rows // part_rows
    panel_first, mine_first, *messages = call(
        functools.partial(first_body, n_parts),
        (
            wide(first_rows, jnp.bfloat16),
            shape((first_rows, CELL_DEV), jnp.float32),
            *[shape((part_rows, CELL_DEV), jnp.bfloat16) for _ in range(n_parts)],
        ),
        0,
        1 + len(shares),
        0,
        AHEAD,
    )(turned, *shares)
    others = [swap_core(part) for part in messages]
    rows = last_rows + kdim * kdim // CELL_DEV
    panel, mine, message = call(
        functools.partial(second_body, order),
        (
            wide(kdim, jnp.bfloat16),
            shape((rows, CELL_DEV), jnp.float32),
            shape((rows, CELL_DEV), jnp.bfloat16),
        ),
        0,
        3,
        0,
        0,
    )(turned, panel_first, seventh)
    other = swap_core(message)

    sent = [5, 3, 1]
    kept = [6, 4, 2, 0]
    updated, next_low, *sends = call(
        functools.partial(cell_body, order, [7], n_parts),
        (
            shape(cell_factor.shape, jnp.float32),
            shape((kdim, CELL_DEV), jnp.bfloat16),
            *([wide(size, jnp.bfloat16), shape((3 * kdim // 2, kdim // 2), jnp.bfloat16)] if paired else []),
        ),
        0,
        6 + n_parts,
        0,
        0,
        [
            pltpu.VMEM((first_rows, CELL_DEV), jnp.bfloat16),
            pltpu.VMEM((kdim, CELL_DEV), jnp.float32),
            pltpu.VMEM((kdim, CELL_DEV), jnp.float32),
            pltpu.VMEM((kdim, CELL_DEV), jnp.float32),
            pltpu.VMEM((size, CELL_DEV), jnp.bfloat16),
        ],
    )(tile, mine_first, mine, other, cell_factor, factor_other, *others)

    if not paired:
        cell_gram = lax.psum(gram_of(next_low), "cell")
        own_cols = lax.psum_scatter(dot(next_low, tile), "cell", scatter_dimension=0, tiled=True)
        gram_part = lax.dynamic_slice_in_dim(cell_gram, lax.axis_index("cell") * size, size, 0)
        rate_gene = 1.0 / (jnp.sqrt(jnp.sum(cell_gram * cell_gram)) + 1e-06)
        stepped = jnp.dot(
            gram_part, panel.astype(jnp.float32), precision=lax.Precision.HIGHEST
        )
        return (updated, jnp.maximum(gene_factor - rate_gene * (stepped - own_cols), 0.0))

    arrived = [swap(sends[0], 1)]
    *parts, keep_third, keep_second, keep_near, own = call(
        functools.partial(keep_body, sent + kept),
        (
            *[wide(size, jnp.bfloat16) for _ in sent],
            *[wide(size, jnp.float32) for _ in kept],
        ),
        0,
        2,
        0,
        AHEAD,
        [pltpu.VMEM((kdim - size, CELL_DEV), jnp.bfloat16)],
    )(next_low, tile)
    gram = sends[1]
    arrived += [swap(part, 1) for part in parts]

    def add_up(cost, keep, *parts):
        body = call(sum_body, wide(size, jnp.bfloat16), 0, 1 + len(parts), 0, cost)
        return body(keep, *parts)

    through = swap(add_up(AHEAD, keep_third, arrived[0]), 2)
    gram_arrived = from_core_1(gram, 4, 1)
    beside = swap(add_up(AHEAD, keep_near, arrived[2]), 2)
    across = add_up(AHEAD, keep_second, arrived[1], through)
    gram = (gram.astype(jnp.float32) + gram_arrived.astype(jnp.float32)).astype(jnp.bfloat16)
    gram_arrived = from_core_1(gram, 2, 1)
    across = swap(across, 4)
    gram = (gram.astype(jnp.float32) + gram_arrived.astype(jnp.float32)).astype(jnp.bfloat16)
    partner = (from_core_1(gram, 1, 1), from_core_1(gram, 1, 0), from_core_1(gram, 0, 0))
    gram, updated = lax.optimization_barrier((gram, updated))
    cell_next = call(copy_body, shape(cell_factor.shape, jnp.float32), 0, 1, 0, 0)(updated)
    own, cell_next = lax.optimization_barrier((own, cell_next))
    *partner, beside = lax.optimization_barrier((*partner, beside))
    base, rate = call(
        base_body,
        (wide(size, jnp.float32), shape((8, 128), jnp.float32)),
        0,
        6,
        0,
        0,
        [pltpu.VMEM((kdim, kdim), jnp.float32)],
    )(gram, *partner, panel, gene_factor)
    gene_next = call(last_body, wide(size, jnp.float32), 0, 6, 0, AHEAD)(
        rate, base, own, arrived[3], beside, across
    )
    return (cell_next, gene_next)


def solution(mesh):
    return jax.shard_map(
        shards,
        mesh=mesh,
        in_specs=(
            P(("groups", "cell"), "gene", None, None, None),
            P(("groups", "cell"), "gene", None),
            P(("groups", "cell"), "gene", None),
            P(("groups", "cell"), "gene"),
            P(("groups", "gene"), "cell"),
            P(("groups", "cell"), "gene"),
        ),
        out_specs=(P(("groups", "gene"), "cell"), P(("groups", "cell"), "gene")),
        check_vma=False,
    )
```

```python
import functools

import jax
import jax.numpy as jnp
from jax import lax
from jax.experimental import pallas as pl
from jax.experimental.pallas import tpu as pltpu
from jax.sharding import PartitionSpec as P

BLK = 128
CELL_DEV = 1024
GENE_DEV = 2048
VMEM_BYTES = 24 * 2**20
AHEAD = 16 * 2**20

NT = (((1,), (1,)), ((), ()))
NN = (((1,), (0,)), ((), ()))
SMEM_SPEC = pl.BlockSpec(memory_space=pltpu.SMEM)
VMEM_SPEC = pl.BlockSpec(memory_space=pltpu.VMEM)


def dot(a, b, dims=NN):
    return lax.dot_general(a, b, dims, preferred_element_type=jnp.float32)


def split_dot(a, b):
    high = a.astype(jnp.bfloat16)
    low = (a - high.astype(jnp.float32)).astype(jnp.bfloat16)
    rows = a.shape[0]
    both = dot(jnp.concatenate([high, low], axis=0), b)
    return both[:rows] + both[rows:]


def call(body, outs, n_smem, n_vmem, flops, traffic, scratch=()):
    return pl.pallas_call(
        body,
        out_shape=outs,
        in_specs=[SMEM_SPEC] * n_smem + [VMEM_SPEC] * n_vmem,
        out_specs=jax.tree.map(lambda _: VMEM_SPEC, outs),
        scratch_shapes=list(scratch),
        compiler_params=pltpu.CompilerParams(vmem_limit_bytes=VMEM_BYTES),
        cost_estimate=pl.CostEstimate(flops=flops, bytes_accessed=traffic, transcendentals=0),
    )


def shape(dims, dtype):
    return jax.ShapeDtypeStruct(dims, dtype)


def dense_body(rows_in, cols_in, count, values, tile, turned, rows, cols, sems, index_sems):
    copies = [
        pltpu.make_async_copy(rows_in, rows, index_sems.at[0]),
        pltpu.make_async_copy(cols_in, cols, index_sems.at[1]),
    ]
    for copy in copies:
        copy.start()
    tile[...] = jnp.zeros_like(tile)
    for copy in copies:
        copy.wait()

    def block(n):
        row = pl.multiple_of(rows[n] * BLK, BLK)
        col = pl.multiple_of(cols[n] * BLK, BLK)
        place = tile.at[pl.ds(row, BLK), pl.ds(col, BLK)]
        return pltpu.make_async_copy(values.at[n], place, sems.at[n])

    def start(n, carry):
        block(n).start()
        return carry

    def wait(n, carry):
        block(n).wait()
        return carry

    lax.fori_loop(0, count[0], start, 0)
    lax.fori_loop(0, count[0], wait, 0)
    for row in range(0, tile.shape[0], TURN):
        turned[:, row : row + TURN] = tile[row : row + TURN].T


def pinned(array):
    return pltpu.with_memory_space_constraint(array, pltpu.HBM)


def dense_tile(values, rows, cols, count):
    anywhere = pl.BlockSpec(memory_space=pltpu.HBM)
    n_blocks = values.shape[0]
    return pl.pallas_call(
        dense_body,
        out_shape=(shape((CELL_DEV, GENE_DEV), jnp.bfloat16), shape((GENE_DEV, CELL_DEV), jnp.bfloat16)),
        in_specs=[anywhere, anywhere, SMEM_SPEC, anywhere],
        out_specs=(VMEM_SPEC, VMEM_SPEC),
        scratch_shapes=[
            pltpu.SMEM((n_blocks,), jnp.int32),
            pltpu.SMEM((n_blocks,), jnp.int32),
            pltpu.SemaphoreType.DMA((n_blocks,)),
            pltpu.SemaphoreType.DMA((2,)),
        ],
        compiler_params=pltpu.CompilerParams(vmem_limit_bytes=VMEM_BYTES),
        cost_estimate=pl.CostEstimate(flops=0, bytes_accessed=0, transcendentals=0),
    )(pinned(rows), pinned(cols), count, pinned(values))


def owned(bits, size):
    return pl.ds(pl.multiple_of((lax.axis_index("cell") ^ bits) * size, size), size)


STEP = 8
TURN = 256
PARTS = 2


def coded(rows):
    above, parts = None, []
    for n in range(0, rows.shape[0], STEP):
        part = rows[n : n + STEP]
        part = (part if above is None else part - above).astype(jnp.bfloat16).astype(jnp.float32)
        above = part if above is None else above + part
        parts.append(part)
    return jnp.concatenate(parts, axis=0).astype(jnp.bfloat16)


def decoded(rows):
    rows, above, parts = rows.astype(jnp.float32), None, []
    for n in range(0, rows.shape[0], STEP):
        above = rows[n : n + STEP] if above is None else above + rows[n : n + STEP]
        parts.append(above)
    return jnp.concatenate(parts, axis=0)


def first_body(count, turned, *refs):
    shares, (panel, mine), messages = refs[: -2 - count], refs[-2 - count : -count], refs[-count:]
    row = 0
    for part in shares:
        panel[row : row + part.shape[0]] = part[...]
        row += part.shape[0]
    mine[...] = dot(panel[...], turned[...])
    row = 0
    for out in messages:
        out[...] = mine[row : row + out.shape[0]].astype(out.dtype)
        row += out.shape[0]


def second_body(order, turned, first, share, panel, mine, message):
    size = share.shape[0]
    if order is None:
        panel[: first.shape[0]] = first[...]
        panel[first.shape[0] :] = share[...]
    else:
        for n, bits in enumerate(order[:-1]):
            panel[owned(bits, size)] = first[n * size : (n + 1) * size]
        panel[owned(order[-1], size)] = share[...]
    mine[:size] = dot(share[...], turned[...])
    low = panel[...]
    gram = dot(low, low, NT)
    rows, width = mine.shape[0] - size, gram.shape[1]
    for n in range(gram.shape[0] // rows):
        mine[size:, n * width : (n + 1) * width] = gram[n * rows : (n + 1) * rows]
    message[...] = mine[...].astype(message.dtype)


def cell_body(
    order, picks, count, tile, mine_first, mine, other, factor_mine, factor_other, *refs
):
    others, (cell_next, low), sends = refs[:count], refs[count : count + 2], refs[count + 2 : -5]
    other_first, factor, data, updated, chosen = refs[-5:]
    for n, part in enumerate(others):
        other_first[n * part.shape[0] : (n + 1) * part.shape[0]] = part[...]
    share = factor_mine.shape[0]
    kdim = factor.shape[0]
    core = lax.axis_index("gene")
    own = pl.ds(pl.multiple_of(core * share, share), share)
    theirs = pl.ds(pl.multiple_of((1 - core) * share, share), share)
    factor[own] = factor_mine[...]
    factor[theirs] = factor_other[...]
    both = mine[...] + other[...].astype(jnp.float32)
    size = kdim - mine_first.shape[0]
    gram = jnp.concatenate([both[size:, n : n + kdim] for n in range(0, CELL_DEV, kdim)], axis=0)
    if order is None:
        data[:-size] = mine_first[...] + other_first[...].astype(jnp.float32)
        data[-size:] = both[:size]
    else:
        for n, bits in enumerate(order[:-1]):
            rows = slice(n * size, (n + 1) * size)
            data[owned(bits, size)] = mine_first[rows] + other_first[rows].astype(jnp.float32)
        data[owned(order[-1], size)] = both[:size]
    norm = jnp.sum(jnp.sum(gram * gram, axis=1, keepdims=True), axis=0, keepdims=True)
    rate = 1.0 / (jnp.sqrt(norm) + 1e-06)
    held = factor[...]
    stepped = split_dot(gram, held.astype(jnp.bfloat16))
    updated[...] = jnp.maximum(held - rate * (stepped - data[...]), 0.0)
    cell_next[...] = updated[own]
    low[...] = updated[...].astype(jnp.bfloat16)
    if sends:
        send, gram_out = sends
        send[...] = coded(picked_product(picks, low, tile, chosen)[0])
        gram_blocks(low, gram_out)


def gram_blocks(low, out):
    half = low.shape[0] // 2
    panel = low[...]
    gram = dot(panel, panel, NT)
    out[:half] = gram[:half, :half].astype(out.dtype)
    out[half : 2 * half] = gram[:half, half:].astype(out.dtype)
    out[2 * half :] = gram[half:, half:].astype(out.dtype)


def picked_product(picks, low, tile, chosen):
    size = chosen.shape[0] // len(picks)
    for n, bits in enumerate(picks):
        chosen[n * size : (n + 1) * size] = low[owned(bits, size)]
    product = dot(chosen[...], tile[...])
    return [product[n * size : (n + 1) * size] for n in range(len(picks))]


def keep_body(picks, low, tile, send_pair, send, *rest):
    first, second, third, *kept = picked_product(picks, low, tile, rest[-1])
    size = first.shape[0]
    send_pair[:size] = coded(first)
    send_pair[size:] = coded(second)
    send[...] = coded(third)
    for out, part in zip(rest[:-1], kept):
        out[...] = part


def copy_body(source, out):
    out[...] = source[...]


def sum_body(which, keep, *refs):
    size = keep.shape[0]
    total = keep[...] + decoded(refs[0][which * size : (which + 1) * size])
    for part in refs[1:-1]:
        total = total + decoded(part[...])
    refs[-1][...] = coded(total)


def base_body(mine, other, panel, factor, base, rate_out, gram):
    half = mine.shape[0] // 3
    quarters = mine[...].astype(jnp.float32) + other[...].astype(jnp.float32)
    upper, side, lower = quarters[:half], quarters[half : 2 * half], quarters[2 * half :]
    gram[:half, :half] = upper
    gram[:half, half:] = side
    gram[half:, :half] = side.T
    gram[half:, half:] = lower
    squares = upper * upper + 2.0 * (side * side) + lower * lower
    norm = jnp.sum(jnp.sum(squares, axis=1, keepdims=True), axis=0, keepdims=True)
    rate = 1.0 / (jnp.sqrt(norm) + 1e-06)
    base[...] = factor[...] - rate * split_dot(gram[owned(0, factor.shape[0])], panel[...])
    rate_out[...] = jnp.broadcast_to(rate, rate_out.shape)


def last_body(rate, base, own, *refs):
    total = own[...]
    for part in refs[:-1]:
        total = total + decoded(part[...])
    refs[-1][...] = jnp.maximum(base[...] + rate[0:1, 0:1] * total, 0.0)


def gram_of(panel):
    return dot(panel, panel, NT)


def shards(block_values, block_rows, block_cols, block_count, cell_factor, gene_factor):
    n_cell = lax.axis_size("cell")
    kdim = cell_factor.shape[0] * lax.axis_size("gene")
    size = gene_factor.shape[0]
    paired = n_cell == 8 and size % 16 == 0 and kdim % (2 * BLK) == 0

    def swap(value, bits):
        return lax.ppermute(value, "cell", [(n, n ^ bits) for n in range(n_cell)])

    def swap_core(value):
        return lax.ppermute(value, "gene", [(0, 1), (1, 0)])

    def wide(rows, dtype):
        return shape((rows, GENE_DEV), dtype)

    low_share = gene_factor.astype(jnp.bfloat16)
    factor_other = swap_core(cell_factor)
    tile, turned = dense_tile(block_values[0, 0], block_rows[0, 0], block_cols[0, 0], block_count[0])
    if paired:
        near = [swap(low_share, bits) for bits in (1, 2, 4)]
        sixth = swap(low_share, 6)
        beside, second, fourth, tile, turned, factor_other = lax.optimization_barrier(
            (*near, tile, turned, factor_other)
        )
        third, fifth = swap(beside, 2), swap(fourth, 1)
        seventh = swap(sixth, 1)
        shares = [low_share, beside, second, third, fourth, fifth, sixth]
        order = range(n_cell)
    else:
        whole = lax.all_gather(low_share, "cell", axis=0, tiled=True)
        shares, seventh, order = [whole[: -kdim // 8]], whole[-kdim // 8 :], None
    last_rows = seventh.shape[0]

    first_rows = kdim - last_rows
    part_rows = first_rows // PARTS if first_rows % (16 * PARTS) == 0 else first_rows
    n_parts = first_rows // part_rows
    panel_first, mine_first, *messages = call(
        functools.partial(first_body, n_parts),
        (
            wide(first_rows, jnp.bfloat16),
            shape((first_rows, CELL_DEV), jnp.float32),
            *[shape((part_rows, CELL_DEV), jnp.bfloat16) for _ in range(n_parts)],
        ),
        0,
        1 + len(shares),
        0,
        AHEAD,
    )(turned, *shares)
    others = [swap_core(part) for part in messages]
    rows = last_rows + kdim * kdim // CELL_DEV
    panel, mine, message = call(
        functools.partial(second_body, order),
        (
            wide(kdim, jnp.bfloat16),
            shape((rows, CELL_DEV), jnp.float32),
            shape((rows, CELL_DEV), jnp.bfloat16),
        ),
        0,
        3,
        0,
        0,
    )(turned, panel_first, seventh)
    other = swap_core(message)

    sent = [5, 3, 1]
    kept = [6, 4, 2, 0]
    updated, next_low, *sends = call(
        functools.partial(cell_body, order, [7], n_parts),
        (
            shape(cell_factor.shape, jnp.float32),
            shape((kdim, CELL_DEV), jnp.bfloat16),
            *([wide(size, jnp.bfloat16), shape((3 * kdim // 2, kdim // 2), jnp.bfloat16)] if paired else []),
        ),
        0,
        6 + n_parts,
        0,
        0,
        [
            pltpu.VMEM((first_rows, CELL_DEV), jnp.bfloat16),
            pltpu.VMEM((kdim, CELL_DEV), jnp.float32),
            pltpu.VMEM((kdim, CELL_DEV), jnp.float32),
            pltpu.VMEM((kdim, CELL_DEV), jnp.float32),
            pltpu.VMEM((size, CELL_DEV), jnp.bfloat16),
        ],
    )(tile, mine_first, mine, other, cell_factor, factor_other, *others)

    if not paired:
        cell_gram = lax.psum(gram_of(next_low), "cell")
        own_cols = lax.psum_scatter(dot(next_low, tile), "cell", scatter_dimension=0, tiled=True)
        gram_part = lax.dynamic_slice_in_dim(cell_gram, lax.axis_index("cell") * size, size, 0)
        rate_gene = 1.0 / (jnp.sqrt(jnp.sum(cell_gram * cell_gram)) + 1e-06)
        stepped = jnp.dot(
            gram_part, panel.astype(jnp.float32), precision=lax.Precision.HIGHEST
        )
        return (updated, jnp.maximum(gene_factor - rate_gene * (stepped - own_cols), 0.0))

    arrived = [swap(sends[0], 1)]
    *parts, keep_third, keep_second, keep_near, own = call(
        functools.partial(keep_body, sent + kept),
        (
            wide(2 * size, jnp.bfloat16),
            wide(size, jnp.bfloat16),
            *[wide(size, jnp.float32) for _ in kept],
        ),
        0,
        2,
        0,
        AHEAD,
        [pltpu.VMEM((kdim - size, CELL_DEV), jnp.bfloat16)],
    )(next_low, tile)
    gram = sends[1]
    arrived += [swap(part, 1) for part in parts]

    def add_up(which, keep, *parts):
        body = functools.partial(sum_body, which)
        return call(body, wide(size, jnp.bfloat16), 0, 1 + len(parts), 0, AHEAD)(keep, *parts)

    through = swap(add_up(0, keep_third, arrived[0]), 2)
    gram_arrived = swap(gram, 4)
    beside = swap(add_up(1, keep_near, arrived[1]), 2)
    across = add_up(0, keep_second, arrived[1], through)
    gram = (gram.astype(jnp.float32) + gram_arrived.astype(jnp.float32)).astype(jnp.bfloat16)
    gram_arrived = swap(gram, 2)
    across = swap(across, 4)
    gram = (gram.astype(jnp.float32) + gram_arrived.astype(jnp.float32)).astype(jnp.bfloat16)
    partner = swap(gram, 1)
    gram, updated = lax.optimization_barrier((gram, updated))
    cell_next = call(copy_body, shape(cell_factor.shape, jnp.float32), 0, 1, 0, 0)(updated)
    own, cell_next = lax.optimization_barrier((own, cell_next))
    base, rate = call(
        base_body,
        (wide(size, jnp.float32), shape((8, 128), jnp.float32)),
        0,
        4,
        0,
        0,
        [pltpu.VMEM((kdim, kdim), jnp.float32)],
    )(gram, partner, panel, gene_factor)
    gene_next = call(last_body, wide(size, jnp.float32), 0, 6, 0, AHEAD)(
        rate, base, own, arrived[2], beside, across
    )
    return (cell_next, gene_next)


def solution(mesh):
    return jax.shard_map(
        shards,
        mesh=mesh,
        in_specs=(
            P(("groups", "cell"), "gene", None, None, None),
            P(("groups", "cell"), "gene", None),
            P(("groups", "cell"), "gene", None),
            P(("groups", "cell"), "gene"),
            P(("groups", "gene"), "cell"),
            P(("groups", "cell"), "gene"),
        ),
        out_specs=(P(("groups", "gene"), "cell"), P(("groups", "cell"), "gene")),
        check_vma=False,
    )
```

```python
import functools

import jax
import jax.numpy as jnp
from jax import lax
from jax.experimental import pallas as pl
from jax.experimental.pallas import tpu as pltpu
from jax.sharding import PartitionSpec as P

BLK = 128
CELL_DEV = 1024
GENE_DEV = 2048
VMEM_BYTES = 24 * 2**20
AHEAD = 16 * 2**20

NT = (((1,), (1,)), ((), ()))
NN = (((1,), (0,)), ((), ()))
SMEM_SPEC = pl.BlockSpec(memory_space=pltpu.SMEM)
VMEM_SPEC = pl.BlockSpec(memory_space=pltpu.VMEM)


def dot(a, b, dims=NN):
    return lax.dot_general(a, b, dims, preferred_element_type=jnp.float32)


def split_dot(a, b):
    high = a.astype(jnp.bfloat16)
    low = (a - high.astype(jnp.float32)).astype(jnp.bfloat16)
    rows = a.shape[0]
    both = dot(jnp.concatenate([high, low], axis=0), b)
    return both[:rows] + both[rows:]


def call(body, outs, n_smem, n_vmem, flops, traffic, scratch=()):
    return pl.pallas_call(
        body,
        out_shape=outs,
        in_specs=[SMEM_SPEC] * n_smem + [VMEM_SPEC] * n_vmem,
        out_specs=jax.tree.map(lambda _: VMEM_SPEC, outs),
        scratch_shapes=list(scratch),
        compiler_params=pltpu.CompilerParams(vmem_limit_bytes=VMEM_BYTES),
        cost_estimate=pl.CostEstimate(flops=flops, bytes_accessed=traffic, transcendentals=0),
    )


def shape(dims, dtype):
    return jax.ShapeDtypeStruct(dims, dtype)


def dense_body(rows_in, cols_in, count, values, tile, turned, rows, cols, sems, index_sems):
    copies = [
        pltpu.make_async_copy(rows_in, rows, index_sems.at[0]),
        pltpu.make_async_copy(cols_in, cols, index_sems.at[1]),
    ]
    for copy in copies:
        copy.start()
    tile[...] = jnp.zeros_like(tile)
    for copy in copies:
        copy.wait()

    def block(n):
        row = pl.multiple_of(rows[n] * BLK, BLK)
        col = pl.multiple_of(cols[n] * BLK, BLK)
        place = tile.at[pl.ds(row, BLK), pl.ds(col, BLK)]
        return pltpu.make_async_copy(values.at[n], place, sems.at[n])

    def start(n, carry):
        block(n).start()
        return carry

    def wait(n, carry):
        block(n).wait()
        return carry

    lax.fori_loop(0, count[0], start, 0)
    lax.fori_loop(0, count[0], wait, 0)
    for row in range(0, tile.shape[0], TURN):
        turned[:, row : row + TURN] = tile[row : row + TURN].T


def pinned(array):
    return pltpu.with_memory_space_constraint(array, pltpu.HBM)


def dense_tile(values, rows, cols, count):
    anywhere = pl.BlockSpec(memory_space=pltpu.HBM)
    n_blocks = values.shape[0]
    return pl.pallas_call(
        dense_body,
        out_shape=(shape((CELL_DEV, GENE_DEV), jnp.bfloat16), shape((GENE_DEV, CELL_DEV), jnp.bfloat16)),
        in_specs=[anywhere, anywhere, SMEM_SPEC, anywhere],
        out_specs=(VMEM_SPEC, VMEM_SPEC),
        scratch_shapes=[
            pltpu.SMEM((n_blocks,), jnp.int32),
            pltpu.SMEM((n_blocks,), jnp.int32),
            pltpu.SemaphoreType.DMA((n_blocks,)),
            pltpu.SemaphoreType.DMA((2,)),
        ],
        compiler_params=pltpu.CompilerParams(vmem_limit_bytes=VMEM_BYTES),
        cost_estimate=pl.CostEstimate(flops=0, bytes_accessed=0, transcendentals=0),
    )(pinned(rows), pinned(cols), count, pinned(values))


def owned(bits, size):
    return pl.ds(pl.multiple_of((lax.axis_index("cell") ^ bits) * size, size), size)


STEP = 8
TURN = 256
PARTS = 2


def coded(rows):
    above, parts = None, []
    for n in range(0, rows.shape[0], STEP):
        part = rows[n : n + STEP]
        part = (part if above is None else part - above).astype(jnp.bfloat16).astype(jnp.float32)
        above = part if above is None else above + part
        parts.append(part)
    return jnp.concatenate(parts, axis=0).astype(jnp.bfloat16)


def decoded(rows):
    rows, above, parts = rows.astype(jnp.float32), None, []
    for n in range(0, rows.shape[0], STEP):
        above = rows[n : n + STEP] if above is None else above + rows[n : n + STEP]
        parts.append(above)
    return jnp.concatenate(parts, axis=0)


def first_body(count, turned, *refs):
    shares, (panel, mine), messages = refs[: -2 - count], refs[-2 - count : -count], refs[-count:]
    row = 0
    for part in shares:
        panel[row : row + part.shape[0]] = part[...]
        row += part.shape[0]
    mine[...] = dot(panel[...], turned[...])
    row = 0
    for out in messages:
        out[...] = mine[row : row + out.shape[0]].astype(out.dtype)
        row += out.shape[0]


def second_body(order, turned, first, share, panel, mine, message):
    size = share.shape[0]
    if order is None:
        panel[: first.shape[0]] = first[...]
        panel[first.shape[0] :] = share[...]
    else:
        for n, bits in enumerate(order[:-1]):
            panel[owned(bits, size)] = first[n * size : (n + 1) * size]
        panel[owned(order[-1], size)] = share[...]
    mine[:size] = dot(share[...], turned[...])
    low = panel[...]
    gram = dot(low, low, NT)
    rows, width = mine.shape[0] - size, gram.shape[1]
    for n in range(gram.shape[0] // rows):
        mine[size:, n * width : (n + 1) * width] = gram[n * rows : (n + 1) * rows]
    message[...] = mine[...].astype(message.dtype)


def cell_body(
    order, picks, count, tile, mine_first, mine, other, factor_mine, factor_other, *refs
):
    others, (cell_next, low), sends = refs[:count], refs[count : count + 2], refs[count + 2 : -5]
    other_first, factor, data, updated, chosen = refs[-5:]
    for n, part in enumerate(others):
        other_first[n * part.shape[0] : (n + 1) * part.shape[0]] = part[...]
    share = factor_mine.shape[0]
    kdim = factor.shape[0]
    core = lax.axis_index("gene")
    own = pl.ds(pl.multiple_of(core * share, share), share)
    theirs = pl.ds(pl.multiple_of((1 - core) * share, share), share)
    factor[own] = factor_mine[...]
    factor[theirs] = factor_other[...]
    both = mine[...] + other[...].astype(jnp.float32)
    size = kdim - mine_first.shape[0]
    gram = jnp.concatenate([both[size:, n : n + kdim] for n in range(0, CELL_DEV, kdim)], axis=0)
    if order is None:
        data[:-size] = mine_first[...] + other_first[...].astype(jnp.float32)
        data[-size:] = both[:size]
    else:
        for n, bits in enumerate(order[:-1]):
            rows = slice(n * size, (n + 1) * size)
            data[owned(bits, size)] = mine_first[rows] + other_first[rows].astype(jnp.float32)
        data[owned(order[-1], size)] = both[:size]
    norm = jnp.sum(jnp.sum(gram * gram, axis=1, keepdims=True), axis=0, keepdims=True)
    rate = 1.0 / (jnp.sqrt(norm) + 1e-06)
    held = factor[...]
    stepped = split_dot(gram, held.astype(jnp.bfloat16))
    updated[...] = jnp.maximum(held - rate * (stepped - data[...]), 0.0)
    cell_next[...] = updated[own]
    low[...] = updated[...].astype(jnp.bfloat16)
    if sends:
        sends[0][...] = coded(picked_product(picks, low, tile, chosen)[0])


def gram_blocks(low, out):
    half = low.shape[0] // 2
    panel = low[...]
    gram = dot(panel, panel, NT)
    out[:half] = gram[:half, :half].astype(out.dtype)
    out[half : 2 * half] = gram[:half, half:].astype(out.dtype)
    out[2 * half :] = gram[half:, half:].astype(out.dtype)


def picked_product(picks, low, tile, chosen):
    size = chosen.shape[0] // len(picks)
    for n, bits in enumerate(picks):
        chosen[n * size : (n + 1) * size] = low[owned(bits, size)]
    product = dot(chosen[...], tile[...])
    return [product[n * size : (n + 1) * size] for n in range(len(picks))]


def keep_body(picks, low, tile, gram, send_pair, send, *rest):
    first, second, third, *kept = picked_product(picks, low, tile, rest[-1])
    size = first.shape[0]
    send_pair[:size] = coded(first)
    send_pair[size:] = coded(second)
    send[...] = coded(third)
    for out, part in zip(rest[:-1], kept):
        out[...] = part
    gram_blocks(low, gram)


def copy_body(source, out):
    out[...] = source[...]


def sum_body(which, keep, *refs):
    size = keep.shape[0]
    total = keep[...] + decoded(refs[0][which * size : (which + 1) * size])
    for part in refs[1:-1]:
        total = total + decoded(part[...])
    refs[-1][...] = coded(total)


def base_body(mine, other, panel, factor, base, rate_out, gram):
    half = mine.shape[0] // 3
    quarters = mine[...].astype(jnp.float32) + other[...].astype(jnp.float32)
    upper, side, lower = quarters[:half], quarters[half : 2 * half], quarters[2 * half :]
    gram[:half, :half] = upper
    gram[:half, half:] = side
    gram[half:, :half] = side.T
    gram[half:, half:] = lower
    squares = upper * upper + 2.0 * (side * side) + lower * lower
    norm = jnp.sum(jnp.sum(squares, axis=1, keepdims=True), axis=0, keepdims=True)
    rate = 1.0 / (jnp.sqrt(norm) + 1e-06)
    base[...] = factor[...] - rate * split_dot(gram[owned(0, factor.shape[0])], panel[...])
    rate_out[...] = jnp.broadcast_to(rate, rate_out.shape)


def last_body(rate, base, own, *refs):
    total = own[...]
    for part in refs[:-1]:
        total = total + decoded(part[...])
    refs[-1][...] = jnp.maximum(base[...] + rate[0:1, 0:1] * total, 0.0)


def gram_of(panel):
    return dot(panel, panel, NT)


def shards(block_values, block_rows, block_cols, block_count, cell_factor, gene_factor):
    n_cell = lax.axis_size("cell")
    kdim = cell_factor.shape[0] * lax.axis_size("gene")
    size = gene_factor.shape[0]
    paired = n_cell == 8 and size % 16 == 0 and kdim % (2 * BLK) == 0

    def swap(value, bits):
        return lax.ppermute(value, "cell", [(n, n ^ bits) for n in range(n_cell)])

    def swap_core(value):
        return lax.ppermute(value, "gene", [(0, 1), (1, 0)])

    def wide(rows, dtype):
        return shape((rows, GENE_DEV), dtype)

    low_share = gene_factor.astype(jnp.bfloat16)
    factor_other = swap_core(cell_factor)
    tile, turned = dense_tile(block_values[0, 0], block_rows[0, 0], block_cols[0, 0], block_count[0])
    if paired:
        near = [swap(low_share, bits) for bits in (1, 2, 4)]
        sixth = swap(low_share, 6)
        beside, second, fourth, tile, turned, factor_other = lax.optimization_barrier(
            (*near, tile, turned, factor_other)
        )
        third, fifth = swap(beside, 2), swap(fourth, 1)
        seventh = swap(sixth, 1)
        shares = [low_share, beside, second, third, fourth, fifth, sixth]
        order = range(n_cell)
    else:
        whole = lax.all_gather(low_share, "cell", axis=0, tiled=True)
        shares, seventh, order = [whole[: -kdim // 8]], whole[-kdim // 8 :], None
    last_rows = seventh.shape[0]

    first_rows = kdim - last_rows
    part_rows = first_rows // PARTS if first_rows % (16 * PARTS) == 0 else first_rows
    n_parts = first_rows // part_rows
    panel_first, mine_first, *messages = call(
        functools.partial(first_body, n_parts),
        (
            wide(first_rows, jnp.bfloat16),
            shape((first_rows, CELL_DEV), jnp.float32),
            *[shape((part_rows, CELL_DEV), jnp.bfloat16) for _ in range(n_parts)],
        ),
        0,
        1 + len(shares),
        0,
        AHEAD,
    )(turned, *shares)
    others = [swap_core(part) for part in messages]
    rows = last_rows + kdim * kdim // CELL_DEV
    panel, mine, message = call(
        functools.partial(second_body, order),
        (
            wide(kdim, jnp.bfloat16),
            shape((rows, CELL_DEV), jnp.float32),
            shape((rows, CELL_DEV), jnp.bfloat16),
        ),
        0,
        3,
        0,
        0,
    )(turned, panel_first, seventh)
    other = swap_core(message)

    sent = [5, 3, 1]
    kept = [6, 4, 2, 0]
    updated, next_low, *sends = call(
        functools.partial(cell_body, order, [7], n_parts),
        (
            shape(cell_factor.shape, jnp.float32),
            shape((kdim, CELL_DEV), jnp.bfloat16),
            *([wide(size, jnp.bfloat16)] if paired else []),
        ),
        0,
        6 + n_parts,
        0,
        0,
        [
            pltpu.VMEM((first_rows, CELL_DEV), jnp.bfloat16),
            pltpu.VMEM((kdim, CELL_DEV), jnp.float32),
            pltpu.VMEM((kdim, CELL_DEV), jnp.float32),
            pltpu.VMEM((kdim, CELL_DEV), jnp.float32),
            pltpu.VMEM((size, CELL_DEV), jnp.bfloat16),
        ],
    )(tile, mine_first, mine, other, cell_factor, factor_other, *others)

    if not paired:
        cell_gram = lax.psum(gram_of(next_low), "cell")
        own_cols = lax.psum_scatter(dot(next_low, tile), "cell", scatter_dimension=0, tiled=True)
        gram_part = lax.dynamic_slice_in_dim(cell_gram, lax.axis_index("cell") * size, size, 0)
        rate_gene = 1.0 / (jnp.sqrt(jnp.sum(cell_gram * cell_gram)) + 1e-06)
        stepped = jnp.dot(
            gram_part, panel.astype(jnp.float32), precision=lax.Precision.HIGHEST
        )
        return (updated, jnp.maximum(gene_factor - rate_gene * (stepped - own_cols), 0.0))

    arrived = [swap(sends[0], 1)]
    gram, *parts, keep_third, keep_second, keep_near, own = call(
        functools.partial(keep_body, sent + kept),
        (
            shape((3 * kdim // 2, kdim // 2), jnp.bfloat16),
            wide(2 * size, jnp.bfloat16),
            wide(size, jnp.bfloat16),
            *[wide(size, jnp.float32) for _ in kept],
        ),
        0,
        2,
        0,
        AHEAD,
        [pltpu.VMEM((kdim - size, CELL_DEV), jnp.bfloat16)],
    )(next_low, tile)
    arrived += [swap(part, 1) for part in parts]

    def add_up(which, keep, *parts):
        body = functools.partial(sum_body, which)
        return call(body, wide(size, jnp.bfloat16), 0, 1 + len(parts), 0, AHEAD)(keep, *parts)

    through = swap(add_up(0, keep_third, arrived[0]), 2)
    gram_arrived = swap(gram, 4)
    beside = swap(add_up(1, keep_near, arrived[1]), 2)
    across = add_up(0, keep_second, arrived[1], through)
    gram = (gram.astype(jnp.float32) + gram_arrived.astype(jnp.float32)).astype(jnp.bfloat16)
    gram_arrived = swap(gram, 2)
    gram_arrived, across = lax.optimization_barrier((gram_arrived, across))
    across = swap(across, 4)
    gram = (gram.astype(jnp.float32) + gram_arrived.astype(jnp.float32)).astype(jnp.bfloat16)
    partner = swap(gram, 1)
    gram, updated = lax.optimization_barrier((gram, updated))
    cell_next = call(copy_body, shape(cell_factor.shape, jnp.float32), 0, 1, 0, 0)(updated)
    own, cell_next = lax.optimization_barrier((own, cell_next))
    base, rate = call(
        base_body,
        (wide(size, jnp.float32), shape((8, 128), jnp.float32)),
        0,
        4,
        0,
        0,
        [pltpu.VMEM((kdim, kdim), jnp.float32)],
    )(gram, partner, panel, gene_factor)
    gene_next = call(last_body, wide(size, jnp.float32), 0, 6, 0, AHEAD)(
        rate, base, own, arrived[2], beside, across
    )
    return (cell_next, gene_next)


def solution(mesh):
    return jax.shard_map(
        shards,
        mesh=mesh,
        in_specs=(
            P(("groups", "cell"), "gene", None, None, None),
            P(("groups", "cell"), "gene", None),
            P(("groups", "cell"), "gene", None),
            P(("groups", "cell"), "gene"),
            P(("groups", "gene"), "cell"),
            P(("groups", "cell"), "gene"),
        ),
        out_specs=(P(("groups", "gene"), "cell"), P(("groups", "cell"), "gene")),
        check_vma=False,
    )
```

```python
import functools

import jax
import jax.numpy as jnp
from jax import lax
from jax.experimental import pallas as pl
from jax.experimental.pallas import tpu as pltpu
from jax.sharding import PartitionSpec as P

BLK = 128
CELL_DEV = 1024
GENE_DEV = 2048
VMEM_BYTES = 24 * 2**20
AHEAD = 16 * 2**20

NT = (((1,), (1,)), ((), ()))
NN = (((1,), (0,)), ((), ()))
SMEM_SPEC = pl.BlockSpec(memory_space=pltpu.SMEM)
VMEM_SPEC = pl.BlockSpec(memory_space=pltpu.VMEM)


def dot(a, b, dims=NN):
    return lax.dot_general(a, b, dims, preferred_element_type=jnp.float32)


def split_dot(a, b):
    high = a.astype(jnp.bfloat16)
    low = (a - high.astype(jnp.float32)).astype(jnp.bfloat16)
    rows = a.shape[0]
    both = dot(jnp.concatenate([high, low], axis=0), b)
    return both[:rows] + both[rows:]


def call(body, outs, n_smem, n_vmem, flops, traffic, scratch=()):
    return pl.pallas_call(
        body,
        out_shape=outs,
        in_specs=[SMEM_SPEC] * n_smem + [VMEM_SPEC] * n_vmem,
        out_specs=jax.tree.map(lambda _: VMEM_SPEC, outs),
        scratch_shapes=list(scratch),
        compiler_params=pltpu.CompilerParams(vmem_limit_bytes=VMEM_BYTES),
        cost_estimate=pl.CostEstimate(flops=flops, bytes_accessed=traffic, transcendentals=0),
    )


def shape(dims, dtype):
    return jax.ShapeDtypeStruct(dims, dtype)


def dense_body(rows_in, cols_in, count, values, tile, turned, rows, cols, sems, index_sems):
    copies = [
        pltpu.make_async_copy(rows_in, rows, index_sems.at[0]),
        pltpu.make_async_copy(cols_in, cols, index_sems.at[1]),
    ]
    for copy in copies:
        copy.start()
    tile[...] = jnp.zeros_like(tile)
    for copy in copies:
        copy.wait()

    def block(n):
        row = pl.multiple_of(rows[n] * BLK, BLK)
        col = pl.multiple_of(cols[n] * BLK, BLK)
        place = tile.at[pl.ds(row, BLK), pl.ds(col, BLK)]
        return pltpu.make_async_copy(values.at[n], place, sems.at[n])

    def start(n, carry):
        block(n).start()
        return carry

    def wait(n, carry):
        block(n).wait()
        return carry

    lax.fori_loop(0, count[0], start, 0)
    lax.fori_loop(0, count[0], wait, 0)
    for row in range(0, tile.shape[0], TURN):
        turned[:, row : row + TURN] = tile[row : row + TURN].T


def pinned(array):
    return pltpu.with_memory_space_constraint(array, pltpu.HBM)


def dense_tile(values, rows, cols, count):
    anywhere = pl.BlockSpec(memory_space=pltpu.HBM)
    n_blocks = values.shape[0]
    return pl.pallas_call(
        dense_body,
        out_shape=(shape((CELL_DEV, GENE_DEV), jnp.bfloat16), shape((GENE_DEV, CELL_DEV), jnp.bfloat16)),
        in_specs=[anywhere, anywhere, SMEM_SPEC, anywhere],
        out_specs=(VMEM_SPEC, VMEM_SPEC),
        scratch_shapes=[
            pltpu.SMEM((n_blocks,), jnp.int32),
            pltpu.SMEM((n_blocks,), jnp.int32),
            pltpu.SemaphoreType.DMA((n_blocks,)),
            pltpu.SemaphoreType.DMA((2,)),
        ],
        compiler_params=pltpu.CompilerParams(vmem_limit_bytes=VMEM_BYTES),
        cost_estimate=pl.CostEstimate(flops=0, bytes_accessed=0, transcendentals=0),
    )(pinned(rows), pinned(cols), count, pinned(values))


def owned(bits, size):
    return pl.ds(pl.multiple_of((lax.axis_index("cell") ^ bits) * size, size), size)


STEP = 8
TURN = 256
PARTS = 2


def coded(rows):
    above, parts = None, []
    for n in range(0, rows.shape[0], STEP):
        part = rows[n : n + STEP]
        part = (part if above is None else part - above).astype(jnp.bfloat16).astype(jnp.float32)
        above = part if above is None else above + part
        parts.append(part)
    return jnp.concatenate(parts, axis=0).astype(jnp.bfloat16)


def decoded(rows):
    rows, above, parts = rows.astype(jnp.float32), None, []
    for n in range(0, rows.shape[0], STEP):
        above = rows[n : n + STEP] if above is None else above + rows[n : n + STEP]
        parts.append(above)
    return jnp.concatenate(parts, axis=0)


def first_body(count, turned, *refs):
    shares, (panel, mine), messages = refs[: -2 - count], refs[-2 - count : -count], refs[-count:]
    row = 0
    for part in shares:
        panel[row : row + part.shape[0]] = part[...]
        row += part.shape[0]
    mine[...] = dot(panel[...], turned[...])
    row = 0
    for out in messages:
        out[...] = mine[row : row + out.shape[0]].astype(out.dtype)
        row += out.shape[0]


def second_body(order, turned, first, share, panel, mine, message):
    size = share.shape[0]
    if order is None:
        panel[: first.shape[0]] = first[...]
        panel[first.shape[0] :] = share[...]
    else:
        for n, bits in enumerate(order[:-1]):
            panel[owned(bits, size)] = first[n * size : (n + 1) * size]
        panel[owned(order[-1], size)] = share[...]
    mine[:size] = dot(share[...], turned[...])
    low = panel[...]
    gram = dot(low, low, NT)
    rows, width = mine.shape[0] - size, gram.shape[1]
    for n in range(gram.shape[0] // rows):
        mine[size:, n * width : (n + 1) * width] = gram[n * rows : (n + 1) * rows]
    message[...] = mine[...].astype(message.dtype)


def cell_body(
    order, picks, count, tile, mine_first, mine, other, factor_mine, factor_other, *refs
):
    others, (cell_next, low), sends = refs[:count], refs[count : count + 2], refs[count + 2 : -5]
    other_first, factor, data, updated, chosen = refs[-5:]
    for n, part in enumerate(others):
        other_first[n * part.shape[0] : (n + 1) * part.shape[0]] = part[...]
    share = factor_mine.shape[0]
    kdim = factor.shape[0]
    core = lax.axis_index("gene")
    own = pl.ds(pl.multiple_of(core * share, share), share)
    theirs = pl.ds(pl.multiple_of((1 - core) * share, share), share)
    factor[own] = factor_mine[...]
    factor[theirs] = factor_other[...]
    both = mine[...] + other[...].astype(jnp.float32)
    size = kdim - mine_first.shape[0]
    gram = jnp.concatenate([both[size:, n : n + kdim] for n in range(0, CELL_DEV, kdim)], axis=0)
    if order is None:
        data[:-size] = mine_first[...] + other_first[...].astype(jnp.float32)
        data[-size:] = both[:size]
    else:
        for n, bits in enumerate(order[:-1]):
            rows = slice(n * size, (n + 1) * size)
            data[owned(bits, size)] = mine_first[rows] + other_first[rows].astype(jnp.float32)
        data[owned(order[-1], size)] = both[:size]
    norm = jnp.sum(jnp.sum(gram * gram, axis=1, keepdims=True), axis=0, keepdims=True)
    rate = 1.0 / (jnp.sqrt(norm) + 1e-06)
    held = factor[...]
    stepped = split_dot(gram, held.astype(jnp.bfloat16))
    updated[...] = jnp.maximum(held - rate * (stepped - data[...]), 0.0)
    cell_next[...] = updated[own]
    low[...] = updated[...].astype(jnp.bfloat16)
    if sends:
        sends[0][...] = coded(picked_product(picks, low, tile, chosen)[0])


def gram_blocks(low, out):
    half = low.shape[0] // 2
    panel = low[...]
    gram = dot(panel, panel, NT)
    out[:half] = gram[:half, :half].astype(out.dtype)
    out[half : 2 * half] = gram[:half, half:].astype(out.dtype)
    out[2 * half :] = gram[half:, half:].astype(out.dtype)


def picked_product(picks, low, tile, chosen):
    size = chosen.shape[0] // len(picks)
    for n, bits in enumerate(picks):
        chosen[n * size : (n + 1) * size] = low[owned(bits, size)]
    product = dot(chosen[...], tile[...])
    return [product[n * size : (n + 1) * size] for n in range(len(picks))]


def keep_body(picks, low, tile, gram, send_pair, send, *rest):
    first, second, third, *kept = picked_product(picks, low, tile, rest[-1])
    size = first.shape[0]
    send_pair[:size] = coded(first)
    send_pair[size:] = coded(second)
    send[...] = coded(third)
    for out, part in zip(rest[:-1], kept):
        out[...] = part
    gram_blocks(low, gram)


def copy_body(source, out):
    out[...] = source[...]


def sum_body(which, keep, *refs):
    size = keep.shape[0]
    total = keep[...] + decoded(refs[0][which * size : (which + 1) * size])
    for part in refs[1:-1]:
        total = total + decoded(part[...])
    refs[-1][...] = coded(total)


def base_body(mine, other, panel, factor, summed, base, rate_out, gram):
    half = mine.shape[0] // 3
    quarters = mine[...].astype(jnp.float32) + other[...].astype(jnp.float32)
    upper, side, lower = quarters[:half], quarters[half : 2 * half], quarters[2 * half :]
    gram[:half, :half] = upper
    gram[:half, half:] = side
    gram[half:, :half] = side.T
    gram[half:, half:] = lower
    squares = upper * upper + 2.0 * (side * side) + lower * lower
    norm = jnp.sum(jnp.sum(squares, axis=1, keepdims=True), axis=0, keepdims=True)
    rate = 1.0 / (jnp.sqrt(norm) + 1e-06)
    base[...] = factor[...] - rate * split_dot(gram[owned(0, factor.shape[0])], panel[...])
    rate_out[...] = jnp.broadcast_to(rate, rate_out.shape)


def last_body(rate, base, own, *refs):
    total = own[...]
    for part in refs[:-1]:
        total = total + decoded(part[...])
    refs[-1][...] = jnp.maximum(base[...] + rate[0:1, 0:1] * total, 0.0)


def gram_of(panel):
    return dot(panel, panel, NT)


def shards(block_values, block_rows, block_cols, block_count, cell_factor, gene_factor):
    n_cell = lax.axis_size("cell")
    kdim = cell_factor.shape[0] * lax.axis_size("gene")
    size = gene_factor.shape[0]
    paired = n_cell == 8 and size % 16 == 0 and kdim % (2 * BLK) == 0

    def swap(value, bits):
        return lax.ppermute(value, "cell", [(n, n ^ bits) for n in range(n_cell)])

    def swap_core(value):
        return lax.ppermute(value, "gene", [(0, 1), (1, 0)])

    def wide(rows, dtype):
        return shape((rows, GENE_DEV), dtype)

    low_share = gene_factor.astype(jnp.bfloat16)
    factor_other = swap_core(cell_factor)
    tile, turned = dense_tile(block_values[0, 0], block_rows[0, 0], block_cols[0, 0], block_count[0])
    if paired:
        near = [swap(low_share, bits) for bits in (1, 2, 4)]
        sixth = swap(low_share, 6)
        beside, second, fourth, tile, turned, factor_other = lax.optimization_barrier(
            (*near, tile, turned, factor_other)
        )
        third, fifth = swap(beside, 2), swap(fourth, 1)
        seventh = swap(sixth, 1)
        shares = [low_share, beside, second, third, fourth, fifth, sixth]
        order = range(n_cell)
    else:
        whole = lax.all_gather(low_share, "cell", axis=0, tiled=True)
        shares, seventh, order = [whole[: -kdim // 8]], whole[-kdim // 8 :], None
    last_rows = seventh.shape[0]

    first_rows = kdim - last_rows
    part_rows = first_rows // PARTS if first_rows % (16 * PARTS) == 0 else first_rows
    n_parts = first_rows // part_rows
    panel_first, mine_first, *messages = call(
        functools.partial(first_body, n_parts),
        (
            wide(first_rows, jnp.bfloat16),
            shape((first_rows, CELL_DEV), jnp.float32),
            *[shape((part_rows, CELL_DEV), jnp.bfloat16) for _ in range(n_parts)],
        ),
        0,
        1 + len(shares),
        0,
        AHEAD,
    )(turned, *shares)
    others = [swap_core(part) for part in messages]
    rows = last_rows + kdim * kdim // CELL_DEV
    panel, mine, message = call(
        functools.partial(second_body, order),
        (
            wide(kdim, jnp.bfloat16),
            shape((rows, CELL_DEV), jnp.float32),
            shape((rows, CELL_DEV), jnp.bfloat16),
        ),
        0,
        3,
        0,
        0,
    )(turned, panel_first, seventh)
    other = swap_core(message)

    sent = [5, 3, 1]
    kept = [6, 4, 2, 0]
    updated, next_low, *sends = call(
        functools.partial(cell_body, order, [7], n_parts),
        (
            shape(cell_factor.shape, jnp.float32),
            shape((kdim, CELL_DEV), jnp.bfloat16),
            *([wide(size, jnp.bfloat16)] if paired else []),
        ),
        0,
        6 + n_parts,
        0,
        0,
        [
            pltpu.VMEM((first_rows, CELL_DEV), jnp.bfloat16),
            pltpu.VMEM((kdim, CELL_DEV), jnp.float32),
            pltpu.VMEM((kdim, CELL_DEV), jnp.float32),
            pltpu.VMEM((kdim, CELL_DEV), jnp.float32),
            pltpu.VMEM((size, CELL_DEV), jnp.bfloat16),
        ],
    )(tile, mine_first, mine, other, cell_factor, factor_other, *others)

    if not paired:
        cell_gram = lax.psum(gram_of(next_low), "cell")
        own_cols = lax.psum_scatter(dot(next_low, tile), "cell", scatter_dimension=0, tiled=True)
        gram_part = lax.dynamic_slice_in_dim(cell_gram, lax.axis_index("cell") * size, size, 0)
        rate_gene = 1.0 / (jnp.sqrt(jnp.sum(cell_gram * cell_gram)) + 1e-06)
        stepped = jnp.dot(
            gram_part, panel.astype(jnp.float32), precision=lax.Precision.HIGHEST
        )
        return (updated, jnp.maximum(gene_factor - rate_gene * (stepped - own_cols), 0.0))

    arrived = [swap(sends[0], 1)]
    gram, *parts, keep_third, keep_second, keep_near, own = call(
        functools.partial(keep_body, sent + kept),
        (
            shape((3 * kdim // 2, kdim // 2), jnp.bfloat16),
            wide(2 * size, jnp.bfloat16),
            wide(size, jnp.bfloat16),
            *[wide(size, jnp.float32) for _ in kept],
        ),
        0,
        2,
        0,
        AHEAD,
        [pltpu.VMEM((kdim - size, CELL_DEV), jnp.bfloat16)],
    )(next_low, tile)
    arrived += [swap(part, 1) for part in parts]

    def add_up(which, keep, *parts):
        body = functools.partial(sum_body, which)
        return call(body, wide(size, jnp.bfloat16), 0, 1 + len(parts), 0, AHEAD)(keep, *parts)

    through = swap(add_up(0, keep_third, arrived[0]), 2)
    gram_arrived = swap(gram, 4)
    beside = swap(add_up(1, keep_near, arrived[1]), 2)
    across = add_up(0, keep_second, arrived[1], through)
    gram = (gram.astype(jnp.float32) + gram_arrived.astype(jnp.float32)).astype(jnp.bfloat16)
    gram_arrived = swap(gram, 2)
    gram_arrived, summed = lax.optimization_barrier((gram_arrived, across))
    across = swap(across, 4)
    gram = (gram.astype(jnp.float32) + gram_arrived.astype(jnp.float32)).astype(jnp.bfloat16)
    partner = swap(gram, 1)
    gram, updated = lax.optimization_barrier((gram, updated))
    cell_next = call(copy_body, shape(cell_factor.shape, jnp.float32), 0, 1, 0, 0)(updated)
    own, cell_next = lax.optimization_barrier((own, cell_next))
    base, rate = call(
        base_body,
        (wide(size, jnp.float32), shape((8, 128), jnp.float32)),
        0,
        5,
        0,
        0,
        [pltpu.VMEM((kdim, kdim), jnp.float32)],
    )(gram, partner, panel, gene_factor, summed)
    gene_next = call(last_body, wide(size, jnp.float32), 0, 6, 0, AHEAD)(
        rate, base, own, arrived[2], beside, across
    )
    return (cell_next, gene_next)


def solution(mesh):
    return jax.shard_map(
        shards,
        mesh=mesh,
        in_specs=(
            P(("groups", "cell"), "gene", None, None, None),
            P(("groups", "cell"), "gene", None),
            P(("groups", "cell"), "gene", None),
            P(("groups", "cell"), "gene"),
            P(("groups", "gene"), "cell"),
            P(("groups", "cell"), "gene"),
        ),
        out_specs=(P(("groups", "gene"), "cell"), P(("groups", "cell"), "gene")),
        check_vma=False,
    )
```

```python
import functools

import jax
import jax.numpy as jnp
from jax import lax
from jax.experimental import pallas as pl
from jax.experimental.pallas import tpu as pltpu
from jax.sharding import PartitionSpec as P

BLK = 128
CELL_DEV = 1024
GENE_DEV = 2048
VMEM_BYTES = 24 * 2**20
AHEAD = 16 * 2**20

NT = (((1,), (1,)), ((), ()))
NN = (((1,), (0,)), ((), ()))
SMEM_SPEC = pl.BlockSpec(memory_space=pltpu.SMEM)
VMEM_SPEC = pl.BlockSpec(memory_space=pltpu.VMEM)


def dot(a, b, dims=NN):
    return lax.dot_general(a, b, dims, preferred_element_type=jnp.float32)


def split_dot(a, b):
    high = a.astype(jnp.bfloat16)
    low = (a - high.astype(jnp.float32)).astype(jnp.bfloat16)
    rows = a.shape[0]
    both = dot(jnp.concatenate([high, low], axis=0), b)
    return both[:rows] + both[rows:]


def call(body, outs, n_smem, n_vmem, flops, traffic, scratch=()):
    return pl.pallas_call(
        body,
        out_shape=outs,
        in_specs=[SMEM_SPEC] * n_smem + [VMEM_SPEC] * n_vmem,
        out_specs=jax.tree.map(lambda _: VMEM_SPEC, outs),
        scratch_shapes=list(scratch),
        compiler_params=pltpu.CompilerParams(vmem_limit_bytes=VMEM_BYTES),
        cost_estimate=pl.CostEstimate(flops=flops, bytes_accessed=traffic, transcendentals=0),
    )


def shape(dims, dtype):
    return jax.ShapeDtypeStruct(dims, dtype)


def dense_body(rows_in, cols_in, count, values, tile, turned, rows, cols, sems, index_sems):
    copies = [
        pltpu.make_async_copy(rows_in, rows, index_sems.at[0]),
        pltpu.make_async_copy(cols_in, cols, index_sems.at[1]),
    ]
    for copy in copies:
        copy.start()
    tile[...] = jnp.zeros_like(tile)
    for copy in copies:
        copy.wait()

    def block(n):
        row = pl.multiple_of(rows[n] * BLK, BLK)
        col = pl.multiple_of(cols[n] * BLK, BLK)
        place = tile.at[pl.ds(row, BLK), pl.ds(col, BLK)]
        return pltpu.make_async_copy(values.at[n], place, sems.at[n])

    def start(n, carry):
        block(n).start()
        return carry

    def wait(n, carry):
        block(n).wait()
        return carry

    lax.fori_loop(0, count[0], start, 0)
    lax.fori_loop(0, count[0], wait, 0)
    for row in range(0, tile.shape[0], TURN):
        turned[:, row : row + TURN] = tile[row : row + TURN].T


def pinned(array):
    return pltpu.with_memory_space_constraint(array, pltpu.HBM)


def dense_tile(values, rows, cols, count):
    anywhere = pl.BlockSpec(memory_space=pltpu.HBM)
    n_blocks = values.shape[0]
    return pl.pallas_call(
        dense_body,
        out_shape=(shape((CELL_DEV, GENE_DEV), jnp.bfloat16), shape((GENE_DEV, CELL_DEV), jnp.bfloat16)),
        in_specs=[anywhere, anywhere, SMEM_SPEC, anywhere],
        out_specs=(VMEM_SPEC, VMEM_SPEC),
        scratch_shapes=[
            pltpu.SMEM((n_blocks,), jnp.int32),
            pltpu.SMEM((n_blocks,), jnp.int32),
            pltpu.SemaphoreType.DMA((n_blocks,)),
            pltpu.SemaphoreType.DMA((2,)),
        ],
        compiler_params=pltpu.CompilerParams(vmem_limit_bytes=VMEM_BYTES),
        cost_estimate=pl.CostEstimate(flops=0, bytes_accessed=0, transcendentals=0),
    )(pinned(rows), pinned(cols), count, pinned(values))


def owned(bits, size):
    return pl.ds(pl.multiple_of((lax.axis_index("cell") ^ bits) * size, size), size)


STEP = 8
TURN = 256
PARTS = 2


def coded(rows):
    above, parts = None, []
    for n in range(0, rows.shape[0], STEP):
        part = rows[n : n + STEP]
        part = (part if above is None else part - above).astype(jnp.bfloat16).astype(jnp.float32)
        above = part if above is None else above + part
        parts.append(part)
    return jnp.concatenate(parts, axis=0).astype(jnp.bfloat16)


def decoded(rows):
    rows, above, parts = rows.astype(jnp.float32), None, []
    for n in range(0, rows.shape[0], STEP):
        above = rows[n : n + STEP] if above is None else above + rows[n : n + STEP]
        parts.append(above)
    return jnp.concatenate(parts, axis=0)


def first_body(count, turned, *refs):
    shares, (panel, mine), messages = refs[: -2 - count], refs[-2 - count : -count], refs[-count:]
    row = 0
    for part in shares:
        panel[row : row + part.shape[0]] = part[...]
        row += part.shape[0]
    mine[...] = dot(panel[...], turned[...])
    row = 0
    for out in messages:
        out[...] = mine[row : row + out.shape[0]].astype(out.dtype)
        row += out.shape[0]


def second_body(order, turned, first, share, panel, mine, message):
    size = share.shape[0]
    if order is None:
        panel[: first.shape[0]] = first[...]
        panel[first.shape[0] :] = share[...]
    else:
        for n, bits in enumerate(order[:-1]):
            panel[owned(bits, size)] = first[n * size : (n + 1) * size]
        panel[owned(order[-1], size)] = share[...]
    mine[:size] = dot(share[...], turned[...])
    low = panel[...]
    gram = dot(low, low, NT)
    rows, width = mine.shape[0] - size, gram.shape[1]
    for n in range(gram.shape[0] // rows):
        mine[size:, n * width : (n + 1) * width] = gram[n * rows : (n + 1) * rows]
    message[...] = mine[...].astype(message.dtype)


def cell_body(
    order, picks, count, tile, mine_first, mine, other, factor_mine, factor_other, *refs
):
    others, (cell_next, low), sends = refs[:count], refs[count : count + 2], refs[count + 2 : -5]
    other_first, factor, data, updated, chosen = refs[-5:]
    for n, part in enumerate(others):
        other_first[n * part.shape[0] : (n + 1) * part.shape[0]] = part[...]
    share = factor_mine.shape[0]
    kdim = factor.shape[0]
    core = lax.axis_index("gene")
    own = pl.ds(pl.multiple_of(core * share, share), share)
    theirs = pl.ds(pl.multiple_of((1 - core) * share, share), share)
    factor[own] = factor_mine[...]
    factor[theirs] = factor_other[...]
    both = mine[...] + other[...].astype(jnp.float32)
    size = kdim - mine_first.shape[0]
    gram = jnp.concatenate([both[size:, n : n + kdim] for n in range(0, CELL_DEV, kdim)], axis=0)
    if order is None:
        data[:-size] = mine_first[...] + other_first[...].astype(jnp.float32)
        data[-size:] = both[:size]
    else:
        for n, bits in enumerate(order[:-1]):
            rows = slice(n * size, (n + 1) * size)
            data[owned(bits, size)] = mine_first[rows] + other_first[rows].astype(jnp.float32)
        data[owned(order[-1], size)] = both[:size]
    norm = jnp.sum(jnp.sum(gram * gram, axis=1, keepdims=True), axis=0, keepdims=True)
    rate = 1.0 / (jnp.sqrt(norm) + 1e-06)
    held = factor[...]
    stepped = split_dot(gram, held.astype(jnp.bfloat16))
    updated[...] = jnp.maximum(held - rate * (stepped - data[...]), 0.0)
    cell_next[...] = updated[own]
    low[...] = updated[...].astype(jnp.bfloat16)
    if sends:
        send, gram_out = sends
        send[...] = coded(picked_product(picks, low, tile, chosen)[0])
        gram_blocks(low, gram_out)


def gram_blocks(low, out):
    half = low.shape[0] // 2
    panel = low[...]
    gram = dot(panel, panel, NT)
    out[:half] = gram[:half, :half].astype(out.dtype)
    out[half : 2 * half] = gram[:half, half:].astype(out.dtype)
    out[2 * half :] = gram[half:, half:].astype(out.dtype)


def picked_product(picks, low, tile, chosen):
    size = chosen.shape[0] // len(picks)
    for n, bits in enumerate(picks):
        chosen[n * size : (n + 1) * size] = low[owned(bits, size)]
    product = dot(chosen[...], tile[...])
    return [product[n * size : (n + 1) * size] for n in range(len(picks))]


def keep_body(picks, low, tile, send_pair, send, *rest):
    first, second, third, *kept = picked_product(picks, low, tile, rest[-1])
    size = first.shape[0]
    send_pair[:size] = coded(first)
    send_pair[size:] = coded(second)
    send[...] = coded(third)
    for out, part in zip(rest[:-1], kept):
        out[...] = part


def copy_body(source, out):
    out[...] = source[...]


def sum_body(which, keep, *refs):
    size = keep.shape[0]
    total = keep[...] + decoded(refs[0][which * size : (which + 1) * size])
    for part in refs[1:-1]:
        total = total + decoded(part[...])
    refs[-1][...] = coded(total)


def base_body(mine, other, panel, factor, summed, base, rate_out, gram):
    half = mine.shape[0] // 3
    quarters = mine[...].astype(jnp.float32) + other[...].astype(jnp.float32)
    upper, side, lower = quarters[:half], quarters[half : 2 * half], quarters[2 * half :]
    gram[:half, :half] = upper
    gram[:half, half:] = side
    gram[half:, :half] = side.T
    gram[half:, half:] = lower
    squares = upper * upper + 2.0 * (side * side) + lower * lower
    norm = jnp.sum(jnp.sum(squares, axis=1, keepdims=True), axis=0, keepdims=True)
    rate = 1.0 / (jnp.sqrt(norm) + 1e-06)
    base[...] = factor[...] - rate * split_dot(gram[owned(0, factor.shape[0])], panel[...])
    rate_out[...] = jnp.broadcast_to(rate, rate_out.shape)


def last_body(rate, base, own, *refs):
    total = own[...]
    for part in refs[:-1]:
        total = total + decoded(part[...])
    refs[-1][...] = jnp.maximum(base[...] + rate[0:1, 0:1] * total, 0.0)


def gram_of(panel):
    return dot(panel, panel, NT)


def shards(block_values, block_rows, block_cols, block_count, cell_factor, gene_factor):
    n_cell = lax.axis_size("cell")
    kdim = cell_factor.shape[0] * lax.axis_size("gene")
    size = gene_factor.shape[0]
    paired = n_cell == 8 and size % 16 == 0 and kdim % (2 * BLK) == 0

    def swap(value, bits):
        return lax.ppermute(value, "cell", [(n, n ^ bits) for n in range(n_cell)])

    def swap_core(value):
        return lax.ppermute(value, "gene", [(0, 1), (1, 0)])

    def wide(rows, dtype):
        return shape((rows, GENE_DEV), dtype)

    low_share = gene_factor.astype(jnp.bfloat16)
    factor_other = swap_core(cell_factor)
    tile, turned = dense_tile(block_values[0, 0], block_rows[0, 0], block_cols[0, 0], block_count[0])
    if paired:
        near = [swap(low_share, bits) for bits in (1, 2, 4)]
        sixth = swap(low_share, 6)
        beside, second, fourth, tile, turned, factor_other = lax.optimization_barrier(
            (*near, tile, turned, factor_other)
        )
        third, fifth = swap(beside, 2), swap(fourth, 1)
        seventh = swap(sixth, 1)
        shares = [low_share, beside, second, third, fourth, fifth, sixth]
        order = range(n_cell)
    else:
        whole = lax.all_gather(low_share, "cell", axis=0, tiled=True)
        shares, seventh, order = [whole[: -kdim // 8]], whole[-kdim // 8 :], None
    last_rows = seventh.shape[0]

    first_rows = kdim - last_rows
    part_rows = first_rows // PARTS if first_rows % (16 * PARTS) == 0 else first_rows
    n_parts = first_rows // part_rows
    panel_first, mine_first, *messages = call(
        functools.partial(first_body, n_parts),
        (
            wide(first_rows, jnp.bfloat16),
            shape((first_rows, CELL_DEV), jnp.float32),
            *[shape((part_rows, CELL_DEV), jnp.bfloat16) for _ in range(n_parts)],
        ),
        0,
        1 + len(shares),
        0,
        AHEAD,
    )(turned, *shares)
    others = [swap_core(part) for part in messages]
    rows = last_rows + kdim * kdim // CELL_DEV
    panel, mine, message = call(
        functools.partial(second_body, order),
        (
            wide(kdim, jnp.bfloat16),
            shape((rows, CELL_DEV), jnp.float32),
            shape((rows, CELL_DEV), jnp.bfloat16),
        ),
        0,
        3,
        0,
        0,
    )(turned, panel_first, seventh)
    other = swap_core(message)

    sent = [5, 3, 1]
    kept = [6, 4, 2, 0]
    updated, next_low, *sends = call(
        functools.partial(cell_body, order, [7], n_parts),
        (
            shape(cell_factor.shape, jnp.float32),
            shape((kdim, CELL_DEV), jnp.bfloat16),
            *([wide(size, jnp.bfloat16), shape((3 * kdim // 2, kdim // 2), jnp.bfloat16)] if paired else []),
        ),
        0,
        6 + n_parts,
        0,
        0,
        [
            pltpu.VMEM((first_rows, CELL_DEV), jnp.bfloat16),
            pltpu.VMEM((kdim, CELL_DEV), jnp.float32),
            pltpu.VMEM((kdim, CELL_DEV), jnp.float32),
            pltpu.VMEM((kdim, CELL_DEV), jnp.float32),
            pltpu.VMEM((size, CELL_DEV), jnp.bfloat16),
        ],
    )(tile, mine_first, mine, other, cell_factor, factor_other, *others)

    if not paired:
        cell_gram = lax.psum(gram_of(next_low), "cell")
        own_cols = lax.psum_scatter(dot(next_low, tile), "cell", scatter_dimension=0, tiled=True)
        gram_part = lax.dynamic_slice_in_dim(cell_gram, lax.axis_index("cell") * size, size, 0)
        rate_gene = 1.0 / (jnp.sqrt(jnp.sum(cell_gram * cell_gram)) + 1e-06)
        stepped = jnp.dot(
            gram_part, panel.astype(jnp.float32), precision=lax.Precision.HIGHEST
        )
        return (updated, jnp.maximum(gene_factor - rate_gene * (stepped - own_cols), 0.0))

    arrived = [swap(sends[0], 1)]
    *parts, keep_third, keep_second, keep_near, own = call(
        functools.partial(keep_body, sent + kept),
        (
            wide(2 * size, jnp.bfloat16),
            wide(size, jnp.bfloat16),
            *[wide(size, jnp.float32) for _ in kept],
        ),
        0,
        2,
        0,
        AHEAD,
        [pltpu.VMEM((kdim - size, CELL_DEV), jnp.bfloat16)],
    )(next_low, tile)
    gram = sends[1]
    arrived += [swap(part, 1) for part in parts]

    def add_up(which, keep, *parts):
        body = functools.partial(sum_body, which)
        return call(body, wide(size, jnp.bfloat16), 0, 1 + len(parts), 0, AHEAD)(keep, *parts)

    through = swap(add_up(0, keep_third, arrived[0]), 2)
    gram_arrived = swap(gram, 4)
    beside = swap(add_up(1, keep_near, arrived[1]), 2)
    across = add_up(0, keep_second, arrived[1], through)
    gram = (gram.astype(jnp.float32) + gram_arrived.astype(jnp.float32)).astype(jnp.bfloat16)
    gram_arrived = swap(gram, 2)
    gram_arrived, summed = lax.optimization_barrier((gram_arrived, across))
    across = swap(across, 4)
    gram = (gram.astype(jnp.float32) + gram_arrived.astype(jnp.float32)).astype(jnp.bfloat16)
    partner = swap(gram, 1)
    gram, updated = lax.optimization_barrier((gram, updated))
    cell_next = call(copy_body, shape(cell_factor.shape, jnp.float32), 0, 1, 0, 0)(updated)
    own, cell_next = lax.optimization_barrier((own, cell_next))
    base, rate = call(
        base_body,
        (wide(size, jnp.float32), shape((8, 128), jnp.float32)),
        0,
        5,
        0,
        0,
        [pltpu.VMEM((kdim, kdim), jnp.float32)],
    )(gram, partner, panel, gene_factor, summed)
    gene_next = call(last_body, wide(size, jnp.float32), 0, 6, 0, AHEAD)(
        rate, base, own, arrived[2], beside, across
    )
    return (cell_next, gene_next)


def solution(mesh):
    return jax.shard_map(
        shards,
        mesh=mesh,
        in_specs=(
            P(("groups", "cell"), "gene", None, None, None),
            P(("groups", "cell"), "gene", None),
            P(("groups", "cell"), "gene", None),
            P(("groups", "cell"), "gene"),
            P(("groups", "gene"), "cell"),
            P(("groups", "cell"), "gene"),
        ),
        out_specs=(P(("groups", "gene"), "cell"), P(("groups", "cell"), "gene")),
        check_vma=False,
    )
```

```python
import functools

import jax
import jax.numpy as jnp
from jax import lax
from jax.experimental import pallas as pl
from jax.experimental.pallas import tpu as pltpu
from jax.sharding import PartitionSpec as P

BLK = 128
CELL_DEV = 1024
GENE_DEV = 2048
VMEM_BYTES = 24 * 2**20
AHEAD = 16 * 2**20

NT = (((1,), (1,)), ((), ()))
NN = (((1,), (0,)), ((), ()))
SMEM_SPEC = pl.BlockSpec(memory_space=pltpu.SMEM)
VMEM_SPEC = pl.BlockSpec(memory_space=pltpu.VMEM)


def dot(a, b, dims=NN):
    return lax.dot_general(a, b, dims, preferred_element_type=jnp.float32)


def split_dot(a, b):
    high = a.astype(jnp.bfloat16)
    low = (a - high.astype(jnp.float32)).astype(jnp.bfloat16)
    rows = a.shape[0]
    both = dot(jnp.concatenate([high, low], axis=0), b)
    return both[:rows] + both[rows:]


def call(body, outs, n_smem, n_vmem, flops, traffic, scratch=()):
    return pl.pallas_call(
        body,
        out_shape=outs,
        in_specs=[SMEM_SPEC] * n_smem + [VMEM_SPEC] * n_vmem,
        out_specs=jax.tree.map(lambda _: VMEM_SPEC, outs),
        scratch_shapes=list(scratch),
        compiler_params=pltpu.CompilerParams(vmem_limit_bytes=VMEM_BYTES),
        cost_estimate=pl.CostEstimate(flops=flops, bytes_accessed=traffic, transcendentals=0),
    )


def shape(dims, dtype):
    return jax.ShapeDtypeStruct(dims, dtype)


def dense_body(rows_in, cols_in, count, values, tile, turned, rows, cols, sems, index_sems):
    copies = [
        pltpu.make_async_copy(rows_in, rows, index_sems.at[0]),
        pltpu.make_async_copy(cols_in, cols, index_sems.at[1]),
    ]
    for copy in copies:
        copy.start()
    tile[...] = jnp.zeros_like(tile)
    for copy in copies:
        copy.wait()

    def block(n):
        row = pl.multiple_of(rows[n] * BLK, BLK)
        col = pl.multiple_of(cols[n] * BLK, BLK)
        place = tile.at[pl.ds(row, BLK), pl.ds(col, BLK)]
        return pltpu.make_async_copy(values.at[n], place, sems.at[n])

    def start(n, carry):
        block(n).start()
        return carry

    def wait(n, carry):
        block(n).wait()
        return carry

    lax.fori_loop(0, count[0], start, 0)
    lax.fori_loop(0, count[0], wait, 0)
    for row in range(0, tile.shape[0], TURN):
        turned[:, row : row + TURN] = tile[row : row + TURN].T


def pinned(array):
    return pltpu.with_memory_space_constraint(array, pltpu.HBM)


def dense_tile(values, rows, cols, count):
    anywhere = pl.BlockSpec(memory_space=pltpu.HBM)
    n_blocks = values.shape[0]
    return pl.pallas_call(
        dense_body,
        out_shape=(shape((CELL_DEV, GENE_DEV), jnp.bfloat16), shape((GENE_DEV, CELL_DEV), jnp.bfloat16)),
        in_specs=[anywhere, anywhere, SMEM_SPEC, anywhere],
        out_specs=(VMEM_SPEC, VMEM_SPEC),
        scratch_shapes=[
            pltpu.SMEM((n_blocks,), jnp.int32),
            pltpu.SMEM((n_blocks,), jnp.int32),
            pltpu.SemaphoreType.DMA((n_blocks,)),
            pltpu.SemaphoreType.DMA((2,)),
        ],
        compiler_params=pltpu.CompilerParams(vmem_limit_bytes=VMEM_BYTES),
        cost_estimate=pl.CostEstimate(flops=0, bytes_accessed=0, transcendentals=0),
    )(pinned(rows), pinned(cols), count, pinned(values))


def owned(bits, size):
    return pl.ds(pl.multiple_of((lax.axis_index("cell") ^ bits) * size, size), size)


STEP = 8
TURN = 256
PARTS = 2


def coded(rows):
    above, parts = None, []
    for n in range(0, rows.shape[0], STEP):
        part = rows[n : n + STEP]
        part = (part if above is None else part - above).astype(jnp.bfloat16).astype(jnp.float32)
        above = part if above is None else above + part
        parts.append(part)
    return jnp.concatenate(parts, axis=0).astype(jnp.bfloat16)


def decoded(rows):
    rows, above, parts = rows.astype(jnp.float32), None, []
    for n in range(0, rows.shape[0], STEP):
        above = rows[n : n + STEP] if above is None else above + rows[n : n + STEP]
        parts.append(above)
    return jnp.concatenate(parts, axis=0)


def first_body(count, turned, *refs):
    shares, (panel, mine), messages = refs[: -2 - count], refs[-2 - count : -count], refs[-count:]
    row = 0
    for part in shares:
        panel[row : row + part.shape[0]] = part[...]
        row += part.shape[0]
    mine[...] = dot(panel[...], turned[...])
    row = 0
    for out in messages:
        out[...] = mine[row : row + out.shape[0]].astype(out.dtype)
        row += out.shape[0]


def second_body(order, turned, first, share, panel, mine, message):
    size = share.shape[0]
    if order is None:
        panel[: first.shape[0]] = first[...]
        panel[first.shape[0] :] = share[...]
    else:
        for n, bits in enumerate(order[:-1]):
            panel[owned(bits, size)] = first[n * size : (n + 1) * size]
        panel[owned(order[-1], size)] = share[...]
    mine[:size] = dot(share[...], turned[...])
    low = panel[...]
    gram = dot(low, low, NT)
    rows, width = mine.shape[0] - size, gram.shape[1]
    for n in range(gram.shape[0] // rows):
        mine[size:, n * width : (n + 1) * width] = gram[n * rows : (n + 1) * rows]
    message[...] = mine[...].astype(message.dtype)


def cell_body(
    order, picks, count, tile, mine_first, mine, other, factor_mine, factor_other, *refs
):
    others, (cell_next, low), sends = refs[:count], refs[count : count + 2], refs[count + 2 : -5]
    other_first, factor, data, updated, chosen = refs[-5:]
    for n, part in enumerate(others):
        other_first[n * part.shape[0] : (n + 1) * part.shape[0]] = part[...]
    share = factor_mine.shape[0]
    kdim = factor.shape[0]
    core = lax.axis_index("gene")
    own = pl.ds(pl.multiple_of(core * share, share), share)
    theirs = pl.ds(pl.multiple_of((1 - core) * share, share), share)
    factor[own] = factor_mine[...]
    factor[theirs] = factor_other[...]
    both = mine[...] + other[...].astype(jnp.float32)
    size = kdim - mine_first.shape[0]
    gram = jnp.concatenate([both[size:, n : n + kdim] for n in range(0, CELL_DEV, kdim)], axis=0)
    if order is None:
        data[:-size] = mine_first[...] + other_first[...].astype(jnp.float32)
        data[-size:] = both[:size]
    else:
        for n, bits in enumerate(order[:-1]):
            rows = slice(n * size, (n + 1) * size)
            data[owned(bits, size)] = mine_first[rows] + other_first[rows].astype(jnp.float32)
        data[owned(order[-1], size)] = both[:size]
    norm = jnp.sum(jnp.sum(gram * gram, axis=1, keepdims=True), axis=0, keepdims=True)
    rate = 1.0 / (jnp.sqrt(norm) + 1e-06)
    held = factor[...]
    stepped = split_dot(gram, held.astype(jnp.bfloat16))
    updated[...] = jnp.maximum(held - rate * (stepped - data[...]), 0.0)
    cell_next[...] = updated[own]
    low[...] = updated[...].astype(jnp.bfloat16)
    if sends:
        sends[0][...] = coded(picked_product(picks, low, tile, chosen)[0])


def gram_blocks(low, out):
    half = low.shape[0] // 2
    panel = low[...]
    gram = dot(panel, panel, NT)
    out[:half] = gram[:half, :half].astype(out.dtype)
    out[half : 2 * half] = gram[:half, half:].astype(out.dtype)
    out[2 * half :] = gram[half:, half:].astype(out.dtype)


def picked_product(picks, low, tile, chosen):
    size = chosen.shape[0] // len(picks)
    for n, bits in enumerate(picks):
        chosen[n * size : (n + 1) * size] = low[owned(bits, size)]
    product = dot(chosen[...], tile[...])
    return [product[n * size : (n + 1) * size] for n in range(len(picks))]


def keep_body(picks, low, tile, gram, send_pair, send, *rest):
    first, second, third, *kept = picked_product(picks, low, tile, rest[-1])
    size = first.shape[0]
    send_pair[:size] = coded(first)
    send_pair[size:] = coded(second)
    send[...] = coded(third)
    for out, part in zip(rest[:-1], kept):
        out[...] = part
    gram_blocks(low, gram)


def copy_body(source, out):
    out[...] = source[...]


def sum_body(which, keep, *refs):
    size = keep.shape[0]
    total = keep[...] + decoded(refs[0][which * size : (which + 1) * size])
    for part in refs[1:-1]:
        total = total + decoded(part[...])
    refs[-1][...] = coded(total)


def base_body(mine, other, panel, factor, base, rate_out, gram):
    half = mine.shape[0] // 3
    quarters = mine[...].astype(jnp.float32) + other[...].astype(jnp.float32)
    upper, side, lower = quarters[:half], quarters[half : 2 * half], quarters[2 * half :]
    gram[:half, :half] = upper
    gram[:half, half:] = side
    gram[half:, :half] = side.T
    gram[half:, half:] = lower
    squares = upper * upper + 2.0 * (side * side) + lower * lower
    norm = jnp.sum(jnp.sum(squares, axis=1, keepdims=True), axis=0, keepdims=True)
    rate = 1.0 / (jnp.sqrt(norm) + 1e-06)
    base[...] = factor[...] - rate * split_dot(gram[owned(0, factor.shape[0])], panel[...])
    rate_out[...] = jnp.broadcast_to(rate, rate_out.shape)


def last_body(rate, base, own, *refs):
    total = own[...]
    for part in refs[:-1]:
        total = total + decoded(part[...])
    refs[-1][...] = jnp.maximum(base[...] + rate[0:1, 0:1] * total, 0.0)


def gram_of(panel):
    return dot(panel, panel, NT)


def shards(block_values, block_rows, block_cols, block_count, cell_factor, gene_factor):
    n_cell = lax.axis_size("cell")
    kdim = cell_factor.shape[0] * lax.axis_size("gene")
    size = gene_factor.shape[0]
    paired = n_cell == 8 and size % 16 == 0 and kdim % (2 * BLK) == 0

    def swap(value, bits):
        return lax.ppermute(value, "cell", [(n, n ^ bits) for n in range(n_cell)])

    def swap_core(value):
        return lax.ppermute(value, "gene", [(0, 1), (1, 0)])

    def wide(rows, dtype):
        return shape((rows, GENE_DEV), dtype)

    low_share = gene_factor.astype(jnp.bfloat16)
    factor_other = swap_core(cell_factor)
    tile, turned = dense_tile(block_values[0, 0], block_rows[0, 0], block_cols[0, 0], block_count[0])
    if paired:
        near = [swap(low_share, bits) for bits in (1, 2, 4)]
        sixth = swap(low_share, 6)
        beside, second, fourth, tile, turned, factor_other = lax.optimization_barrier(
            (*near, tile, turned, factor_other)
        )
        third, fifth = swap(beside, 2), swap(fourth, 1)
        seventh = swap(sixth, 1)
        shares = [low_share, beside, second, third, fourth, fifth, sixth]
        order = range(n_cell)
    else:
        whole = lax.all_gather(low_share, "cell", axis=0, tiled=True)
        shares, seventh, order = [whole[: -kdim // 8]], whole[-kdim // 8 :], None
    last_rows = seventh.shape[0]

    first_rows = kdim - last_rows
    part_rows = first_rows // PARTS if first_rows % (16 * PARTS) == 0 else first_rows
    n_parts = first_rows // part_rows
    panel_first, mine_first, *messages = call(
        functools.partial(first_body, n_parts),
        (
            wide(first_rows, jnp.bfloat16),
            shape((first_rows, CELL_DEV), jnp.float32),
            *[shape((part_rows, CELL_DEV), jnp.bfloat16) for _ in range(n_parts)],
        ),
        0,
        1 + len(shares),
        0,
        AHEAD,
    )(turned, *shares)
    others = [swap_core(part) for part in messages]
    rows = last_rows + kdim * kdim // CELL_DEV
    panel, mine, message = call(
        functools.partial(second_body, order),
        (
            wide(kdim, jnp.bfloat16),
            shape((rows, CELL_DEV), jnp.float32),
            shape((rows, CELL_DEV), jnp.bfloat16),
        ),
        0,
        3,
        0,
        0,
    )(turned, panel_first, seventh)
    other = swap_core(message)

    sent = [5, 3, 1]
    kept = [6, 4, 2, 0]
    updated, next_low, *sends = call(
        functools.partial(cell_body, order, [7], n_parts),
        (
            shape(cell_factor.shape, jnp.float32),
            shape((kdim, CELL_DEV), jnp.bfloat16),
            *([wide(size, jnp.bfloat16)] if paired else []),
        ),
        0,
        6 + n_parts,
        0,
        0,
        [
            pltpu.VMEM((first_rows, CELL_DEV), jnp.bfloat16),
            pltpu.VMEM((kdim, CELL_DEV), jnp.float32),
            pltpu.VMEM((kdim, CELL_DEV), jnp.float32),
            pltpu.VMEM((kdim, CELL_DEV), jnp.float32),
            pltpu.VMEM((size, CELL_DEV), jnp.bfloat16),
        ],
    )(tile, mine_first, mine, other, cell_factor, factor_other, *others)

    if not paired:
        cell_gram = lax.psum(gram_of(next_low), "cell")
        own_cols = lax.psum_scatter(dot(next_low, tile), "cell", scatter_dimension=0, tiled=True)
        gram_part = lax.dynamic_slice_in_dim(cell_gram, lax.axis_index("cell") * size, size, 0)
        rate_gene = 1.0 / (jnp.sqrt(jnp.sum(cell_gram * cell_gram)) + 1e-06)
        stepped = jnp.dot(
            gram_part, panel.astype(jnp.float32), precision=lax.Precision.HIGHEST
        )
        return (updated, jnp.maximum(gene_factor - rate_gene * (stepped - own_cols), 0.0))

    arrived = [swap(sends[0], 1)]
    gram, *parts, keep_third, keep_second, keep_near, own = call(
        functools.partial(keep_body, sent + kept),
        (
            shape((3 * kdim // 2, kdim // 2), jnp.bfloat16),
            wide(2 * size, jnp.bfloat16),
            wide(size, jnp.bfloat16),
            *[wide(size, jnp.float32) for _ in kept],
        ),
        0,
        2,
        0,
        AHEAD,
        [pltpu.VMEM((kdim - size, CELL_DEV), jnp.bfloat16)],
    )(next_low, tile)
    arrived += [swap(part, 1) for part in parts]

    def add_up(which, keep, *parts):
        body = functools.partial(sum_body, which)
        return call(body, wide(size, jnp.bfloat16), 0, 1 + len(parts), 0, AHEAD)(keep, *parts)

    through = swap(add_up(0, keep_third, arrived[0]), 2)
    gram_arrived = swap(gram, 4)
    beside = swap(add_up(1, keep_near, arrived[1]), 2)
    across = add_up(0, keep_second, arrived[1], through)
    gram = (gram.astype(jnp.float32) + gram_arrived.astype(jnp.float32)).astype(jnp.bfloat16)
    gram_arrived = swap(gram, 2)
    across = swap(across, 4)
    gram = (gram.astype(jnp.float32) + gram_arrived.astype(jnp.float32)).astype(jnp.bfloat16)
    partner = swap(gram, 1)
    gram, updated = lax.optimization_barrier((gram, updated))
    cell_next = call(copy_body, shape(cell_factor.shape, jnp.float32), 0, 1, 0, 0)(updated)
    own, cell_next = lax.optimization_barrier((own, cell_next))
    base, rate = call(
        base_body,
        (wide(size, jnp.float32), shape((8, 128), jnp.float32)),
        0,
        4,
        0,
        0,
        [pltpu.VMEM((kdim, kdim), jnp.float32)],
    )(gram, partner, panel, gene_factor)
    gene_next = call(last_body, wide(size, jnp.float32), 0, 6, 0, AHEAD)(
        rate, base, own, arrived[2], beside, across
    )
    return (cell_next, gene_next)


def solution(mesh):
    return jax.shard_map(
        shards,
        mesh=mesh,
        in_specs=(
            P(("groups", "cell"), "gene", None, None, None),
            P(("groups", "cell"), "gene", None),
            P(("groups", "cell"), "gene", None),
            P(("groups", "cell"), "gene"),
            P(("groups", "gene"), "cell"),
            P(("groups", "cell"), "gene"),
        ),
        out_specs=(P(("groups", "gene"), "cell"), P(("groups", "cell"), "gene")),
        check_vma=False,
    )
```
